128 devices in a mesh: gx: 16 (over z, x), gy: 8 (over y, core).
Axes of the slice: x: 4, y: 4, z: 4, core: 2. Of those that a mesh axis runs over, the one named last changes fastest.
Arguments:
- velocity: float32 [3, 64, 256, 2048], P(None, None, 'gx', 'gy'), may hold values from -6 to 6
- screen: float32 [64, 256, 2048], P(None, 'gx', 'gy'), may hold values from 0.0002 to 0.24
- levels: int32 [32], replicated, may hold values from 0 to 31, each once
Outputs:
- pressure: float32 [64, 256, 2048], P(None, 'gx', 'gy')
- acoustic: float32 [32, 128, 1024], P('gx', None, 'gy')
The draws below stay inside these ranges and needn't reach their ends.
Inputs may be any that keep to these rules, and one draw needn't show every extreme that they name: `levels`: each acoustic level appears exactly once.
All inputs are finite; a program needn't handle non-finite values.
Results may differ from the reference program's by a relative error of at most 0.0003.
Values sent between devices are 32-bit elements; how exact they have to be, the bound alone decides.
A program may use at most 256 MiB of HBM per device.

```python
import math
import jax
import jax.numpy as jnp

NZ = 64
LEVELS = 3
SMOOTH = 2
COARSE_SWEEPS = 4
CYCLES = 2
NX = 256
NY = 2048
NZA = 32


def draw_screen(key, part):
    key = jax.random.fold_in(key, 11)
    block_key, factor_key = jax.random.split(key)
    block_size = 2 ** (LEVELS - 1)
    coarse_shape = (NZ // block_size, NX // block_size, NY // block_size)
    high_end = 0.015
    ramp_ratio = 8.0
    cell_factor = jnp.exp(jax.random.uniform(factor_key, (NZ, NX, NY), jnp.float32, math.log(0.5), math.log(2.0)))
    block_factor = jnp.exp(jax.random.uniform(block_key, coarse_shape, jnp.float32, math.log(0.0004), math.log(high_end)))
    spread = jnp.repeat(jnp.repeat(jnp.repeat(block_factor, block_size, 0), block_size, 1), block_size, 2)
    row_pos = (jnp.arange(NX, dtype=jnp.float32) / (NX - 1))[None, :, None]
    ramp = jnp.exp(math.log(ramp_ratio) * row_pos)
    return spread * cell_factor * ramp


def draw_velocity(key, part):
    key = jax.random.fold_in(key, 23)
    noise_key, amplitude_key, phase_key, frequency_key = jax.random.split(key, 4)
    full_shape = (3, NZ, NX, NY)
    noise = 0.12 * jax.random.truncated_normal(noise_key, -2.5, 2.5, full_shape, jnp.float32)
    amplitude = jax.random.uniform(amplitude_key, (3, 2), jnp.float32, 2.4, 2.8)
    phases = jax.random.uniform(phase_key, (3, 2), jnp.float32, -math.pi, math.pi)
    frequency = jax.random.randint(frequency_key, (3, 2, 3), 1, 3).astype(jnp.float32)
    depth_pos = ((jnp.arange(NZ, dtype=jnp.float32) + 0.5) / NZ)[:, None, None]
    row_pos = ((jnp.arange(NX, dtype=jnp.float32) + 0.5) / NX)[None, :, None]
    column_pos = ((jnp.arange(NY, dtype=jnp.float32) + 0.5) / NY)[None, None, :]
    components = []
    for component in range(3):
        smooth = jnp.zeros((NZ, NX, NY), jnp.float32)
        for mode_index in range(2):
            phase_arg = 2.0 * math.pi * (frequency[component, mode_index, 0] * depth_pos + frequency[component, mode_index, 1] * row_pos + frequency[component, mode_index, 2] * column_pos) + phases[component, mode_index]
            smooth = smooth + amplitude[component, mode_index] * jnp.sin(phase_arg)
        components.append(smooth)
    components[0] = components[0]
    components[1] = components[1]
    return noise + jnp.stack(components)


def setup_inputs(seed: int = 0) -> dict:
    arg_keys = jax.random.split(jax.random.key(seed), 4)
    velocity = draw_velocity(jax.random.fold_in(arg_keys[3], 71), 0)
    screen = draw_screen(jax.random.fold_in(arg_keys[3], 71), 0)
    levels = jax.random.permutation(arg_keys[2], NZA).astype(jnp.int32)
    return {"velocity": velocity, "screen": screen, "levels": levels}


OMEGA = 0.8


def neighbours(padded):
    return (padded[2:, 1:-1, 1:-1] + padded[:-2, 1:-1, 1:-1] + padded[1:-1, 2:, 1:-1]
            + padded[1:-1, :-2, 1:-1] + padded[1:-1, 1:-1, 2:] + padded[1:-1, 1:-1, :-2])


def central(padded, axis_number):
    if axis_number == 0:
        return (padded[2:, 1:-1, 1:-1] - padded[:-2, 1:-1, 1:-1]) * 0.5
    if axis_number == 1:
        return (padded[1:-1, 2:, 1:-1] - padded[1:-1, :-2, 1:-1]) * 0.5
    return (padded[1:-1, 1:-1, 2:] - padded[1:-1, 1:-1, :-2]) * 0.5


def apply_operator(field, padded, shifted, level_scale):
    return (6.0 * level_scale + shifted) * field - level_scale * neighbours(padded)


def smooth_once(field, padded, target, shifted, level_scale):
    return field + OMEGA * (target - apply_operator(field, padded, shifted, level_scale)) / (6.0 * level_scale + shifted)


def restrict(field):
    depth, rows, cols = field.shape
    return field.reshape(depth // 2, 2, rows // 2, 2, cols // 2, 2).mean(axis=(1, 3, 5))


def prolong(field):
    return jnp.repeat(jnp.repeat(jnp.repeat(field, 2, 0), 2, 1), 2, 2)


def full_pad(field):
    return jnp.pad(field, 1)


def vcycle(level, field, target, shift_list):
    level_scale = 0.25 ** level
    shifted = shift_list[level]
    if level == LEVELS - 1:
        for sweep_index in range(COARSE_SWEEPS):
            field = smooth_once(field, full_pad(field), target, shifted, level_scale)
        depth, rows, cols = field.shape
        remainder = target - apply_operator(field, full_pad(field), shifted, level_scale)
        faces = 2.0 * (depth * rows + rows * cols + depth * cols)
        mean_shift = jnp.sum(remainder) / (jnp.sum(shifted) + level_scale * faces)
        return field + mean_shift
    for sweep_index in range(SMOOTH):
        field = smooth_once(field, full_pad(field), target, shifted, level_scale)
    remainder = target - apply_operator(field, full_pad(field), shifted, level_scale)
    coarse_target = restrict(remainder)
    correction = vcycle(level + 1, jnp.zeros_like(coarse_target), coarse_target, shift_list)
    field = field + prolong(correction)
    for sweep_index in range(SMOOTH):
        field = smooth_once(field, full_pad(field), target, shifted, level_scale)
    return field


def vector_pad(field):
    return jnp.pad(field, ((0, 0), (1, 1), (1, 1), (1, 1)))


def reference(velocity, screen, levels):
    upad = vector_pad(velocity)
    target = -(central(upad[0], 0) + central(upad[1], 1) + central(upad[2], 2))
    shift_list = [screen]
    for level in range(1, LEVELS):
        shift_list.append(restrict(shift_list[-1]))
    pressure = jnp.zeros_like(screen)
    for cycle_index in range(CYCLES):
        pressure = vcycle(0, pressure, target, shift_list)
    ppad = full_pad(pressure)
    moved = velocity - jnp.stack([central(ppad, 0), central(ppad, 1), central(ppad, 2)])
    mpad = vector_pad(moved)
    flux_parts = []
    for first in range(3):
        total = central(mpad[first] * mpad[0], 0)
        total = total + central(mpad[first] * mpad[1], 1)
        total = total + central(mpad[first] * mpad[2], 2)
        flux_parts.append(total)
    fpad = vector_pad(jnp.stack(flux_parts))
    source = central(fpad[0], 0) + central(fpad[1], 1) + central(fpad[2], 2)
    acoustic = jnp.take(restrict(source), levels.astype(jnp.int32), axis=0)
    return pressure, acoustic
```

```python
import functools

import jax
import jax.numpy as jnp
from jax import lax
from jax.experimental import pallas as pl
from jax.experimental.pallas import tpu as pltpu
from jax.sharding import PartitionSpec as P


F32 = jnp.float32
MESH = pl.DeviceIdType.MESH
PAD = 16


class Level:
    def __init__(self, nx, ny, lane, scale, chunks):
        self.nx, self.ny, self.lane, self.scale = nx, ny, lane, scale
        self.rows = ny + 2 * PAD
        step = (ny + 16) // chunks
        self.parts = [(8 + k * step, step) for k in range(chunks)]
        own = ny // max(1, ny // 64)
        self.own = [(PAD + k * own, own) for k in range(ny // own)]


L0 = Level(16, 128, 1, 1.0, 3)
L1 = Level(8, 64, 2, 0.25, 2)
L2 = Level(4, 32, 4, 0.0625, 1)

FIELDS = {
    "U0": (L0, 1), "U1": (L0, 2), "U2": (L0, 1),
    "S": (L0, 2), "W": (L0, 2), "B": (L0, 2),
    "VA": (L0, 2), "VB": (L0, 2), "VC": (L0, 2),
    "PA": (L0, 2), "PB": (L0, 2),
    "P1": (L0, 3), "P2": (L0, 3),
    "S1": (L1, 4), "W1": (L1, 4), "BA1": (L1, 4), "BB1": (L1, 4),
    "X1": (L1, 4), "Y1": (L1, 4), "Z1": (L1, 4), "Q1": (L1, 4),
    "S2": (L2, 5), "W2": (L2, 5), "BA2": (L2, 5), "BB2": (L2, 5), "I2": (L2, 5),
    "X2": (L2, 5), "Y2": (L2, 5), "Z2": (L2, 5),
    "SS2": (L2, 1), "SA2": (L2, 1), "SB2": (L2, 1),
}
EXCHANGES = {
    "u0": (L0, 1, 0), "u1": (L0, 2, 0), "u2": (L0, 1, 0), "s": (L0, 2, 0), "b": (L0, 2, 0), "v": (L0, 2, 0),
    "s1": (L1, 4, 0), "ba1": (L1, 4, 0), "bb1": (L1, 4, 0),
    "s2": (L2, 5, 1), "ba2": (L2, 5, 1), "bb2": (L2, 5, 1),
}
X_ONLY = ("va", "p1", "p2")
SUMS = ("ra", "rb")


def scratch(ngx, ngy):
    shapes = {}
    for name, (level, halo) in FIELDS.items():
        shapes[name] = pltpu.VMEM((level.nx + 2 * halo, level.rows, 128), F32)
    for name, (level, halo, more) in EXCHANGES.items():
        for side in "lr":
            shapes[name + "_s" + side] = pltpu.VMEM((level.nx + 2 * more, 8, 128), F32)
            shapes[name + "_y" + side] = pltpu.VMEM((level.nx + 2 * halo, 8, 128), F32)
    for name in SUMS:
        shapes[name + "_a"] = pltpu.VMEM((2, 8, 128), F32)
        shapes[name + "_b"] = pltpu.VMEM((2, 8, 128), F32)
        shapes[name + "_ya"] = pltpu.VMEM((ngy, 2, 8, 128), F32)
        shapes[name + "_yb"] = pltpu.VMEM((ngx, 2, 8, 128), F32)
    shapes["raw"] = pltpu.VMEM((4, 2, 1024, 128), F32)
    shapes["back"] = pltpu.VMEM((2, 1024, 128), F32)
    shapes["UP"] = pltpu.VMEM((10, L0.rows, 128), F32)
    shapes["UP1"] = pltpu.VMEM((8, L1.rows, 128), F32)
    shapes["RS"] = pltpu.VMEM((8, 128, 128), F32)
    shapes["RC"] = pltpu.VMEM((8, 64, 128), F32)
    shapes["G"] = pltpu.VMEM((64 * 8, 128), F32)
    shapes["GZ"] = pltpu.VMEM((32, 8, 128), F32)
    shapes["out"] = pltpu.VMEM((32, 8, 128), F32)
    shapes["ship"] = pltpu.SemaphoreType.DMA((256,))
    shapes["land"] = pltpu.SemaphoreType.DMA((256,))
    shapes["local"] = pltpu.SemaphoreType.DMA((16,))
    return shapes


def kernel(names, ngx, ngy, levels_ref, u_hbm, s_hbm, p_hbm, a_hbm, *refs):
    R = dict(zip(names, refs, strict=True))
    gx, gy = lax.axis_index("gx"), lax.axis_index("gy")
    slots = [0]
    sent = []

    def at(dx, dy):
        return (lax.rem(gx + dx + ngx, ngx), lax.rem(gy + dy + ngy, ngy))

    def remote(src, dst, dx, dy):
        k = slots[0]
        slots[0] += 1
        copy = pltpu.make_async_remote_copy(
            src_ref=src,
            dst_ref=dst,
            send_sem=R["ship"].at[k],
            recv_sem=R["land"].at[k],
            device_id=at(dx, dy),
            device_id_type=MESH,
        )
        copy.start()
        sent.append(copy)
        return copy

    def lanes(n):
        return lax.broadcasted_iota(jnp.int32, (n, 128), 1)

    def loop(lo, hi, fn, step=2):
        whole = (hi - lo) // step

        def body(i, carry):
            for k in range(step):
                fn(lo + i * step + k)
            return carry

        if whole:
            lax.fori_loop(0, whole, body, 0)
        for x in range(lo + whole * step, hi):
            fn(x)

    barrier = pltpu.get_barrier_semaphore()
    others = [(k, 0) for k in range(1, ngx)] + [(0, k) for k in range(1, ngy)]
    others += [(1, 1), (1, -1), (-1, 1), (-1, -1)]
    for dx, dy in others:
        pl.semaphore_signal(barrier, inc=1, device_id=at(dx, dy), device_id_type=MESH)

    loads = []
    for k, part in enumerate((1, 2, 0, 3)):
        for half in range(2):
            cols = pl.ds(128 * half, 128)
            src = s_hbm.at[:, cols] if part == 3 else u_hbm.at[part, :, cols]
            copy = pltpu.make_async_copy(src, R["raw"].at[part, half], R["local"].at[2 * k + half])
            copy.start()
            loads.append(copy)

    def turn(part, name, xs):
        dst, halo = R[name], FIELDS[name][1]

        def one(x):
            both = [R["raw"][part, half, pl.ds(x, 64, stride=16), :] for half in range(2)]
            dst[x + halo, pl.ds(PAD, 128), :] = jnp.concatenate(both, axis=0).T

        if len(xs) <= 2:
            for x in xs:
                one(x)
        else:
            loop(xs[0], xs[-1] + 1, one, 2)

    class Exchange:
        def __init__(self, name, field, source=None):
            self.name, self.field, self.source = name, field, source or field
            self.level, self.h, self.more = EXCHANGES[name]
            self.halo, self.shalo = FIELDS[field][1], FIELDS[self.source][1]
            self.sl, self.sr, self.yl, self.yr = (R[name + k] for k in ("_sl", "_sr", "_yl", "_yr"))

        def start_y(self):
            lv, src = self.level, R[self.source]
            n, lo = lv.nx + 2 * self.more, self.shalo - self.more
            for buf, row in ((self.sl, PAD), (self.sr, PAD + lv.ny - 8)):
                val = src[pl.ds(lo, n), pl.ds(row, 8), :]
                buf[...] = pltpu.roll(val.reshape(n * 8, 128), 64, 1).reshape(n, 8, 128)
            own, to = pl.ds(self.more, lv.nx), pl.ds(self.h, lv.nx)
            self.y = [
                remote(self.sr.at[own], self.yl.at[to], 0, 1),
                remote(self.sl.at[own], self.yr.at[to], 0, -1),
            ]

        def start_diagonal(self):
            nx, h, e = self.level.nx, self.h, self.more
            last, first = pl.ds(nx - h + e, h), pl.ds(e, h)
            low, high = pl.ds(0, h), pl.ds(nx + h, h)
            self.d = [
                remote(self.sr.at[last], self.yl.at[low], 1, 1),
                remote(self.sr.at[first], self.yl.at[high], -1, 1),
                remote(self.sl.at[last], self.yr.at[low], 1, -1),
                remote(self.sl.at[first], self.yr.at[high], -1, -1),
            ]

        def start_x(self, near=0, far=None):
            lv = self.level
            nx, far = lv.nx, far or self.h
            n, cols = far - near, pl.ds(PAD, lv.ny)
            src, dst, e, a = R[self.source], R[self.field], self.shalo, self.halo
            self.x = getattr(self, "x", []) + [
                remote(src.at[pl.ds(e + nx - far, n), cols], dst.at[pl.ds(a - far, n), cols], 1, 0),
                remote(src.at[pl.ds(e + near, n), cols], dst.at[pl.ds(a + nx + near, n), cols], -1, 0),
            ]

        def start(self):
            self.start_x()
            self.start_y()
            self.start_diagonal()

        def wait(self, which):
            for copy in getattr(self, which):
                copy.wait_recv()

        def join(self, lo, hi):
            lv, f = self.level, R[self.field]
            n = hi - lo
            rows = pl.ds(lo + self.halo, n)
            inside = jnp.where(gx > 0, 1.0, 0.0) if hi <= 0 else jnp.where(gx < ngx - 1, 1.0, 0.0) if lo >= lv.nx else 1.0
            left = jnp.where(gy > 0, 1.0, 0.0) * inside
            right = jnp.where(gy < ngy - 1, 1.0, 0.0) * inside
            first = lanes(n * 8) < 64
            top = f[rows, pl.ds(PAD + lv.ny - 8, 8), :].reshape(n * 8, 128)
            got = self.yl[pl.ds(lo + self.h, n)].reshape(n * 8, 128) * left
            f[rows, pl.ds(PAD - 8, 8), :] = jnp.where(first, got, pltpu.roll(top, 64, 1)).reshape(n, 8, 128)
            low = f[rows, pl.ds(PAD, 8), :].reshape(n * 8, 128)
            got = self.yr[pl.ds(lo + self.h, n)].reshape(n * 8, 128) * right
            f[rows, pl.ds(PAD + lv.ny, 8), :] = jnp.where(first, pltpu.roll(low, 64, 1), got).reshape(n, 8, 128)

        def finish(self, own=True):
            nx, h = self.level.nx, self.h
            self.wait("x")
            clear_x(self.field, h)
            if own:
                self.wait("y")
                self.join(0, nx)
            self.wait("d")
            self.join(-h, 0)
            self.join(nx, nx + h)

    def clear_x(name, h):
        level, halo = FIELDS[name]
        f, zero = R[name], jnp.zeros((level.rows, 128), F32)

        @pl.when(gx == 0)
        def _():
            for x in range(-h, 0):
                f[x + halo] = zero

        @pl.when(gx == ngx - 1)
        def _():
            for x in range(level.nx, level.nx + h):
                f[x + halo] = zero

    def clear_y(name, h):
        level, halo = FIELDS[name]
        f, n = R[name], level.nx + 2 * h
        rows = pl.ds(halo - h, n)

        def side(row, first):
            cells = (rows, pl.ds(row, 8), slice(None))
            val = f[cells].reshape(n * 8, 128)
            keep = lanes(n * 8) >= 64 if first else lanes(n * 8) < 64
            f[cells] = jnp.where(keep, val, 0.0).reshape(n, 8, 128)

        @pl.when(gy == 0)
        def _():
            side(PAD - 8, True)

        @pl.when(gy == ngy - 1)
        def _():
            side(PAD + level.ny, False)

    class Rows:
        def __init__(self, field, h):
            self.field, self.h = field, h
            level, a = FIELDS[field]
            nx, f, cols = level.nx, R[field], pl.ds(8, level.ny + 16)
            self.x = [
                remote(f.at[pl.ds(a + nx - h, h), cols], f.at[pl.ds(a - h, h), cols], 1, 0),
                remote(f.at[pl.ds(a, h), cols], f.at[pl.ds(a + nx, h), cols], -1, 0),
            ]

        def finish(self):
            for copy in self.x:
                copy.wait_recv()
            clear_x(self.field, self.h)

    def z_pair(c, lane):
        n = c.shape[0]
        z = lanes(n) & 63
        before = jnp.where(z >= lane, pltpu.roll(c, lane, 1), 0.0)
        after = jnp.where(z < 64 - lane, pltpu.roll(c, 128 - lane, 1), 0.0)
        return before, after

    def around(name, x, r, n):
        level, halo = FIELDS[name]
        f, i = R[name], x + halo
        c = f[i, pl.ds(r, n), :]
        before, after = z_pair(c, level.lane)
        side = f[i - 1, pl.ds(r, n), :] + f[i + 1, pl.ds(r, n), :]
        side = side + (f[i, pl.ds(r - 1, n), :] + f[i, pl.ds(r + 1, n), :])
        return c, side + (before + after)

    def get(name, x, r, n):
        return R[name][x + FIELDS[name][1], pl.ds(r, n), :]

    def put(name, x, r, n, val):
        R[name][x + FIELDS[name][1], pl.ds(r, n), :] = val

    def each(level, lo, hi, fn, own=False, step=2):
        def row(x):
            for r, n in level.own if own else level.parts:
                fn(x, r, n)

        loop(lo, hi, row, step)

    def first_sweep(w, b, to, lo, hi):
        def fn(x, r, n):
            put(to, x, r, n, get(w, x, r, n) * get(b, x, r, n))

        each(FIELDS[to][0], lo, hi, fn)

    def sweep(v, w, b, to, lo, hi, also=None):
        level = FIELDS[v][0]

        def fn(x, r, n, twice=also is not None):
            c, s = around(v, x, r, n)
            s = s if level.scale == 1.0 else s * level.scale
            new = 0.2 * c + get(w, x, r, n) * (get(b, x, r, n) + s)
            put(to, x, r, n, new)
            if twice:
                put(also, x, r, n, new)

        if also is None:
            each(level, lo, hi, fn)
        else:
            each(level, 0, level.nx, fn)
            each(level, lo, 0, functools.partial(fn, twice=False))
            each(level, level.nx, hi, functools.partial(fn, twice=False))

    def remainder(v, s, b, x, r, n):
        level = FIELDS[v][0]
        c, around_sum = around(v, x, r, n)
        return get(b, x, r, n) + level.scale * around_sum - (6.0 * level.scale + get(s, x, r, n)) * c

    def halve(pair, buf, k, lane):
        ny = pair[0].shape[0] * len(pair)
        for j, val in enumerate(pair):
            R[buf][k, pl.ds(j * val.shape[0], val.shape[0]), :] = val
        a = R[buf][k, pl.ds(0, ny // 2, stride=2), :] + R[buf][k, pl.ds(1, ny // 2, stride=2), :]
        even = (lanes(ny // 2) & lane) == 0
        return (a + jnp.where(even, pltpu.roll(a, 128 - lane, 1), pltpu.roll(a, lane, 1))) * 0.125

    def coarsen(level, fn, lo, hi, write, buf):
        def row(x):
            pair = [fn(2 * x, r, n) + fn(2 * x + 1, r, n) for r, n in level.own]
            write(x, halve(pair, buf, (x + 2) & 7 if lo < 0 else x, level.lane))

        loop(lo, hi, row, 2)

    def spread(name, up, lo, hi):
        level = FIELDS[name][0]
        n = level.ny + 8

        def row(x):
            val = get(name, x, PAD - 4, n)
            R[up][x - lo, pl.ds(8, n, stride=2), :] = val
            R[up][x - lo, pl.ds(9, n, stride=2), :] = val

        loop(lo, hi, row, 2)

    for copy in loads[0:2]:
        copy.wait()
    turn(1, "U1", (0, 15))
    pl.semaphore_wait(barrier, len(others))
    ex_u1 = Exchange("u1", "U1")
    ex_u1.start_x(0, 1)
    turn(1, "U1", range(1, 15))
    for copy in loads[2:4]:
        copy.wait()
    turn(2, "U2", range(16))
    ex_u2 = Exchange("u2", "U2")
    ex_u2.start_y()
    for copy in loads[6:8]:
        copy.wait()
    turn(3, "S", range(16))
    ex_s = Exchange("s", "S")
    ex_s.start()
    for copy in loads[4:6]:
        copy.wait()
    turn(0, "U0", range(16))

    ex_u2.wait("y")
    ex_u2.join(0, 16)
    ex_u1.wait("x")
    clear_x("U1", 1)

    def target(x, r, n):
        before, after = z_pair(get("U0", x, r, n), 1)
        d = (after - before) + (get("U1", x + 1, r, n) - get("U1", x - 1, r, n))
        d = d + (get("U2", x, r + 1, n) - get("U2", x, r - 1, n))
        put("B", x, r, n, -0.5 * d)

    each(L0, 0, 16, target, own=True)
    ex_b = Exchange("b", "B")
    ex_b.start()

    coarsen(L0, lambda x, r, n: get("S", x, r, n), 0, 8, lambda x, v: put("S1", x, PAD, 64, v), "RS")
    ex_s1 = Exchange("s1", "S1")
    ex_s1.start()

    def weights(s, w, h):
        level = FIELDS[s][0]

        def fn(x, r, n):
            put(w, x, r, n, 0.8 / (6.0 * level.scale + get(s, x, r, n)))

        each(level, -h, level.nx + h, fn)
        clear_x(w, h)
        clear_y(w, h)

    ex_s.finish()
    weights("S", "W", 2)
    ex_s1.finish()
    weights("S1", "W1", 4)

    def coarsen_2(fn, source, field):
        coarsen(L1, fn, -1, 5, lambda x, v: put(source, x, PAD, 32, v), "RC")
        for x in range(4):
            put(field, x, PAD, 32, get(source, x, PAD, 32))

    coarsen_2(lambda x, r, n: get("S1", x, r, n), "SS2", "S2")
    ex_s2 = Exchange("s2", "S2", "SS2")
    ex_s2.start()

    def down_0(v1, keep, r_to):
        sweep(v1, "W", "B", "VB", -1, 17, also=keep)
        coarsen(L0, functools.partial(remainder, "VB", "S", "B"), 0, 8, lambda x, v: put(r_to, x, PAD, 64, v), "RS")

    def coarse_weights():
        ex_s2.finish()
        weights("S2", "W2", 5)
        one = jnp.ones((L2.rows, 128), F32)
        for x in range(14):
            R["I2"][x] = one
        clear_x("I2", 5)
        clear_y("I2", 5)

        def a_one(x, r, n):
            c, s = around("I2", x, r, n)
            put("X2", x, r, n, (6.0 * L2.scale + get("S2", x, r, n)) * c - L2.scale * s)

        each(L2, -4, 8, a_one)

        def left(x, r, n):
            put("Z2", x, r, n, get("I2", x, r, n))

        each(L2, -4, 8, left)
        lo, hi = -4, 8
        for k in range(4):

            def weigh(x, r, n):
                e = get("W2", x, r, n) * get("X2", x, r, n)
                put("Y2", x, r, n, e)
                put("Z2", x, r, n, get("Z2", x, r, n) - e)

            each(L2, lo, hi, weigh)
            lo, hi = lo + 1, hi - 1
            if k < 3:

                def again(x, r, n):
                    put("X2", x, r, n, 0.2 * get("X2", x, r, n) + L2.scale * around("Y2", x, r, n)[1])

                each(L2, lo, hi, again)
        spread("Z2", "UP1", -1, 5)

        def scaled(x2):
            for k in range(2):
                for r, n in L1.parts:
                    put("X1", 2 * x2 + k, r, n, 0.125 * R["UP1"][x2 + 1, pl.ds(r, n), :])

        loop(-1, 5, scaled, 1)

        def a_of(x, r, n):
            c, s = around("X1", x, r, n)
            y = (6.0 * L1.scale + get("S1", x, r, n)) * c - L1.scale * s
            put("Y1", x, r, n, y)
            put("Z1", x, r, n, get("W1", x, r, n) * y)

        each(L1, -1, 9, a_of)

        def last(x, r, n):
            e, s = around("Z1", x, r, n)
            t = 0.2 * get("Y1", x, r, n) + L1.scale * s
            put("Q1", x, r, n, get("X1", x, r, n) - (e + get("W1", x, r, n) * t))

        each(L1, 0, 8, last)

    def coarse(b1, b2, source, ex1, ex2, sums, work, first):
        total = jnp.zeros((8, 128), F32)
        for x in range(8):
            val = get("Q1", x, PAD, 64) * get(b1, x, PAD, 64)
            total = total + jnp.sum(val.reshape(8, 8, 128), axis=0)
        R[sums + "_a"][0] = total * 0.5
        if first:
            mass = jnp.zeros((8, 128), F32)
            for x in range(4):
                mass = mass + jnp.sum(get("S2", x, PAD, 32).reshape(4, 8, 128), axis=0)
            R[sums + "_a"][1] = mass * 0.25
        else:
            R[sums + "_a"][1] = jnp.zeros((8, 128), F32)
        part_a = [remote(R[sums + "_a"], R[sums + "_ya"].at[k], 0, k) for k in range(1, ngy)]
        ex1 = Exchange(ex1, b1) if isinstance(ex1, str) else ex1
        ex1.finish()
        first_sweep("W1", b1, "X1", -4, 12)
        sweep("X1", "W1", b1, "Y1", -3, 11)
        coarsen_2(functools.partial(remainder, "Y1", "S1", b1), source, b2)
        ex2 = Exchange(ex2, b2, source)
        ex2.start()
        both = R[sums + "_a"][...]
        for k, copy in zip(range(1, ngy), part_a, strict=True):
            copy.wait_recv()
            both = both + R[sums + "_ya"][k]
        R[sums + "_b"][...] = both
        part_b = [remote(R[sums + "_b"], R[sums + "_yb"].at[k], k, 0) for k in range(1, ngx)]
        work()
        ex2.finish()
        first_sweep("W2", b2, "X2", -5, 9)
        sweep("X2", "W2", b2, "Y2", -4, 8)
        sweep("Y2", "W2", b2, "X2", -3, 7)
        sweep("X2", "W2", b2, "Y2", -2, 6)
        for k, copy in zip(range(1, ngx), part_b, strict=True):
            copy.wait_recv()
            both = both + R[sums + "_yb"][k]
        return both

    def total_of(tile):
        return jnp.sum(jnp.sum(tile, axis=0, keepdims=True), axis=1, keepdims=True)

    def up(shift, b1):
        def lift(x, r, n):
            put("X2", x, r, n, get("Y2", x, r, n) + shift * get("I2", x, r, n))

        each(L2, -2, 6, lift)
        spread("X2", "UP1", -2, 6)

        def add_1(x2):
            for k in range(2):
                for r, n in L1.parts:
                    x = 2 * x2 + k
                    put("Y1", x, r, n, get("Y1", x, r, n) + R["UP1"][x2 + 2, pl.ds(r, n), :])

        loop(-2, 6, add_1, 1)
        sweep("Y1", "W1", b1, "X1", -2, 10)
        sweep("X1", "W1", b1, "Z1", -1, 9)
        spread("Z1", "UP", -1, 9)

    def add_0(kept):
        def row(x1):
            for k in range(2):
                for r, n in L0.parts:
                    x = 2 * x1 + k
                    put(kept, x, r, n, get(kept, x, r, n) + R["UP"][x1 + 1, pl.ds(r, n), :])

        loop(-1, 9, row, 1)

    ex_b.finish()
    first_sweep("W", "B", "VA", -2, 18)
    down_0("VA", "PA", "BA1")
    ex1 = Exchange("ba1", "BA1")
    ex1.start()
    coarse_weights()
    bg = {}

    def send_more():
        bg["v"] = Rows("PA", 2)
        ex_u0 = bg["u0"] = Exchange("u0", "U0")
        ex_u0.start()
        ex_u1.start_x(1, 2)
        ex_u1.start_y()
        ex_u1.start_diagonal()
        ex_u2.start_x()
        ex_u2.start_diagonal()

    sums_a = coarse("BA1", "BA2", "SA2", ex1, "ba2", "ra", send_more, True)
    whole = (64 // 4, 16 * ngx // 4, 256 * ngy // 4)
    faces = 2.0 * (whole[0] * whole[1] + whole[1] * whole[2] + whole[0] * whole[2])
    mass = total_of(sums_a[1]) + L2.scale * faces
    up(total_of(sums_a[0]) / mass, "BA1")
    bg["v"].finish()
    for copy in bg["v"].x:
        copy.wait_send()
    add_0("PA")
    sweep("PA", "W", "B", "VC", -1, 17)
    sweep("VC", "W", "B", "P1", 0, 16)
    rows_p1 = Rows("P1", 3)
    bg["u0"].finish()
    ex_u1.x = ex_u1.x[2:]
    ex_u1.finish()
    ex_u2.finish(own=False)

    rows_p1.finish()
    sweep("P1", "W", "B", "VA", -2, 18)
    down_0("VA", "PB", "BB1")
    ex1 = Exchange("bb1", "BB1")
    ex1.start()
    ex_v = Exchange("v", "PB")
    sums_b = coarse("BB1", "BB2", "SB2", ex1, "bb2", "rb", ex_v.start, False)
    up(total_of(sums_b[0]) / mass, "BB1")
    ex_v.finish()
    for copy in ex_v.x:
        copy.wait_send()
    add_0("PB")
    sweep("PB", "W", "B", "VC", -1, 17)
    sweep("VC", "W", "B", "P2", 0, 16)
    rows_p2 = Rows("P2", 3)

    def back(x):
        t = get("P2", x, PAD, 128).T
        for half in range(2):
            R["back"][half, pl.ds(x, 64, stride=16), :] = t[64 * half : 64 * half + 64]

    loop(0, 16, back, 2)
    stores = []
    for half in range(2):
        copy = pltpu.make_async_copy(R["back"].at[half], p_hbm.at[:, pl.ds(128 * half, 128)], R["local"].at[8 + half])
        copy.start()
        stores.append(copy)

    rows_p2.finish()

    def move_1(x, r, n):
        put("VB", x, r, n, get("U1", x, r, n) - 0.5 * (get("P2", x + 1, r, n) - get("P2", x - 1, r, n)))

    each(L0, -2, 18, move_1)

    def move_02(x, r, n):
        before, after = z_pair(get("P2", x, r, n), 1)
        put("VA", x, r, n, get("U0", x, r, n) - 0.5 * (after - before))
        put("VC", x, r, n, get("U2", x, r, n) - 0.5 * (get("P2", x, r + 1, n) - get("P2", x, r - 1, n)))

    each(L0, -1, 17, move_02)
    clear_x("VB", 2)
    clear_y("VB", 2)
    for name in ("VA", "VC"):
        clear_x(name, 1)
        clear_y(name, 1)

    def product(a, b, x, r, n):
        return get(a, x, r, n) * get(b, x, r, n)

    def flux_1(x, r, n):
        d = product("VB", "VB", x + 1, r, n) - product("VB", "VB", x - 1, r, n)
        d = d + 2.0 * (product("VB", "VC", x, r + 1, n) - product("VB", "VC", x, r - 1, n))
        put("PB", x, r, n, d)

    each(L0, -1, 17, flux_1, own=True)
    clear_x("PB", 1)

    def flux_2(x, r, n):
        put("W", x, r, n, product("VC", "VC", x, r + 1, n) - product("VC", "VC", x, r - 1, n))

    each(L0, 0, 16, flux_2)
    clear_y("W", 0)

    def source(x, r, n):
        before, after = z_pair(product("VA", "VA", x, r, n), 1)
        d = product("VA", "VB", x + 1, r, n) - product("VA", "VB", x - 1, r, n)
        d = d + (product("VA", "VC", x, r + 1, n) - product("VA", "VC", x, r - 1, n))
        before, after = z_pair((after - before) + 2.0 * d, 1)
        d = (after - before) + (get("PB", x + 1, r, n) - get("PB", x - 1, r, n))
        return 0.25 * (d + (get("W", x, r + 1, n) - get("W", x, r - 1, n)))

    coarsen(L0, source, 0, 8, lambda x, v: put("X1", x, PAD, 64, v), "RS")

    first = lanes(64) < 64
    for x in range(0, 8, 2):
        t = jnp.concatenate([get("X1", x, PAD, 64), get("X1", x + 1, PAD, 64)], axis=0).T
        low, high = t[:64], t[64:]
        R["G"][pl.ds(x, 64, stride=8), :] = jnp.where(first, low, pltpu.roll(high, 64, 1))
        R["G"][pl.ds(x + 1, 64, stride=8), :] = jnp.where(first, pltpu.roll(low, 64, 1), high)
    for z in range(32):
        R["GZ"][z] = R["G"][pl.ds(16 * z, 8), :]
    for p in range(32):
        R["out"][p] = R["GZ"][levels_ref[p]]
    own = 32 // ngx
    mine = a_hbm.at[:, pl.ds(gx * 8, 8), :]
    copy = pltpu.make_async_copy(R["out"].at[pl.ds(gx * own, own)], mine, R["local"].at[10])
    copy.start()
    stores.append(copy)
    last_ones = []
    for k in range(1, ngx):
        peer = lax.rem(gx + k, ngx)
        last_ones.append(remote(R["out"].at[pl.ds(peer * own, own)], mine, k, 0))
    for copy in last_ones:
        copy.wait_recv()
    for copy in stores:
        copy.wait()
    done = [id(copy) for copy in bg["v"].x + ex_v.x]
    for copy in sent:
        if id(copy) not in done:
            copy.wait_send()


def solution(mesh):
    ngx, ngy = mesh.shape["gx"], mesh.shape["gy"]
    shapes = scratch(ngx, ngy)

    def body(velocity, screen, levels):
        pressure, acoustic = pl.pallas_call(
            functools.partial(kernel, tuple(shapes), ngx, ngy),
            out_shape=(
                jax.ShapeDtypeStruct((1024, 256), F32),
                jax.ShapeDtypeStruct((32 // ngx, 8 * ngx, 128), F32),
            ),
            in_specs=[
                pl.BlockSpec(memory_space=pltpu.SMEM),
                pl.BlockSpec(memory_space=pl.ANY),
                pl.BlockSpec(memory_space=pl.ANY),
            ],
            out_specs=(pl.BlockSpec(memory_space=pl.ANY), pl.BlockSpec(memory_space=pl.ANY)),
            scratch_shapes=list(shapes.values()),
            compiler_params=pltpu.CompilerParams(
                collective_id=0, has_side_effects=True, vmem_limit_bytes=60 * 2**20
            ),
        )(levels, velocity.reshape(3, 1024, 256), screen.reshape(1024, 256))
        return pressure.reshape(64, 16, 256), acoustic

    in_specs = (P(None, None, "gx", "gy"), P(None, "gx", "gy"), P())
    out_specs = (P(None, "gx", "gy"), P("gx", None, "gy"))
    return jax.shard_map(body, mesh=mesh, in_specs=in_specs, out_specs=out_specs, check_vma=False)
```

```python
import functools

import jax
import jax.numpy as jnp
from jax import lax
from jax.experimental import pallas as pl
from jax.experimental.pallas import tpu as pltpu
from jax.sharding import PartitionSpec as P


F32 = jnp.float32
MESH = pl.DeviceIdType.MESH
PAD = 16


class Level:
    def __init__(self, nx, ny, lane, scale, chunks):
        self.nx, self.ny, self.lane, self.scale = nx, ny, lane, scale
        self.rows = ny + 2 * PAD
        step = (ny + 16) // chunks
        self.parts = [(8 + k * step, step) for k in range(chunks)]
        own = ny // max(1, ny // 64)
        self.own = [(PAD + k * own, own) for k in range(ny // own)]


L0 = Level(16, 128, 1, 1.0, 3)
L1 = Level(8, 64, 2, 0.25, 2)
L2 = Level(4, 32, 4, 0.0625, 1)

FIELDS = {
    "U0": (L0, 1), "U1": (L0, 2), "U2": (L0, 1),
    "S": (L0, 4), "W": (L0, 4), "B": (L0, 4),
    "VA": (L0, 2), "VB": (L0, 2), "VC": (L0, 4),
    "PA": (L0, 5), "PB": (L0, 5),
    "P1": (L0, 3), "P2": (L0, 3),
    "S1": (L1, 6), "W1": (L1, 6), "BA1": (L1, 6), "BB1": (L1, 6),
    "X1": (L1, 6), "Y1": (L1, 6), "Z1": (L1, 6), "Q1": (L1, 0),
    "S2": (L2, 6), "W2": (L2, 6), "BA2": (L2, 6), "BB2": (L2, 6), "I2": (L2, 6),
    "X2": (L2, 6), "Y2": (L2, 6), "Z2": (L2, 6),
    "SA2": (L2, 2), "SB2": (L2, 2),
}
EXCHANGES = {
    "u0": (L0, 1, 0, False), "u1": (L0, 1, 0, False), "u2": (L0, 1, 0, False), "s": (L0, 2, 0, False), "v": (L0, 5, 0, False),
    "s1": (L1, 6, 0, False), "ba1": (L1, 6, 0, False), "bb1": (L1, 6, 0, False),
    "s2": (L2, 6, 0, True), "ba2": (L2, 6, 2, False), "bb2": (L2, 6, 2, False),
}
SUMS = ("ra", "rb")


def scratch(ngx, ngy):
    shapes = {}
    for name, (level, halo) in FIELDS.items():
        shapes[name] = pltpu.VMEM((level.nx + 2 * halo, level.rows, 128), F32)
    for name, (level, halo, more, _) in EXCHANGES.items():
        if level.lane > 1:
            packed = level.ny // level.lane
            shapes[name + "_px"] = pltpu.VMEM((level.nx + 2 * more, packed, 128), F32)
            shapes[name + "_qx"] = pltpu.VMEM((2, halo, packed, 128), F32)
        for side in "lr":
            shapes[name + "_s" + side] = pltpu.VMEM((level.nx + 2 * more, 8, 128), F32)
            shapes[name + "_y" + side] = pltpu.VMEM((level.nx + 2 * halo, 8, 128), F32)
    for name in SUMS:
        shapes[name + "_a"] = pltpu.VMEM((8, 128), F32)
        shapes[name + "_b"] = pltpu.VMEM((8, 128), F32)
        shapes[name + "_ya"] = pltpu.VMEM((ngy, 8, 128), F32)
        shapes[name + "_yb"] = pltpu.VMEM((ngx, 8, 128), F32)
    shapes["BE"] = pltpu.VMEM((4, L0.rows, 128), F32)
    shapes["raw"] = pltpu.VMEM((4, 2, 1024, 128), F32)
    shapes["back"] = pltpu.VMEM((2, 1024, 128), F32)
    shapes["UP"] = pltpu.VMEM((14, L0.rows, 128), F32)
    shapes["UP1"] = pltpu.VMEM((10, L1.rows, 128), F32)
    shapes["RS"] = pltpu.VMEM((8, 128, 128), F32)
    shapes["RC"] = pltpu.VMEM((8, 64, 128), F32)
    shapes["G"] = pltpu.VMEM((64 * 8, 128), F32)
    shapes["GZ"] = pltpu.VMEM((32, 8, 128), F32)
    shapes["out"] = pltpu.VMEM((32, 8, 128), F32)
    shapes["ship"] = pltpu.SemaphoreType.DMA((256,))
    shapes["land"] = pltpu.SemaphoreType.DMA((256,))
    shapes["local"] = pltpu.SemaphoreType.DMA((16,))
    return shapes


def kernel(names, ngx, ngy, levels_ref, u_hbm, s_hbm, p_hbm, a_hbm, *refs):
    R = dict(zip(names, refs, strict=True))
    gx, gy = lax.axis_index("gx"), lax.axis_index("gy")
    slots = [0]
    sent = []

    def at(dx, dy):
        return (lax.rem(gx + dx + ngx, ngx), lax.rem(gy + dy + ngy, ngy))

    def remote(src, dst, dx, dy):
        k = slots[0]
        slots[0] += 1
        copy = pltpu.make_async_remote_copy(
            src_ref=src,
            dst_ref=dst,
            send_sem=R["ship"].at[k],
            recv_sem=R["land"].at[k],
            device_id=at(dx, dy),
            device_id_type=MESH,
        )
        copy.start()
        sent.append(copy)
        return copy

    def lanes(n):
        return lax.broadcasted_iota(jnp.int32, (n, 128), 1)

    def loop(lo, hi, fn, step=None):
        n = hi - lo
        if step is None:
            step = next((k for k in (5, 4, 6, 3) if n % k == 0), 4)
        whole = n // step

        def body(i, carry):
            for k in range(step):
                fn(lo + i * step + k)
            return carry

        if whole > 1:
            lax.fori_loop(0, whole, body, 0)
        else:
            whole = 0
        for x in range(lo + whole * step, hi):
            fn(x)

    barrier = pltpu.get_barrier_semaphore()
    others = [(k, 0) for k in range(1, ngx)] + [(0, k) for k in range(1, ngy)]
    others += [(dx, dy) for dx in (-2, -1, 1, 2) for dy in (-1, 1)]
    for dx, dy in others:
        pl.semaphore_signal(barrier, inc=1, device_id=at(dx, dy), device_id_type=MESH)

    loads = []
    for k, part in enumerate((1, 2, 0, 3)):
        for half in range(2):
            cols = pl.ds(128 * half, 128)
            src = s_hbm.at[:, cols] if part == 3 else u_hbm.at[part, :, cols]
            copy = pltpu.make_async_copy(src, R["raw"].at[part, half], R["local"].at[2 * k + half])
            copy.start()
            loads.append(copy)

    def turn(part, name):
        dst, halo = R[name], FIELDS[name][1]

        def one(x):
            both = [R["raw"][part, half, pl.ds(x, 64, stride=16), :] for half in range(2)]
            dst[x + halo, pl.ds(PAD, 128), :] = jnp.concatenate(both, axis=0).T

        loop(0, 16, one, 8)

    class Exchange:
        def __init__(self, name, field, source=None):
            self.name, self.field, self.source = name, field, source or field
            self.level, self.h, self.more, self.far = EXCHANGES[name]
            self.halo, self.shalo = FIELDS[field][1], FIELDS[self.source][1]
            self.sl, self.sr, self.yl, self.yr = (R[name + k] for k in ("_sl", "_sr", "_yl", "_yr"))

        def start_y(self):
            lv, src = self.level, R[self.source]
            n, lo = lv.nx + 2 * self.more, self.shalo - self.more
            for buf, row in ((self.sl, PAD), (self.sr, PAD + lv.ny - 8)):
                val = src[pl.ds(lo, n), pl.ds(row, 8), :]
                buf[...] = pltpu.roll(val.reshape(n * 8, 128), 64, 1).reshape(n, 8, 128)
            own, to = pl.ds(self.more, lv.nx), pl.ds(self.h, lv.nx)
            self.y = [
                remote(self.sr.at[own], self.yl.at[to], 0, 1),
                remote(self.sl.at[own], self.yr.at[to], 0, -1),
            ]

        def hops(self):
            nx, h = self.level.nx, self.h
            if not self.far:
                return [(1, (nx - h, h), 0), (-1, (0, h), h + nx)]
            more = h - nx
            return [(1, (0, nx), more), (-1, (0, nx), h + nx), (2, (nx - more, more), 0), (-2, (0, more), h + nx + nx)]

        def start_diagonal(self):
            self.d = []
            for dx, (lo, n), to in self.hops():
                rows, to = pl.ds(lo + self.more, n), pl.ds(to, n)
                self.d.append(remote(self.sr.at[rows], self.yl.at[to], dx, 1))
                self.d.append(remote(self.sl.at[rows], self.yr.at[to], dx, -1))

        def start_x(self):
            lv, src, dst = self.level, R[self.source], R[self.field]
            self.x = []
            if lv.lane == 1:
                cols = pl.ds(PAD, lv.ny)
                for dx, (lo, n), to in self.hops():
                    rows, to = pl.ds(lo + self.shalo, n), pl.ds(to + self.halo - self.h, n)
                    self.x.append(remote(src.at[rows, cols], dst.at[to, cols], dx, 0))
                return
            px, qx, m = R[self.name + "_px"], R[self.name + "_qx"], lv.ny // lv.lane
            which = lanes(m) & (lv.lane - 1)
            for i in range(lv.nx + 2 * self.more):
                val = src[i + self.shalo - self.more, pl.ds(PAD, m), :]
                for g in range(1, lv.lane):
                    val = jnp.where(which == g, src[i + self.shalo - self.more, pl.ds(PAD + g * m, m), :], val)
                px[i] = val
            for dx, (lo, n), to in self.hops():
                side, to = (0, to) if dx > 0 else (1, to - self.h - lv.nx)
                self.x.append(remote(px.at[pl.ds(lo + self.more, n)], qx.at[side, pl.ds(to, n)], dx, 0))

        def unpack(self):
            lv, f, qx = self.level, R[self.field], R[self.name + "_qx"]
            m = lv.ny // lv.lane
            which = lanes(m) & (lv.lane - 1)
            for side in range(2):
                for i in range(self.h):
                    val = qx[side, i]
                    row = self.halo - self.h + i if side == 0 else self.halo + lv.nx + i
                    for g in range(lv.lane):
                        t = jnp.where(which == g, val, 0.0)
                        for bit in (1, 2)[: lv.lane // 2]:
                            t = t + pltpu.roll(t, 128 - bit if g & bit else bit, 1)
                        f[row, pl.ds(PAD + g * m, m), :] = t

        def start(self):
            self.start_x()
            self.start_y()
            self.start_diagonal()

        def wait(self, which):
            for copy in getattr(self, which):
                copy.wait_recv()

        def join(self, lo, hi):
            lv, f = self.level, R[self.field]
            n = hi - lo
            rows = pl.ds(lo + self.halo, n)
            inside = jnp.where(gx > 0, 1.0, 0.0) if hi <= 0 else jnp.where(gx < ngx - 1, 1.0, 0.0) if lo >= lv.nx else 1.0
            left = jnp.where(gy > 0, 1.0, 0.0) * inside
            right = jnp.where(gy < ngy - 1, 1.0, 0.0) * inside
            first = lanes(n * 8) < 64
            top = f[rows, pl.ds(PAD + lv.ny - 8, 8), :].reshape(n * 8, 128)
            got = self.yl[pl.ds(lo + self.h, n)].reshape(n * 8, 128) * left
            f[rows, pl.ds(PAD - 8, 8), :] = jnp.where(first, got, pltpu.roll(top, 64, 1)).reshape(n, 8, 128)
            low = f[rows, pl.ds(PAD, 8), :].reshape(n * 8, 128)
            got = self.yr[pl.ds(lo + self.h, n)].reshape(n * 8, 128) * right
            f[rows, pl.ds(PAD + lv.ny, 8), :] = jnp.where(first, pltpu.roll(low, 64, 1), got).reshape(n, 8, 128)

        def finish_x(self):
            self.wait("x")
            if self.level.lane > 1:
                self.unpack()
            clear_x(self.field, self.h)
            self.wait("d")
            self.join(-self.h, 0)
            self.join(self.level.nx, self.level.nx + self.h)

        def finish_y(self):
            self.wait("y")
            self.join(0, self.level.nx)

        def finish(self):
            self.finish_y()
            self.finish_x()

    def clear_x(name, h):
        level, halo = FIELDS[name]
        f, zero = R[name], jnp.zeros((level.rows, 128), F32)

        @pl.when(gx == 0)
        def _():
            for x in range(-h, 0):
                f[x + halo] = zero

        @pl.when(gx == ngx - 1)
        def _():
            for x in range(level.nx, level.nx + h):
                f[x + halo] = zero

        if h > level.nx:

            @pl.when(gx == 1)
            def _():
                for x in range(-h, -level.nx):
                    f[x + halo] = zero

            @pl.when(gx == ngx - 2)
            def _():
                for x in range(2 * level.nx, level.nx + h):
                    f[x + halo] = zero

    def clear_y(name, lo, hi):
        level, halo = FIELDS[name]
        f, n = R[name], hi - lo
        rows = pl.ds(halo + lo, n)

        def side(row, first):
            cells = (rows, pl.ds(row, 8), slice(None))
            val = f[cells].reshape(n * 8, 128)
            keep = lanes(n * 8) >= 64 if first else lanes(n * 8) < 64
            f[cells] = jnp.where(keep, val, 0.0).reshape(n, 8, 128)

        @pl.when(gy == 0)
        def _():
            side(PAD - 8, True)

        @pl.when(gy == ngy - 1)
        def _():
            side(PAD + level.ny, False)

    class Rows:
        def __init__(self, field, far, near=0, source=None):
            self.field, self.h = field, far
            level, a = FIELDS[field]
            nx, f, cols, n = level.nx, R[field], pl.ds(8, level.ny + 16), far - near
            last, first = (f.at[pl.ds(a + nx - far, n), cols], f.at[pl.ds(a + near, n), cols])
            if source is not None:
                last, first = source.at[pl.ds(n, n), cols], source.at[pl.ds(0, n), cols]
            self.x = [
                remote(last, f.at[pl.ds(a - far, n), cols], 1, 0),
                remote(first, f.at[pl.ds(a + nx + near, n), cols], -1, 0),
            ]

        def finish(self):
            for copy in self.x:
                copy.wait_recv()
            clear_x(self.field, self.h)

    def z_pair(c, lane):
        n = c.shape[0]
        z = lanes(n) & 63
        before = jnp.where(z >= lane, pltpu.roll(c, lane, 1), 0.0)
        after = jnp.where(z < 64 - lane, pltpu.roll(c, 128 - lane, 1), 0.0)
        return before, after

    def around(name, x, r, n):
        level, halo = FIELDS[name]
        f, i = R[name], x + halo
        c = f[i, pl.ds(r, n), :]
        before, after = z_pair(c, level.lane)
        side = f[i - 1, pl.ds(r, n), :] + f[i + 1, pl.ds(r, n), :]
        side = side + (f[i, pl.ds(r - 1, n), :] + f[i, pl.ds(r + 1, n), :])
        return c, side + (before + after)

    def get(name, x, r, n):
        return R[name][x + FIELDS[name][1], pl.ds(r, n), :]

    def put(name, x, r, n, val):
        R[name][x + FIELDS[name][1], pl.ds(r, n), :] = val

    def each(level, lo, hi, fn, own=False, step=None):
        def row(x):
            for r, n in level.own if own else level.parts:
                fn(x, r, n)

        loop(lo, hi, row, step)

    def first_sweep(w, b, to, lo, hi):
        def fn(x, r, n):
            put(to, x, r, n, get(w, x, r, n) * get(b, x, r, n))

        each(FIELDS[to][0], lo, hi, fn)

    def sweep(v, w, b, to, lo, hi, also=None):
        level = FIELDS[v][0]

        def fn(x, r, n, twice=also is not None):
            c, s = around(v, x, r, n)
            s = s if level.scale == 1.0 else s * level.scale
            new = 0.2 * c + get(w, x, r, n) * (get(b, x, r, n) + s)
            put(to, x, r, n, new)
            if twice:
                put(also, x, r, n, new)

        if also is None:
            each(level, lo, hi, fn)
        else:
            each(level, max(lo, 0), min(hi, level.nx), fn)
            each(level, lo, min(hi, 0), functools.partial(fn, twice=False))
            each(level, max(lo, level.nx), hi, functools.partial(fn, twice=False))

    def remainder(v, s, b, x, r, n):
        level = FIELDS[v][0]
        c, around_sum = around(v, x, r, n)
        return get(b, x, r, n) + level.scale * around_sum - (6.0 * level.scale + get(s, x, r, n)) * c

    def halve(pair, buf, k, lane):
        ny = pair[0].shape[0] * len(pair)
        for j, val in enumerate(pair):
            R[buf][k, pl.ds(j * val.shape[0], val.shape[0]), :] = val
        a = R[buf][k, pl.ds(0, ny // 2, stride=2), :] + R[buf][k, pl.ds(1, ny // 2, stride=2), :]
        even = (lanes(ny // 2) & lane) == 0
        return (a + jnp.where(even, pltpu.roll(a, 128 - lane, 1), pltpu.roll(a, lane, 1))) * 0.125

    def coarsen(level, fn, lo, hi, write, buf):
        def row(x):
            pair = [fn(2 * x, r, n) + fn(2 * x + 1, r, n) for r, n in level.own]
            write(x, halve(pair, buf, (x + 2) & 7 if lo < 0 else x, level.lane))

        loop(lo, hi, row)

    def spread(name, up, lo, hi):
        level = FIELDS[name][0]
        n = level.ny + 8

        def row(x):
            val = get(name, x, PAD - 4, n)
            R[up][x - lo, pl.ds(8, n, stride=2), :] = val
            R[up][x - lo, pl.ds(9, n, stride=2), :] = val

        loop(lo, hi, row)

    for k, name in enumerate(("U1", "U2", "U0", "S")):
        for copy in loads[2 * k : 2 * k + 2]:
            copy.wait()
        turn((1, 2, 0, 3)[k], name)
    pl.semaphore_wait(barrier, len(others))
    ex_u0, ex_u1, ex_u2, ex_s = Exchange("u0", "U0"), Exchange("u1", "U1"), Exchange("u2", "U2"), Exchange("s", "S")
    for ex in (ex_u1, ex_u2, ex_u0):
        ex.start_y()
    ex_u1.start_x()
    ex_u1.start_diagonal()
    ex_s.start()

    coarsen(L0, lambda x, r, n: get("S", x, r, n), 0, 8, lambda x, v: put("S1", x, PAD, 64, v), "RS")
    coarsen(L1, lambda x, r, n: get("S1", x, r, n), 0, 4, lambda x, v: put("S2", x, PAD, 32, v), "RC")

    for ex in (ex_u1, ex_u2, ex_u0):
        ex.finish_y()

    def target(x, r, n, low=True, high=True):
        before, after = z_pair(get("U0", x, r, n), 1)
        d = (after - before) + (get("U2", x, r + 1, n) - get("U2", x, r - 1, n))
        if high:
            d = d + get("U1", x + 1, r, n)
        if low:
            d = d - get("U1", x - 1, r, n)
        put("B", x, r, n, -0.5 * d)

    for k, x in enumerate((0, 1, 14, 15)):
        for r, n in L0.parts:
            target(x, r, n, low=x > 0, high=x < 15)
            R["BE"][k, pl.ds(r, n), :] = get("B", x, r, n)
    rows_b = Rows("B", 2, 0, R["BE"])
    ex_s1, ex_s2 = Exchange("s1", "S1"), Exchange("s2", "S2")
    ex_s2.start()
    ex_s1.start()
    each(L0, 2, 14, target)

    def weights(s, w, lo, hi):
        level = FIELDS[s][0]

        def fn(x, r, n):
            put(w, x, r, n, 0.8 / (6.0 * level.scale + get(s, x, r, n)))

        each(level, lo, hi, fn)
        clear_y(w, lo, hi)

    def down_0(v1, keep, r_to, parts):
        for lo, hi in parts[0]:
            sweep(v1, "W", "B", "VB", lo, hi, also=keep)
        for lo, hi in parts[1]:
            coarsen(L0, functools.partial(remainder, "VB", "S", "B"), lo, hi, lambda x, v: put(r_to, x, PAD, 64, v), "RS")

    def coarse_weights_2():
        ex_s2.finish()
        weights("S2", "W2", -6, 10)
        clear_x("W2", 6)
        one = jnp.ones((L2.rows, 128), F32)
        for x in range(16):
            R["I2"][x] = one
        clear_x("I2", 6)
        clear_y("I2", -6, 10)

        def a_one(x, r, n):
            c, s = around("I2", x, r, n)
            put("X2", x, r, n, (6.0 * L2.scale + get("S2", x, r, n)) * c - L2.scale * s)
            put("Z2", x, r, n, c)

        each(L2, -4, 8, a_one)
        lo, hi = -4, 8
        for k in range(4):

            def weigh(x, r, n):
                e = get("W2", x, r, n) * get("X2", x, r, n)
                put("Y2", x, r, n, e)
                put("Z2", x, r, n, get("Z2", x, r, n) - e)

            each(L2, lo, hi, weigh)
            lo, hi = lo + 1, hi - 1
            if k < 3:

                def again(x, r, n):
                    put("X2", x, r, n, 0.2 * get("X2", x, r, n) + L2.scale * around("Y2", x, r, n)[1])

                each(L2, lo, hi, again)
        spread("Z2", "UP1", -1, 5)

    def coarse_weights_1():
        ex_s1.finish()
        weights("S1", "W1", -6, 14)
        clear_x("W1", 6)

        def scaled(x2):
            for k in range(2):
                for r, n in L1.parts:
                    put("X1", 2 * x2 + k, r, n, 0.125 * R["UP1"][x2 + 1, pl.ds(r, n), :])

        loop(-1, 5, scaled, 3)

        def a_of(x, r, n):
            c, s = around("X1", x, r, n)
            y = (6.0 * L1.scale + get("S1", x, r, n)) * c - L1.scale * s
            put("Y1", x, r, n, y)
            put("Z1", x, r, n, get("W1", x, r, n) * y)

        each(L1, -1, 9, a_of)

        def last(x, r, n):
            e, s = around("Z1", x, r, n)
            t = 0.2 * get("Y1", x, r, n) + L1.scale * s
            put("Q1", x, r, n, get("X1", x, r, n) - (e + get("W1", x, r, n) * t))

        each(L1, 0, 8, last)

    def coarse(b1, b2, source, ex1, ex2, sums, work, first):
        total = jnp.zeros((8, 128), F32)
        for x in range(8):
            val = get("Q1", x, PAD, 64) * get(b1, x, PAD, 64)
            total = total + jnp.sum(val.reshape(8, 8, 128), axis=0)
        R[sums + "_a"][...] = jnp.zeros((8, 128), F32)
        R[sums + "_a"][0:1] = jnp.sum(total, axis=0, keepdims=True) * 0.5
        if first:
            mass = jnp.zeros((8, 128), F32)
            for x in range(4):
                mass = mass + jnp.sum(get("S2", x, PAD, 32).reshape(4, 8, 128), axis=0)
            R[sums + "_a"][1:2] = jnp.sum(mass, axis=0, keepdims=True) * 0.25
        part_a = [remote(R[sums + "_a"], R[sums + "_ya"].at[k], 0, k) for k in range(1, ngy)]
        ex1.finish()
        first_sweep("W1", b1, "X1", -6, 14)
        sweep("X1", "W1", b1, "Y1", -5, 13)
        coarsen(L1, functools.partial(remainder, "Y1", "S1", b1), -2, 6, lambda x, v: put(source, x, PAD, 32, v), "RC")
        for x in range(4):
            put(b2, x, PAD, 32, get(source, x, PAD, 32))
        ex2 = Exchange(ex2, b2, source)
        ex2.start()
        both = R[sums + "_a"][...]
        for k, copy in zip(range(1, ngy), part_a, strict=True):
            copy.wait_recv()
            both = both + R[sums + "_ya"][k]
        R[sums + "_b"][...] = both
        part_b = [remote(R[sums + "_b"], R[sums + "_yb"].at[k], k, 0) for k in range(1, ngx)]
        work()
        ex2.finish()
        first_sweep("W2", b2, "X2", -6, 10)
        sweep("X2", "W2", b2, "Y2", -5, 9)
        sweep("Y2", "W2", b2, "X2", -4, 8)
        sweep("X2", "W2", b2, "Y2", -3, 7)
        for k, copy in zip(range(1, ngx), part_b, strict=True):
            copy.wait_recv()
            both = both + R[sums + "_yb"][k]
        return both

    def total_of(row):
        return jnp.sum(row, axis=1, keepdims=True)

    def up(shift, b1):
        def lift(x, r, n):
            put("X2", x, r, n, get("Y2", x, r, n) + shift * get("I2", x, r, n))

        each(L2, -3, 7, lift)
        spread("X2", "UP1", -3, 7)

        def add(x2):
            for k in range(2):
                for r, n in L1.parts:
                    x = 2 * x2 + k
                    put("Y1", x, r, n, get("Y1", x, r, n) + R["UP1"][x2 + 3, pl.ds(r, n), :])

        loop(-3, 7, add, 2)
        sweep("Y1", "W1", b1, "X1", -4, 12)
        sweep("X1", "W1", b1, "Z1", -3, 11)
        spread("Z1", "UP", -3, 11)

    def up_0(kept, p):
        def add(x, x1):
            for r, n in L0.parts:
                put(kept, x, r, n, get(kept, x, r, n) + R["UP"][x1 + 3, pl.ds(r, n), :])

        def pair(x1):
            add(2 * x1, x1)
            add(2 * x1 + 1, x1)

        add(-5, -3)
        loop(-2, 10, pair, 3)
        add(20, 10)
        sweep(kept, "W", "B", "VC", -4, 20)
        sweep("VC", "W", "B", p, -3, 19)

    ex_s.finish_y()
    weights("S", "W", 0, 16)
    first_sweep("W", "B", "VA", 1, 15)
    down_0("VA", "PA", "BA1", ([(2, 14)], [(2, 6)]))
    coarse_weights_2()
    ex_u1.finish_x()
    ex_s.finish_x()
    weights("S", "W", -2, 0)
    weights("S", "W", 16, 18)
    clear_x("W", 2)
    for copy in rows_b.x:
        copy.wait_recv()
    for x, beside, sign in ((-1, 0, -0.5), (0, -1, 0.5), (15, 16, -0.5), (16, 15, 0.5)):
        for r, n in L0.parts:
            put("B", x, r, n, get("B", x, r, n) + sign * get("U1", beside, r, n))
    first_sweep("W", "B", "VA", -2, 1)
    first_sweep("W", "B", "VA", 15, 18)
    down_0("VA", "PA", "BA1", ([(-1, 2), (14, 17)], [(0, 2), (6, 8)]))
    ex1 = Exchange("ba1", "BA1")
    ex1.start()
    rows_v = Rows("PA", 5)
    coarse_weights_1()
    later = []

    def send_bs():
        later.append(Rows("B", 4, 2))
        later.append(Rows("S", 4, 2))

    sums_a = coarse("BA1", "BA2", "SA2", ex1, "ba2", "ra", send_bs, True)
    whole = (64 // 4, 16 * ngx // 4, 256 * ngy // 4)
    faces = 2.0 * (whole[0] * whole[1] + whole[1] * whole[2] + whole[0] * whole[2])
    mass = total_of(sums_a[1:2]) + L2.scale * faces
    up(total_of(sums_a[0:1]) / mass, "BA1")
    for rows in later:
        rows.finish()
    weights("S", "W", -4, -2)
    weights("S", "W", 18, 20)
    clear_x("W", 4)
    rows_v.finish()
    for copy in rows_v.x:
        copy.wait_send()
    up_0("PA", "P1")

    sweep("P1", "W", "B", "VA", -2, 18)
    down_0("VA", "PB", "BB1", ([(-1, 17)], [(0, 8)]))
    ex1 = Exchange("bb1", "BB1")
    ex1.start()
    ex_v = Exchange("v", "PB")
    ex_v.start()
    later = []

    def send_u():
        later.append(Rows("U1", 2, 1))
        later.append(Rows("U0", 1))
        later.append(Rows("U2", 1))

    sums_b = coarse("BB1", "BB2", "SB2", ex1, "bb2", "rb", send_u, False)
    up(total_of(sums_b[0:1]) / mass, "BB1")
    ex_v.finish()
    for copy in ex_v.x:
        copy.wait_send()
    up_0("PB", "P2")

    def back(x):
        t = get("P2", x, PAD, 128).T
        for half in range(2):
            R["back"][half, pl.ds(x, 64, stride=16), :] = t[64 * half : 64 * half + 64]

    loop(0, 16, back, 8)
    stores = []
    for half in range(2):
        copy = pltpu.make_async_copy(R["back"].at[half], p_hbm.at[:, pl.ds(128 * half, 128)], R["local"].at[8 + half])
        copy.start()
        stores.append(copy)

    for rows in later:
        rows.finish()

    def move_1(x, r, n):
        put("VB", x, r, n, get("U1", x, r, n) - 0.5 * (get("P2", x + 1, r, n) - get("P2", x - 1, r, n)))

    each(L0, -2, 18, move_1)

    def move_02(x, r, n):
        before, after = z_pair(get("P2", x, r, n), 1)
        put("VA", x, r, n, get("U0", x, r, n) - 0.5 * (after - before))
        put("VC", x, r, n, get("U2", x, r, n) - 0.5 * (get("P2", x, r + 1, n) - get("P2", x, r - 1, n)))

    each(L0, -1, 17, move_02)
    clear_x("VB", 2)
    clear_y("VB", -2, 18)
    for name in ("VA", "VC"):
        clear_x(name, 1)
        clear_y(name, -1, 17)

    def product(a, b, x, r, n):
        return get(a, x, r, n) * get(b, x, r, n)

    def flux_1(x, r, n):
        d = product("VB", "VB", x + 1, r, n) - product("VB", "VB", x - 1, r, n)
        d = d + 2.0 * (product("VB", "VC", x, r + 1, n) - product("VB", "VC", x, r - 1, n))
        put("PB", x, r, n, d)

    each(L0, -1, 17, flux_1, own=True)
    clear_x("PB", 1)

    def flux_2(x, r, n):
        put("W", x, r, n, product("VC", "VC", x, r + 1, n) - product("VC", "VC", x, r - 1, n))

    each(L0, 0, 16, flux_2)
    clear_y("W", 0, 16)

    def source(x, r, n):
        before, after = z_pair(product("VA", "VA", x, r, n), 1)
        d = product("VA", "VB", x + 1, r, n) - product("VA", "VB", x - 1, r, n)
        d = d + (product("VA", "VC", x, r + 1, n) - product("VA", "VC", x, r - 1, n))
        before, after = z_pair((after - before) + 2.0 * d, 1)
        d = (after - before) + (get("PB", x + 1, r, n) - get("PB", x - 1, r, n))
        return 0.25 * (d + (get("W", x, r + 1, n) - get("W", x, r - 1, n)))

    coarsen(L0, source, 0, 8, lambda x, v: put("X1", x, PAD, 64, v), "RS")

    first = lanes(64) < 64
    for x in range(0, 8, 2):
        t = jnp.concatenate([get("X1", x, PAD, 64), get("X1", x + 1, PAD, 64)], axis=0).T
        low, high = t[:64], t[64:]
        R["G"][pl.ds(x, 64, stride=8), :] = jnp.where(first, low, pltpu.roll(high, 64, 1))
        R["G"][pl.ds(x + 1, 64, stride=8), :] = jnp.where(first, pltpu.roll(low, 64, 1), high)
    for z in range(32):
        R["GZ"][z] = R["G"][pl.ds(16 * z, 8), :]
    for p in range(32):
        R["out"][p] = R["GZ"][levels_ref[p]]
    own = 32 // ngx
    mine = a_hbm.at[:, pl.ds(gx * 8, 8), :]
    copy = pltpu.make_async_copy(R["out"].at[pl.ds(gx * own, own)], mine, R["local"].at[10])
    copy.start()
    stores.append(copy)
    last_ones = []
    for k in range(1, ngx):
        peer = lax.rem(gx + k, ngx)
        last_ones.append(remote(R["out"].at[pl.ds(peer * own, own)], mine, k, 0))
    for copy in last_ones:
        copy.wait_recv()
    for copy in stores:
        copy.wait()
    done = [id(copy) for copy in rows_v.x + ex_v.x]
    for copy in sent:
        if id(copy) not in done:
            copy.wait_send()


def solution(mesh):
    ngx, ngy = mesh.shape["gx"], mesh.shape["gy"]
    shapes = scratch(ngx, ngy)

    def body(velocity, screen, levels):
        pressure, acoustic = pl.pallas_call(
            functools.partial(kernel, tuple(shapes), ngx, ngy),
            out_shape=(
                jax.ShapeDtypeStruct((1024, 256), F32),
                jax.ShapeDtypeStruct((32 // ngx, 8 * ngx, 128), F32),
            ),
            in_specs=[
                pl.BlockSpec(memory_space=pltpu.SMEM),
                pl.BlockSpec(memory_space=pl.ANY),
                pl.BlockSpec(memory_space=pl.ANY),
            ],
            out_specs=(pl.BlockSpec(memory_space=pl.ANY), pl.BlockSpec(memory_space=pl.ANY)),
            scratch_shapes=list(shapes.values()),
            compiler_params=pltpu.CompilerParams(
                collective_id=0, has_side_effects=True, vmem_limit_bytes=60 * 2**20
            ),
        )(levels, velocity.reshape(3, 1024, 256), screen.reshape(1024, 256))
        return pressure.reshape(64, 16, 256), acoustic

    in_specs = (P(None, None, "gx", "gy"), P(None, "gx", "gy"), P())
    out_specs = (P(None, "gx", "gy"), P("gx", None, "gy"))
    return jax.shard_map(body, mesh=mesh, in_specs=in_specs, out_specs=out_specs, check_vma=False)
```

```python
import functools

import jax
import jax.numpy as jnp
from jax import lax
from jax.experimental import pallas as pl
from jax.experimental.pallas import tpu as pltpu
from jax.sharding import PartitionSpec as P


F32 = jnp.float32
MESH = pl.DeviceIdType.MESH
PAD = 16


class Level:
    def __init__(self, nx, ny, lane, scale, chunks):
        self.nx, self.ny, self.lane, self.scale = nx, ny, lane, scale
        self.rows = ny + 2 * PAD
        step = (ny + 16) // chunks
        self.parts = [(8 + k * step, step) for k in range(chunks)]
        own = ny // max(1, ny // 64)
        self.own = [(PAD + k * own, own) for k in range(ny // own)]


L0 = Level(16, 128, 1, 1.0, 3)
L1 = Level(8, 64, 2, 0.25, 2)
L2 = Level(4, 32, 4, 0.0625, 1)

FIELDS = {
    "U0": (L0, 1), "U1": (L0, 2), "U2": (L0, 1),
    "S": (L0, 4), "W": (L0, 4), "B": (L0, 4),
    "VA": (L0, 2), "VB": (L0, 2), "VC": (L0, 4),
    "PA": (L0, 5), "PB": (L0, 5),
    "P1": (L0, 3), "P2": (L0, 3),
    "S1": (L1, 6), "W1": (L1, 6), "BA1": (L1, 6), "BB1": (L1, 6),
    "X1": (L1, 6), "Y1": (L1, 6), "Z1": (L1, 6), "Q1": (L1, 0),
    "S2": (L2, 6), "W2": (L2, 6), "BA2": (L2, 6), "BB2": (L2, 6), "I2": (L2, 6),
    "X2": (L2, 6), "Y2": (L2, 6), "Z2": (L2, 6),
    "SA2": (L2, 2), "SB2": (L2, 2),
}
EXCHANGES = {
    "u0": (L0, 1, 0, False), "u1": (L0, 1, 0, False), "u2": (L0, 1, 0, False), "s": (L0, 2, 0, False), "v": (L0, 5, 0, False),
    "s1": (L1, 6, 0, False), "ba1": (L1, 6, 0, False), "bb1": (L1, 6, 0, False),
    "s2": (L2, 6, 0, True), "ba2": (L2, 6, 2, False), "bb2": (L2, 6, 2, False),
}
SUMS = ("ra", "rb")


def scratch(ngx, ngy):
    shapes = {}
    for name, (level, halo) in FIELDS.items():
        shapes[name] = pltpu.VMEM((level.nx + 2 * halo, level.rows, 128), F32)
    for name, (level, halo, more, _) in EXCHANGES.items():
        if level.lane > 1:
            packed = level.ny // level.lane
            shapes[name + "_px"] = pltpu.VMEM((level.nx + 2 * more, packed, 128), F32)
            shapes[name + "_qx"] = pltpu.VMEM((2, halo, packed, 128), F32)
        slots = max(-(-halo // level.lane), -(-level.nx // level.lane))
        for side in "lr":
            shapes[name + "_s" + side] = pltpu.VMEM((3, slots, 8, 128), F32)
            shapes[name + "_y" + side] = pltpu.VMEM((3, slots, 8, 128), F32)
    for name in SUMS:
        shapes[name + "_a"] = pltpu.VMEM((8, 128), F32)
        shapes[name + "_b"] = pltpu.VMEM((8, 128), F32)
        shapes[name + "_ya"] = pltpu.VMEM((ngy, 8, 128), F32)
        shapes[name + "_yb"] = pltpu.VMEM((ngx, 8, 128), F32)
    shapes["BE"] = pltpu.VMEM((4, L0.rows, 128), F32)
    shapes["raw"] = pltpu.VMEM((4, 2, 1024, 128), F32)
    shapes["back"] = pltpu.VMEM((2, 1024, 128), F32)
    shapes["UP"] = pltpu.VMEM((14, L0.rows, 128), F32)
    shapes["UP1"] = pltpu.VMEM((10, L1.rows, 128), F32)
    shapes["RS"] = pltpu.VMEM((8, 128, 128), F32)
    shapes["RC"] = pltpu.VMEM((8, 64, 128), F32)
    shapes["G"] = pltpu.VMEM((64 * 8, 128), F32)
    shapes["GZ"] = pltpu.VMEM((32, 8, 128), F32)
    shapes["out"] = pltpu.VMEM((32, 8, 128), F32)
    shapes["ship"] = pltpu.SemaphoreType.DMA((256,))
    shapes["land"] = pltpu.SemaphoreType.DMA((256,))
    shapes["local"] = pltpu.SemaphoreType.DMA((16,))
    return shapes


def kernel(names, ngx, ngy, levels_ref, u_hbm, s_hbm, p_hbm, a_hbm, *refs):
    R = dict(zip(names, refs, strict=True))
    gx, gy = lax.axis_index("gx"), lax.axis_index("gy")
    slots = [0]
    sent = []

    def at(dx, dy):
        return (lax.rem(gx + dx + ngx, ngx), lax.rem(gy + dy + ngy, ngy))

    def remote(src, dst, dx, dy):
        k = slots[0]
        slots[0] += 1
        copy = pltpu.make_async_remote_copy(
            src_ref=src,
            dst_ref=dst,
            send_sem=R["ship"].at[k],
            recv_sem=R["land"].at[k],
            device_id=at(dx, dy),
            device_id_type=MESH,
        )
        copy.start()
        sent.append(copy)
        return copy

    def lanes(n):
        return lax.broadcasted_iota(jnp.int32, (n, 128), 1)

    def loop(lo, hi, fn, step=None):
        n = hi - lo
        if step is None:
            step = next((k for k in (5, 4, 6, 3) if n % k == 0), 4)
        whole = n // step

        def body(i, carry):
            for k in range(step):
                fn(lo + i * step + k)
            return carry

        if whole > 1:
            lax.fori_loop(0, whole, body, 0)
        else:
            whole = 0
        for x in range(lo + whole * step, hi):
            fn(x)

    loads = []
    for k, part in enumerate((1, 2, 0, 3)):
        for half in range(2):
            cols = pl.ds(128 * half, 128)
            src = s_hbm.at[:, cols] if part == 3 else u_hbm.at[part, :, cols]
            copy = pltpu.make_async_copy(src, R["raw"].at[part, half], R["local"].at[2 * k + half])
            copy.start()
            loads.append(copy)

    barrier = pltpu.get_barrier_semaphore()
    others = [(k, 0) for k in range(1, ngx)] + [(0, k) for k in range(1, ngy)]
    others += [(dx, dy) for dx in (-2, -1, 1, 2) for dy in (-1, 1)]
    for dx, dy in others:
        pl.semaphore_signal(barrier, inc=1, device_id=at(dx, dy), device_id_type=MESH)

    def turn(part, name):
        dst, halo = R[name], FIELDS[name][1]

        def one(x):
            both = [R["raw"][part, half, pl.ds(x, 64, stride=16), :] for half in range(2)]
            dst[x + halo, pl.ds(PAD, 128), :] = jnp.concatenate(both, axis=0).T

        loop(0, 16, one, 8)

    class Exchange:
        def __init__(self, name, field, source=None):
            self.name, self.field, self.source = name, field, source or field
            self.level, self.h, self.more, self.far = EXCHANGES[name]
            self.halo, self.shalo = FIELDS[field][1], FIELDS[self.source][1]
            self.sl, self.sr, self.yl, self.yr = (R[name + k] for k in ("_sl", "_sr", "_yl", "_yr"))

        def hops(self):
            nx, h = self.level.nx, self.h
            if not self.far:
                return [(1, 0, 0, range(nx - h, nx)), (-1, 2, 0, range(h))]
            more = h - nx
            return [(1, 0, 1, range(nx)), (-1, 2, 0, range(nx)), (2, 0, 0, range(nx - more, nx)), (-2, 2, 1, range(more))]

        def slot(self, x):
            nx, h, d = self.level.nx, self.h, self.level.lane
            if 0 <= x < nx:
                return 1, x // d, x % d
            if x < 0:
                k, cut, kind = x + h, h - nx, 0
            else:
                k, cut, kind = x - nx, nx, 2
            if not self.far:
                return kind, k // d, k % d
            return (kind, 0, k) if k < cut else (kind, 1, k - cut)

        def pack(self, kind, slot, rows):
            lv, src, d = self.level, R[self.source], self.level.lane
            count = -(-len(rows) // d)
            which = lanes(8) & (d - 1)
            for buf, row in ((self.sl, PAD), (self.sr, PAD + lv.ny - 8)):
                if d == 1:
                    n = len(rows)
                    val = src[pl.ds(rows[0] + self.shalo, n), pl.ds(row, 8), :].reshape(n * 8, 128)
                    buf[kind, pl.ds(slot, n)] = pltpu.roll(val, 64, 1).reshape(n, 8, 128)
                    continue
                for q in range(count):
                    val = None
                    for g, x in enumerate(rows[q * d : q * d + d]):
                        edge = src[x + self.shalo, pl.ds(row, 8), :]
                        val = edge if val is None else jnp.where(which == g, edge, val)
                    buf[kind, slot + q] = pltpu.roll(val, 64, 1)
            return pl.ds(slot, count)

        def start_y(self):
            at = self.pack(1, 0, range(self.level.nx)) or pl.ds(0, self.level.nx)
            self.y = [
                remote(self.sr.at[1, at], self.yl.at[1, at], 0, 1),
                remote(self.sl.at[1, at], self.yr.at[1, at], 0, -1),
            ]

        def start_diagonal(self):
            self.d = []
            for dx, kind, slot, rows in self.hops():
                at = self.pack(kind, slot, rows) or pl.ds(slot, len(rows))
                self.d.append(remote(self.sr.at[kind, at], self.yl.at[kind, at], dx, 1))
                self.d.append(remote(self.sl.at[kind, at], self.yr.at[kind, at], dx, -1))

        def start_x(self, near=0, far=None):
            lv, src, dst = self.level, R[self.source], R[self.field]
            if lv.lane == 1:
                far = far or self.h
                cols, n, a, e = pl.ds(PAD, lv.ny), far - near, self.halo, self.shalo
                self.x = getattr(self, "x", []) + [
                    remote(src.at[pl.ds(e + lv.nx - far, n), cols], dst.at[pl.ds(a - far, n), cols], 1, 0),
                    remote(src.at[pl.ds(e + near, n), cols], dst.at[pl.ds(a + lv.nx + near, n), cols], -1, 0),
                ]
                return
            px, qx, m = R[self.name + "_px"], R[self.name + "_qx"], lv.ny // lv.lane
            which = lanes(m) & (lv.lane - 1)
            for i in range(lv.nx + 2 * self.more):
                val = src[i + self.shalo - self.more, pl.ds(PAD, m), :]
                for g in range(1, lv.lane):
                    val = jnp.where(which == g, src[i + self.shalo - self.more, pl.ds(PAD + g * m, m), :], val)
                px[i] = val
            self.x = []
            for dx, kind, slot, rows in self.hops():
                to = (self.h - lv.nx if kind == 0 else lv.nx) if slot else 0
                rows = pl.ds(rows[0] + self.more, len(rows))
                self.x.append(remote(px.at[rows], qx.at[kind // 2, pl.ds(to, rows.size)], dx, 0))

        def spread_lanes(self, val, g):
            which = lanes(val.shape[0]) & (self.level.lane - 1)
            t = jnp.where(which == g, val, 0.0)
            for bit in (1, 2)[: self.level.lane // 2]:
                t = t + pltpu.roll(t, 128 - bit if g & bit else bit, 1)
            return t

        def unpack(self):
            lv, f, qx = self.level, R[self.field], R[self.name + "_qx"]
            m = lv.ny // lv.lane
            for side in range(2):
                for i in range(self.h):
                    val = qx[side, i]
                    row = self.halo - self.h + i if side == 0 else self.halo + lv.nx + i
                    for g in range(lv.lane):
                        f[row, pl.ds(PAD + g * m, m), :] = self.spread_lanes(val, g)

        def start(self):
            self.start_diagonal()
            self.start_x()
            self.start_y()

        def wait(self, which):
            for copy in getattr(self, which):
                copy.wait_recv()

        def join(self, lo, hi):
            lv, f = self.level, R[self.field]
            inside = jnp.where(gx > 0, 1.0, 0.0) if hi <= 0 else jnp.where(gx < ngx - 1, 1.0, 0.0) if lo >= lv.nx else 1.0
            left = jnp.where(gy > 0, 1.0, 0.0) * inside
            right = jnp.where(gy < ngy - 1, 1.0, 0.0) * inside
            first = lanes(8) < 64
            if lv.lane > 1:
                for x in range(lo, hi):
                    kind, slot, g = self.slot(x)
                    cells = f.at[x + self.halo]
                    top, low = cells[pl.ds(PAD + lv.ny - 8, 8), :], cells[pl.ds(PAD, 8), :]
                    got = self.spread_lanes(self.yl[kind, slot] * left, g)
                    cells[pl.ds(PAD - 8, 8), :] = jnp.where(first, got, pltpu.roll(top, 64, 1))
                    got = self.spread_lanes(self.yr[kind, slot] * right, g)
                    cells[pl.ds(PAD + lv.ny, 8), :] = jnp.where(first, pltpu.roll(low, 64, 1), got)
                return
            n = hi - lo
            rows = pl.ds(lo + self.halo, n)
            kind, slot, _ = self.slot(lo)
            first = lanes(n * 8) < 64
            top = f[rows, pl.ds(PAD + lv.ny - 8, 8), :].reshape(n * 8, 128)
            got = self.yl[kind, pl.ds(slot, n)].reshape(n * 8, 128) * left
            f[rows, pl.ds(PAD - 8, 8), :] = jnp.where(first, got, pltpu.roll(top, 64, 1)).reshape(n, 8, 128)
            low = f[rows, pl.ds(PAD, 8), :].reshape(n * 8, 128)
            got = self.yr[kind, pl.ds(slot, n)].reshape(n * 8, 128) * right
            f[rows, pl.ds(PAD + lv.ny, 8), :] = jnp.where(first, pltpu.roll(low, 64, 1), got).reshape(n, 8, 128)

        def finish_x(self):
            self.wait("x")
            if self.level.lane > 1:
                self.unpack()
            clear_x(self.field, self.h)
            self.wait("d")
            self.join(-self.h, 0)
            self.join(self.level.nx, self.level.nx + self.h)

        def finish_y(self):
            self.wait("y")
            self.join(0, self.level.nx)

        def finish(self):
            self.finish_y()
            self.finish_x()

    def clear_x(name, h):
        level, halo = FIELDS[name]
        f, zero = R[name], jnp.zeros((level.rows, 128), F32)

        @pl.when(gx == 0)
        def _():
            for x in range(-h, 0):
                f[x + halo] = zero

        @pl.when(gx == ngx - 1)
        def _():
            for x in range(level.nx, level.nx + h):
                f[x + halo] = zero

        if h > level.nx:

            @pl.when(gx == 1)
            def _():
                for x in range(-h, -level.nx):
                    f[x + halo] = zero

            @pl.when(gx == ngx - 2)
            def _():
                for x in range(2 * level.nx, level.nx + h):
                    f[x + halo] = zero

    def clear_y(name, lo, hi):
        level, halo = FIELDS[name]
        f, n = R[name], hi - lo
        rows = pl.ds(halo + lo, n)

        def side(row, first):
            cells = (rows, pl.ds(row, 8), slice(None))
            val = f[cells].reshape(n * 8, 128)
            keep = lanes(n * 8) >= 64 if first else lanes(n * 8) < 64
            f[cells] = jnp.where(keep, val, 0.0).reshape(n, 8, 128)

        @pl.when(gy == 0)
        def _():
            side(PAD - 8, True)

        @pl.when(gy == ngy - 1)
        def _():
            side(PAD + level.ny, False)

    class Rows:
        def __init__(self, field, far, near=0, source=None):
            self.field, self.h = field, far
            level, a = FIELDS[field]
            nx, f, cols, n = level.nx, R[field], pl.ds(8, level.ny + 16), far - near
            last, first = (f.at[pl.ds(a + nx - far, n), cols], f.at[pl.ds(a + near, n), cols])
            if source is not None:
                last, first = source.at[pl.ds(n, n), cols], source.at[pl.ds(0, n), cols]
            self.x = [
                remote(last, f.at[pl.ds(a - far, n), cols], 1, 0),
                remote(first, f.at[pl.ds(a + nx + near, n), cols], -1, 0),
            ]

        def finish(self):
            for copy in self.x:
                copy.wait_recv()
            clear_x(self.field, self.h)

    def z_pair(c, lane):
        n = c.shape[0]
        z = lanes(n) & 63
        before = jnp.where(z >= lane, pltpu.roll(c, lane, 1), 0.0)
        after = jnp.where(z < 64 - lane, pltpu.roll(c, 128 - lane, 1), 0.0)
        return before, after

    def around(name, x, r, n):
        level, halo = FIELDS[name]
        f, i = R[name], x + halo
        c = f[i, pl.ds(r, n), :]
        before, after = z_pair(c, level.lane)
        side = f[i - 1, pl.ds(r, n), :] + f[i + 1, pl.ds(r, n), :]
        side = side + (f[i, pl.ds(r - 1, n), :] + f[i, pl.ds(r + 1, n), :])
        return c, side + (before + after)

    def get(name, x, r, n):
        return R[name][x + FIELDS[name][1], pl.ds(r, n), :]

    def put(name, x, r, n, val):
        R[name][x + FIELDS[name][1], pl.ds(r, n), :] = val

    def each(level, lo, hi, fn, own=False, step=None):
        def row(x):
            for r, n in level.own if own else level.parts:
                fn(x, r, n)

        loop(lo, hi, row, step)

    def first_sweep(w, b, to, lo, hi):
        def fn(x, r, n):
            put(to, x, r, n, get(w, x, r, n) * get(b, x, r, n))

        each(FIELDS[to][0], lo, hi, fn)

    def sweep(v, w, b, to, lo, hi, also=None):
        level = FIELDS[v][0]

        def fn(x, r, n, twice=also is not None):
            c, s = around(v, x, r, n)
            s = s if level.scale == 1.0 else s * level.scale
            new = 0.2 * c + get(w, x, r, n) * (get(b, x, r, n) + s)
            put(to, x, r, n, new)
            if twice:
                put(also, x, r, n, new)

        if also is None:
            each(level, lo, hi, fn)
        else:
            each(level, max(lo, 0), min(hi, level.nx), fn)
            each(level, lo, min(hi, 0), functools.partial(fn, twice=False))
            each(level, max(lo, level.nx), hi, functools.partial(fn, twice=False))

    def remainder(v, s, b, x, r, n):
        level = FIELDS[v][0]
        c, around_sum = around(v, x, r, n)
        return get(b, x, r, n) + level.scale * around_sum - (6.0 * level.scale + get(s, x, r, n)) * c

    def halve(pair, buf, k, lane):
        ny = pair[0].shape[0] * len(pair)
        for j, val in enumerate(pair):
            R[buf][k, pl.ds(j * val.shape[0], val.shape[0]), :] = val
        a = R[buf][k, pl.ds(0, ny // 2, stride=2), :] + R[buf][k, pl.ds(1, ny // 2, stride=2), :]
        even = (lanes(ny // 2) & lane) == 0
        return (a + jnp.where(even, pltpu.roll(a, 128 - lane, 1), pltpu.roll(a, lane, 1))) * 0.125

    def coarsen(level, fn, lo, hi, write, buf):
        def row(x):
            pair = [fn(2 * x, r, n) + fn(2 * x + 1, r, n) for r, n in level.own]
            write(x, halve(pair, buf, (x + 2) & 7 if lo < 0 else x, level.lane))

        loop(lo, hi, row)

    def spread(name, up, lo, hi):
        level = FIELDS[name][0]
        n = level.ny + 8

        def row(x):
            val = get(name, x, PAD - 4, n)
            R[up][x - lo, pl.ds(8, n, stride=2), :] = val
            R[up][x - lo, pl.ds(9, n, stride=2), :] = val

        loop(lo, hi, row)

    for k, name in enumerate(("U1", "U2", "U0", "S")):
        for copy in loads[2 * k : 2 * k + 2]:
            copy.wait()
        turn((1, 2, 0, 3)[k], name)
    pl.semaphore_wait(barrier, len(others))
    ex_u0, ex_u1, ex_u2, ex_s = Exchange("u0", "U0"), Exchange("u1", "U1"), Exchange("u2", "U2"), Exchange("s", "S")
    for ex in (ex_u1, ex_u2, ex_u0):
        ex.start_y()
    ex_u1.start_x()
    ex_u1.start_diagonal()
    ex_s.start()

    coarsen(L0, lambda x, r, n: get("S", x, r, n), 0, 8, lambda x, v: put("S1", x, PAD, 64, v), "RS")
    coarsen(L1, lambda x, r, n: get("S1", x, r, n), 0, 4, lambda x, v: put("S2", x, PAD, 32, v), "RC")

    for ex in (ex_u1, ex_u2, ex_u0):
        ex.finish_y()

    def target(x, r, n, low=True, high=True):
        before, after = z_pair(get("U0", x, r, n), 1)
        d = (after - before) + (get("U2", x, r + 1, n) - get("U2", x, r - 1, n))
        if high:
            d = d + get("U1", x + 1, r, n)
        if low:
            d = d - get("U1", x - 1, r, n)
        put("B", x, r, n, -0.5 * d)

    for k, x in enumerate((0, 1, 14, 15)):
        for r, n in L0.parts:
            target(x, r, n, low=x > 0, high=x < 15)
            R["BE"][k, pl.ds(r, n), :] = get("B", x, r, n)
    rows_b = Rows("B", 2, 0, R["BE"])
    ex_s1, ex_s2 = Exchange("s1", "S1"), Exchange("s2", "S2")
    ex_s2.start()
    ex_s1.start()
    each(L0, 2, 14, target)

    def weights(s, w, lo, hi):
        level = FIELDS[s][0]

        def fn(x, r, n):
            put(w, x, r, n, 0.8 / (6.0 * level.scale + get(s, x, r, n)))

        each(level, lo, hi, fn)
        clear_y(w, lo, hi)

    def down_0(v1, keep, r_to, parts):
        for lo, hi in parts[0]:
            sweep(v1, "W", "B", "VB", lo, hi, also=keep)
        for lo, hi in parts[1]:
            coarsen(L0, functools.partial(remainder, "VB", "S", "B"), lo, hi, lambda x, v: put(r_to, x, PAD, 64, v), "RS")

    def coarse_weights_2():
        ex_s2.finish()
        weights("S2", "W2", -6, 10)
        clear_x("W2", 6)
        one = jnp.ones((L2.rows, 128), F32)
        for x in range(16):
            R["I2"][x] = one
        clear_x("I2", 6)
        clear_y("I2", -6, 10)

        def a_one(x, r, n):
            c, s = around("I2", x, r, n)
            put("X2", x, r, n, (6.0 * L2.scale + get("S2", x, r, n)) * c - L2.scale * s)
            put("Z2", x, r, n, c)

        each(L2, -4, 8, a_one)
        lo, hi = -4, 8
        for k in range(4):

            def weigh(x, r, n):
                e = get("W2", x, r, n) * get("X2", x, r, n)
                put("Y2", x, r, n, e)
                put("Z2", x, r, n, get("Z2", x, r, n) - e)

            each(L2, lo, hi, weigh)
            lo, hi = lo + 1, hi - 1
            if k < 3:

                def again(x, r, n):
                    put("X2", x, r, n, 0.2 * get("X2", x, r, n) + L2.scale * around("Y2", x, r, n)[1])

                each(L2, lo, hi, again)
        spread("Z2", "UP1", -1, 5)

    def coarse_weights_1():
        ex_s1.finish()
        weights("S1", "W1", -6, 14)
        clear_x("W1", 6)

        def scaled(x2):
            for k in range(2):
                for r, n in L1.parts:
                    put("X1", 2 * x2 + k, r, n, 0.125 * R["UP1"][x2 + 1, pl.ds(r, n), :])

        loop(-1, 5, scaled, 3)

        def a_of(x, r, n):
            c, s = around("X1", x, r, n)
            y = (6.0 * L1.scale + get("S1", x, r, n)) * c - L1.scale * s
            put("Y1", x, r, n, y)
            put("Z1", x, r, n, get("W1", x, r, n) * y)

        each(L1, -1, 9, a_of)

        def last(x, r, n):
            e, s = around("Z1", x, r, n)
            t = 0.2 * get("Y1", x, r, n) + L1.scale * s
            put("Q1", x, r, n, get("X1", x, r, n) - (e + get("W1", x, r, n) * t))

        each(L1, 0, 8, last)

    def coarse(b1, b2, source, ex1, ex2, sums, work, first):
        total = jnp.zeros((8, 128), F32)
        for x in range(8):
            val = get("Q1", x, PAD, 64) * get(b1, x, PAD, 64)
            total = total + jnp.sum(val.reshape(8, 8, 128), axis=0)
        R[sums + "_a"][...] = jnp.zeros((8, 128), F32)
        R[sums + "_a"][0:1] = jnp.sum(total, axis=0, keepdims=True) * 0.5
        if first:
            mass = jnp.zeros((8, 128), F32)
            for x in range(4):
                mass = mass + jnp.sum(get("S2", x, PAD, 32).reshape(4, 8, 128), axis=0)
            R[sums + "_a"][1:2] = jnp.sum(mass, axis=0, keepdims=True) * 0.25
        part_a = [remote(R[sums + "_a"], R[sums + "_ya"].at[k], 0, k) for k in range(1, ngy)]
        ex1.finish()
        first_sweep("W1", b1, "X1", -6, 14)
        sweep("X1", "W1", b1, "Y1", -5, 13)
        coarsen(L1, functools.partial(remainder, "Y1", "S1", b1), -2, 6, lambda x, v: put(source, x, PAD, 32, v), "RC")
        for x in range(4):
            put(b2, x, PAD, 32, get(source, x, PAD, 32))
        ex2 = Exchange(ex2, b2, source)
        ex2.start()
        both = R[sums + "_a"][...]
        for k, copy in zip(range(1, ngy), part_a, strict=True):
            copy.wait_recv()
            both = both + R[sums + "_ya"][k]
        R[sums + "_b"][...] = both
        part_b = [remote(R[sums + "_b"], R[sums + "_yb"].at[k], k, 0) for k in range(1, ngx)]
        work()
        ex2.finish()
        first_sweep("W2", b2, "X2", -6, 10)
        sweep("X2", "W2", b2, "Y2", -5, 9)
        sweep("Y2", "W2", b2, "X2", -4, 8)
        sweep("X2", "W2", b2, "Y2", -3, 7)
        for k, copy in zip(range(1, ngx), part_b, strict=True):
            copy.wait_recv()
            both = both + R[sums + "_yb"][k]
        return both

    def total_of(row):
        return jnp.sum(row, axis=1, keepdims=True)

    def up(shift, b1):
        def lift(x, r, n):
            put("X2", x, r, n, get("Y2", x, r, n) + shift * get("I2", x, r, n))

        each(L2, -3, 7, lift)
        spread("X2", "UP1", -3, 7)

        def add(x2):
            for k in range(2):
                for r, n in L1.parts:
                    x = 2 * x2 + k
                    put("Y1", x, r, n, get("Y1", x, r, n) + R["UP1"][x2 + 3, pl.ds(r, n), :])

        loop(-3, 7, add, 2)
        sweep("Y1", "W1", b1, "X1", -4, 12)
        sweep("X1", "W1", b1, "Z1", -3, 11)
        spread("Z1", "UP", -3, 11)

    def up_0(kept, p):
        def add(x, x1):
            for r, n in L0.parts:
                put(kept, x, r, n, get(kept, x, r, n) + R["UP"][x1 + 3, pl.ds(r, n), :])

        def pair(x1):
            add(2 * x1, x1)
            add(2 * x1 + 1, x1)

        add(-5, -3)
        loop(-2, 10, pair, 3)
        add(20, 10)
        sweep(kept, "W", "B", "VC", -4, 20)
        sweep("VC", "W", "B", p, -3, 19)

    ex_s.finish_y()
    weights("S", "W", 0, 16)
    first_sweep("W", "B", "VA", 1, 15)
    down_0("VA", "PA", "BA1", ([(2, 14)], [(2, 6)]))
    rows_v = [Rows("PA", 5, 2)]
    coarse_weights_2()
    ex_u1.finish_x()
    ex_s.finish_x()
    weights("S", "W", -2, 0)
    weights("S", "W", 16, 18)
    clear_x("W", 2)
    for copy in rows_b.x:
        copy.wait_recv()
    for x, beside, sign in ((-1, 0, -0.5), (0, -1, 0.5), (15, 16, -0.5), (16, 15, 0.5)):
        for r, n in L0.parts:
            put("B", x, r, n, get("B", x, r, n) + sign * get("U1", beside, r, n))
    first_sweep("W", "B", "VA", -2, 1)
    first_sweep("W", "B", "VA", 15, 18)
    down_0("VA", "PA", "BA1", ([(-1, 2), (14, 17)], [(0, 2), (6, 8)]))
    ex1 = Exchange("ba1", "BA1")
    ex1.start()
    rows_v.append(Rows("PA", 2))
    coarse_weights_1()
    later = []

    def send_bs():
        later.append(Rows("B", 4, 2))
        later.append(Rows("S", 4, 2))

    sums_a = coarse("BA1", "BA2", "SA2", ex1, "ba2", "ra", send_bs, True)
    whole = (64 // 4, 16 * ngx // 4, 256 * ngy // 4)
    faces = 2.0 * (whole[0] * whole[1] + whole[1] * whole[2] + whole[0] * whole[2])
    mass = total_of(sums_a[1:2]) + L2.scale * faces
    up(total_of(sums_a[0:1]) / mass, "BA1")
    for rows in later:
        rows.finish()
    weights("S", "W", -4, -2)
    weights("S", "W", 18, 20)
    clear_x("W", 4)
    for copy in rows_v[0].x + rows_v[1].x:
        copy.wait()
    clear_x("PA", 5)
    later = [Rows("U1", 2, 1), Rows("U0", 1), Rows("U2", 1)]
    up_0("PA", "P1")

    sweep("P1", "W", "B", "VA", -2, 18)
    down_0("VA", "PB", "BB1", ([(-1, 17)], [(0, 8)]))
    ex1 = Exchange("bb1", "BB1")
    ex1.start()
    ex_v = Exchange("v", "PB")
    ex_v.start_x(0, 3)
    ex_v.start_diagonal()
    ex_v.start_y()
    sums_b = coarse("BB1", "BB2", "SB2", ex1, "bb2", "rb", lambda: ex_v.start_x(3, 5), False)
    up(total_of(sums_b[0:1]) / mass, "BB1")
    ex_v.finish()
    for copy in ex_v.x:
        copy.wait_send()
    up_0("PB", "P2")

    for rows in later:
        rows.finish()

    def move_1(x, r, n):
        put("VB", x, r, n, get("U1", x, r, n) - 0.5 * (get("P2", x + 1, r, n) - get("P2", x - 1, r, n)))

    each(L0, -2, 18, move_1)

    def move_02(x, r, n):
        before, after = z_pair(get("P2", x, r, n), 1)
        put("VA", x, r, n, get("U0", x, r, n) - 0.5 * (after - before))
        put("VC", x, r, n, get("U2", x, r, n) - 0.5 * (get("P2", x, r + 1, n) - get("P2", x, r - 1, n)))

    each(L0, -1, 17, move_02)
    clear_x("VB", 2)
    clear_y("VB", -2, 18)
    for name in ("VA", "VC"):
        clear_x(name, 1)
        clear_y(name, -1, 17)

    def product(a, b, x, r, n):
        return get(a, x, r, n) * get(b, x, r, n)

    def flux_1(x, r, n):
        d = product("VB", "VB", x + 1, r, n) - product("VB", "VB", x - 1, r, n)
        d = d + 2.0 * (product("VB", "VC", x, r + 1, n) - product("VB", "VC", x, r - 1, n))
        put("PB", x, r, n, d)

    each(L0, -1, 17, flux_1, own=True)
    clear_x("PB", 1)

    def flux_2(x, r, n):
        put("W", x, r, n, product("VC", "VC", x, r + 1, n) - product("VC", "VC", x, r - 1, n))

    each(L0, 0, 16, flux_2)
    clear_y("W", 0, 16)

    def source(x, r, n):
        before, after = z_pair(product("VA", "VA", x, r, n), 1)
        d = product("VA", "VB", x + 1, r, n) - product("VA", "VB", x - 1, r, n)
        d = d + (product("VA", "VC", x, r + 1, n) - product("VA", "VC", x, r - 1, n))
        before, after = z_pair((after - before) + 2.0 * d, 1)
        d = (after - before) + (get("PB", x + 1, r, n) - get("PB", x - 1, r, n))
        return 0.25 * (d + (get("W", x, r + 1, n) - get("W", x, r - 1, n)))

    coarsen(L0, source, 0, 8, lambda x, v: put("X1", x, PAD, 64, v), "RS")

    first = lanes(64) < 64
    for x in range(0, 8, 2):
        t = jnp.concatenate([get("X1", x, PAD, 64), get("X1", x + 1, PAD, 64)], axis=0).T
        low, high = t[:64], t[64:]
        R["G"][pl.ds(x, 64, stride=8), :] = jnp.where(first, low, pltpu.roll(high, 64, 1))
        R["G"][pl.ds(x + 1, 64, stride=8), :] = jnp.where(first, pltpu.roll(low, 64, 1), high)
    for z in range(32):
        R["GZ"][z] = R["G"][pl.ds(16 * z, 8), :]
    for p in range(32):
        R["out"][p] = R["GZ"][levels_ref[p]]
    own = 32 // ngx
    stores = []
    mine = a_hbm.at[:, pl.ds(gx * 8, 8), :]
    copy = pltpu.make_async_copy(R["out"].at[pl.ds(gx * own, own)], mine, R["local"].at[10])
    copy.start()
    stores.append(copy)
    last_ones = []
    for k in range(1, ngx):
        peer = lax.rem(gx + k, ngx)
        last_ones.append(remote(R["out"].at[pl.ds(peer * own, own)], mine, k, 0))
    def back(x):
        t = get("P2", x, PAD, 128).T
        for half in range(2):
            R["back"][half, pl.ds(x, 64, stride=16), :] = t[64 * half : 64 * half + 64]

    loop(0, 16, back, 8)
    for half in range(2):
        copy = pltpu.make_async_copy(R["back"].at[half], p_hbm.at[:, pl.ds(128 * half, 128)], R["local"].at[8 + half])
        copy.start()
        stores.append(copy)

    for copy in last_ones:
        copy.wait_recv()
    for copy in stores:
        copy.wait()
    done = [id(copy) for copy in rows_v[0].x + rows_v[1].x + ex_v.x]
    for copy in sent:
        if id(copy) not in done:
            copy.wait_send()


def hand_on(p_ref, a_ref, p_out, a_out, p_buf, a_buf, come, go):
    copies = []
    for k in range(9):
        rows = pl.ds(128 * k, 128)
        refs = [r.at[rows] for r in (p_ref, p_buf, p_out)] if k < 8 else [a_ref, a_buf, a_out]
        copies.append(
            (
                pltpu.make_async_copy(refs[0], refs[1], come.at[k]),
                pltpu.make_async_copy(refs[1], refs[2], go.at[k]),
            )
        )
    for first, _ in copies:
        first.start()
    for first, second in copies:
        first.wait()
        second.start()
    for _, second in copies:
        second.wait()


def solution(mesh):
    ngx, ngy = mesh.shape["gx"], mesh.shape["gy"]
    shapes = scratch(ngx, ngy)

    def body(velocity, screen, levels):
        pressure, acoustic = pl.pallas_call(
            functools.partial(kernel, tuple(shapes), ngx, ngy),
            out_shape=(
                jax.ShapeDtypeStruct((1024, 256), F32),
                jax.ShapeDtypeStruct((32 // ngx, 8 * ngx, 128), F32),
            ),
            in_specs=[
                pl.BlockSpec(memory_space=pltpu.SMEM),
                pl.BlockSpec(memory_space=pl.ANY),
                pl.BlockSpec(memory_space=pl.ANY),
            ],
            out_specs=(pl.BlockSpec(memory_space=pl.ANY), pl.BlockSpec(memory_space=pl.ANY)),
            scratch_shapes=list(shapes.values()),
            compiler_params=pltpu.CompilerParams(
                collective_id=0, has_side_effects=True, vmem_limit_bytes=60 * 2**20
            ),
        )(levels, velocity.reshape(3, 1024, 256), screen.reshape(1024, 256))
        pressure, acoustic = pl.pallas_call(
            hand_on,
            out_shape=(
                jax.ShapeDtypeStruct(pressure.shape, F32),
                jax.ShapeDtypeStruct(acoustic.shape, F32),
            ),
            in_specs=[pl.BlockSpec(memory_space=pl.ANY)] * 2,
            out_specs=[pl.BlockSpec(memory_space=pl.ANY)] * 2,
            scratch_shapes=[
                pltpu.VMEM(pressure.shape, F32),
                pltpu.VMEM(acoustic.shape, F32),
                pltpu.SemaphoreType.DMA((9,)),
                pltpu.SemaphoreType.DMA((9,)),
            ],
            compiler_params=pltpu.CompilerParams(vmem_limit_bytes=60 * 2**20),
        )(pressure, acoustic)
        return pressure.reshape(64, 16, 256), acoustic

    in_specs = (P(None, None, "gx", "gy"), P(None, "gx", "gy"), P())
    out_specs = (P(None, "gx", "gy"), P("gx", None, "gy"))
    return jax.shard_map(body, mesh=mesh, in_specs=in_specs, out_specs=out_specs, check_vma=False)
```

```python
import functools

import jax
import jax.numpy as jnp
from jax import lax
from jax.experimental import pallas as pl
from jax.experimental.pallas import tpu as pltpu
from jax.sharding import PartitionSpec as P


F32 = jnp.float32
MESH = pl.DeviceIdType.MESH
PAD = 16


class Level:
    def __init__(self, nx, ny, lane, scale, chunks):
        self.nx, self.ny, self.lane, self.scale = nx, ny, lane, scale
        self.rows = ny + 2 * PAD
        step = (ny + 16) // chunks
        self.parts = [(8 + k * step, step) for k in range(chunks)]
        own = ny // max(1, ny // 64)
        self.own = [(PAD + k * own, own) for k in range(ny // own)]


L0 = Level(16, 128, 1, 1.0, 3)
L1 = Level(8, 64, 2, 0.25, 2)
L2 = Level(4, 32, 4, 0.0625, 1)

FIELDS = {
    "U0": (L0, 1), "U1": (L0, 2), "U2": (L0, 1),
    "S": (L0, 4), "W": (L0, 4), "B": (L0, 4),
    "VA": (L0, 2), "VB": (L0, 2), "VC": (L0, 4),
    "PA": (L0, 5), "PB": (L0, 5),
    "P1": (L0, 3), "P2": (L0, 3),
    "S1": (L1, 6), "W1": (L1, 6), "BA1": (L1, 6), "BB1": (L1, 6),
    "X1": (L1, 6), "Y1": (L1, 6), "Z1": (L1, 6), "Q1": (L1, 0),
    "S2": (L2, 6), "W2": (L2, 6), "BA2": (L2, 6), "BB2": (L2, 6), "I2": (L2, 6),
    "X2": (L2, 6), "Y2": (L2, 6), "Z2": (L2, 6),
    "SA2": (L2, 2), "SB2": (L2, 2),
}
EXCHANGES = {
    "u0": (L0, 1, 0, False), "u1": (L0, 1, 0, False), "u2": (L0, 1, 0, False), "s": (L0, 2, 0, False), "v": (L0, 5, 0, False),
    "s1": (L1, 6, 0, False), "ba1": (L1, 6, 0, False), "bb1": (L1, 6, 0, False),
    "s2": (L2, 6, 0, True), "ba2": (L2, 6, 2, False), "bb2": (L2, 6, 2, False),
}
SUMS = ("ra", "rb")


def scratch(ngx, ngy):
    shapes = {}
    for name, (level, halo) in FIELDS.items():
        shapes[name] = pltpu.VMEM((level.nx + 2 * halo, level.rows, 128), F32)
    for name, (level, halo, more, _) in EXCHANGES.items():
        if level.lane > 1:
            packed = level.ny // level.lane
            shapes[name + "_px"] = pltpu.VMEM((level.nx + 2 * more, packed, 128), F32)
            shapes[name + "_qx"] = pltpu.VMEM((2, halo, packed, 128), F32)
        slots = max(-(-halo // level.lane), -(-level.nx // level.lane))
        for side in "lr":
            shapes[name + "_s" + side] = pltpu.VMEM((3, slots, 8, 128), F32)
            shapes[name + "_y" + side] = pltpu.VMEM((3, slots, 8, 128), F32)
    for name in SUMS:
        shapes[name + "_a"] = pltpu.VMEM((8, 128), F32)
        shapes[name + "_b"] = pltpu.VMEM((8, 128), F32)
        shapes[name + "_ya"] = pltpu.VMEM((ngy, 8, 128), F32)
        shapes[name + "_yb"] = pltpu.VMEM((ngx, 8, 128), F32)
    shapes["BE"] = pltpu.VMEM((4, L0.rows, 128), F32)
    shapes["raw"] = pltpu.VMEM((4, 2, 1024, 128), F32)
    shapes["back"] = pltpu.VMEM((2, 1024, 128), F32)
    shapes["UP"] = pltpu.VMEM((14, L0.rows, 128), F32)
    shapes["UP1"] = pltpu.VMEM((10, L1.rows, 128), F32)
    shapes["RS"] = pltpu.VMEM((8, 128, 128), F32)
    shapes["RC"] = pltpu.VMEM((8, 64, 128), F32)
    shapes["G"] = pltpu.VMEM((64 * 8, 128), F32)
    shapes["GZ"] = pltpu.VMEM((32, 8, 128), F32)
    shapes["out"] = pltpu.VMEM((32, 8, 128), F32)
    shapes["ship"] = pltpu.SemaphoreType.DMA((256,))
    shapes["land"] = pltpu.SemaphoreType.DMA((256,))
    shapes["local"] = pltpu.SemaphoreType.DMA((16,))
    return shapes


def kernel(names, ngx, ngy, levels_ref, u_hbm, s_hbm, p_hbm, a_hbm, *refs):
    R = dict(zip(names, refs, strict=True))
    gx, gy = lax.axis_index("gx"), lax.axis_index("gy")
    slots = [0]
    sent = []

    def at(dx, dy):
        return (lax.rem(gx + dx + ngx, ngx), lax.rem(gy + dy + ngy, ngy))

    def remote(src, dst, dx, dy):
        k = slots[0]
        slots[0] += 1
        copy = pltpu.make_async_remote_copy(
            src_ref=src,
            dst_ref=dst,
            send_sem=R["ship"].at[k],
            recv_sem=R["land"].at[k],
            device_id=at(dx, dy),
            device_id_type=MESH,
        )
        copy.start()
        sent.append(copy)
        return copy

    def lanes(n):
        return lax.broadcasted_iota(jnp.int32, (n, 128), 1)

    def loop(lo, hi, fn, step=None):
        n = hi - lo
        if step is None:
            step = next((k for k in (8, 9, 10, 7, 6, 5) if n % k == 0), n)
        whole = n // step

        def body(i, carry):
            for k in range(step):
                fn(lo + i * step + k)
            return carry

        if whole > 1:
            lax.fori_loop(0, whole, body, 0)
        else:
            whole = 0
        for x in range(lo + whole * step, hi):
            fn(x)

    loads = []
    for k, part in enumerate((1, 2, 0, 3)):
        for half in range(2):
            cols = pl.ds(128 * half, 128)
            src = s_hbm.at[:, cols] if part == 3 else u_hbm.at[part, :, cols]
            copy = pltpu.make_async_copy(src, R["raw"].at[part, half], R["local"].at[2 * k + half])
            copy.start()
            loads.append(copy)

    barrier = pltpu.get_barrier_semaphore()
    others = [(k, 0) for k in range(1, ngx)] + [(0, k) for k in range(1, ngy)]
    others += [(dx, dy) for dx in (-2, -1, 1, 2) for dy in (-1, 1)]
    for dx, dy in others:
        pl.semaphore_signal(barrier, inc=1, device_id=at(dx, dy), device_id_type=MESH)

    def turn(part, name):
        dst, halo = R[name], FIELDS[name][1]

        def one(x):
            both = [R["raw"][part, half, pl.ds(x, 64, stride=16), :] for half in range(2)]
            dst[x + halo, pl.ds(PAD, 128), :] = jnp.concatenate(both, axis=0).T

        loop(0, 16, one, 8)

    class Exchange:
        def __init__(self, name, field, source=None):
            self.name, self.field, self.source = name, field, source or field
            self.level, self.h, self.more, self.far = EXCHANGES[name]
            self.halo, self.shalo = FIELDS[field][1], FIELDS[self.source][1]
            self.sl, self.sr, self.yl, self.yr = (R[name + k] for k in ("_sl", "_sr", "_yl", "_yr"))

        def hops(self):
            nx, h = self.level.nx, self.h
            if not self.far:
                return [(1, 0, 0, range(nx - h, nx)), (-1, 2, 0, range(h))]
            more = h - nx
            return [(1, 0, 1, range(nx)), (-1, 2, 0, range(nx)), (2, 0, 0, range(nx - more, nx)), (-2, 2, 1, range(more))]

        def slot(self, x):
            nx, h, d = self.level.nx, self.h, self.level.lane
            if 0 <= x < nx:
                return 1, x // d, x % d
            if x < 0:
                k, cut, kind = x + h, h - nx, 0
            else:
                k, cut, kind = x - nx, nx, 2
            if not self.far:
                return kind, k // d, k % d
            return (kind, 0, k) if k < cut else (kind, 1, k - cut)

        def pack(self, kind, slot, rows):
            lv, src, d = self.level, R[self.source], self.level.lane
            count = -(-len(rows) // d)
            which = lanes(8) & (d - 1)
            for buf, row in ((self.sl, PAD), (self.sr, PAD + lv.ny - 8)):
                if d == 1:
                    n = len(rows)
                    val = src[pl.ds(rows[0] + self.shalo, n), pl.ds(row, 8), :].reshape(n * 8, 128)
                    buf[kind, pl.ds(slot, n)] = pltpu.roll(val, 64, 1).reshape(n, 8, 128)
                    continue
                for q in range(count):
                    val = None
                    for g, x in enumerate(rows[q * d : q * d + d]):
                        edge = src[x + self.shalo, pl.ds(row, 8), :]
                        val = edge if val is None else jnp.where(which == g, edge, val)
                    buf[kind, slot + q] = pltpu.roll(val, 64, 1)
            return pl.ds(slot, count)

        def start_y(self):
            at = self.pack(1, 0, range(self.level.nx)) or pl.ds(0, self.level.nx)
            self.y = [
                remote(self.sr.at[1, at], self.yl.at[1, at], 0, 1),
                remote(self.sl.at[1, at], self.yr.at[1, at], 0, -1),
            ]

        def start_diagonal(self):
            self.d = []
            for dx, kind, slot, rows in self.hops():
                at = self.pack(kind, slot, rows) or pl.ds(slot, len(rows))
                self.d.append(remote(self.sr.at[kind, at], self.yl.at[kind, at], dx, 1))
                self.d.append(remote(self.sl.at[kind, at], self.yr.at[kind, at], dx, -1))

        def start_x(self, near=0, far=None):
            lv, src, dst = self.level, R[self.source], R[self.field]
            if lv.lane == 1:
                far = far or self.h
                cols, n, a, e = pl.ds(PAD, lv.ny), far - near, self.halo, self.shalo
                self.x = getattr(self, "x", []) + [
                    remote(src.at[pl.ds(e + lv.nx - far, n), cols], dst.at[pl.ds(a - far, n), cols], 1, 0),
                    remote(src.at[pl.ds(e + near, n), cols], dst.at[pl.ds(a + lv.nx + near, n), cols], -1, 0),
                ]
                return
            px, qx, m = R[self.name + "_px"], R[self.name + "_qx"], lv.ny // lv.lane
            which = lanes(m) & (lv.lane - 1)
            for i in range(lv.nx + 2 * self.more):
                val = src[i + self.shalo - self.more, pl.ds(PAD, m), :]
                for g in range(1, lv.lane):
                    val = jnp.where(which == g, src[i + self.shalo - self.more, pl.ds(PAD + g * m, m), :], val)
                px[i] = val
            self.x = []
            for dx, kind, slot, rows in self.hops():
                to = (self.h - lv.nx if kind == 0 else lv.nx) if slot else 0
                rows = pl.ds(rows[0] + self.more, len(rows))
                self.x.append(remote(px.at[rows], qx.at[kind // 2, pl.ds(to, rows.size)], dx, 0))

        def spread_lanes(self, val, g):
            which = lanes(val.shape[0]) & (self.level.lane - 1)
            t = jnp.where(which == g, val, 0.0)
            for bit in (1, 2)[: self.level.lane // 2]:
                t = t + pltpu.roll(t, 128 - bit if g & bit else bit, 1)
            return t

        def unpack(self):
            lv, f, qx = self.level, R[self.field], R[self.name + "_qx"]
            m = lv.ny // lv.lane
            for side in range(2):
                for i in range(self.h):
                    val = qx[side, i]
                    row = self.halo - self.h + i if side == 0 else self.halo + lv.nx + i
                    for g in range(lv.lane):
                        f[row, pl.ds(PAD + g * m, m), :] = self.spread_lanes(val, g)

        def start(self):
            self.start_diagonal()
            self.start_x()
            self.start_y()

        def wait(self, which):
            for copy in getattr(self, which):
                copy.wait_recv()

        def join(self, lo, hi):
            lv, f = self.level, R[self.field]
            inside = jnp.where(gx > 0, 1.0, 0.0) if hi <= 0 else jnp.where(gx < ngx - 1, 1.0, 0.0) if lo >= lv.nx else 1.0
            left = jnp.where(gy > 0, 1.0, 0.0) * inside
            right = jnp.where(gy < ngy - 1, 1.0, 0.0) * inside
            first = lanes(8) < 64
            if lv.lane > 1:
                for x in range(lo, hi):
                    kind, slot, g = self.slot(x)
                    cells = f.at[x + self.halo]
                    top, low = cells[pl.ds(PAD + lv.ny - 8, 8), :], cells[pl.ds(PAD, 8), :]
                    got = self.spread_lanes(self.yl[kind, slot] * left, g)
                    cells[pl.ds(PAD - 8, 8), :] = jnp.where(first, got, pltpu.roll(top, 64, 1))
                    got = self.spread_lanes(self.yr[kind, slot] * right, g)
                    cells[pl.ds(PAD + lv.ny, 8), :] = jnp.where(first, pltpu.roll(low, 64, 1), got)
                return
            n = hi - lo
            rows = pl.ds(lo + self.halo, n)
            kind, slot, _ = self.slot(lo)
            first = lanes(n * 8) < 64
            top = f[rows, pl.ds(PAD + lv.ny - 8, 8), :].reshape(n * 8, 128)
            got = self.yl[kind, pl.ds(slot, n)].reshape(n * 8, 128) * left
            f[rows, pl.ds(PAD - 8, 8), :] = jnp.where(first, got, pltpu.roll(top, 64, 1)).reshape(n, 8, 128)
            low = f[rows, pl.ds(PAD, 8), :].reshape(n * 8, 128)
            got = self.yr[kind, pl.ds(slot, n)].reshape(n * 8, 128) * right
            f[rows, pl.ds(PAD + lv.ny, 8), :] = jnp.where(first, pltpu.roll(low, 64, 1), got).reshape(n, 8, 128)

        def finish_x(self):
            self.wait("x")
            if self.level.lane > 1:
                self.unpack()
            clear_x(self.field, self.h)
            self.wait("d")
            self.join(-self.h, 0)
            self.join(self.level.nx, self.level.nx + self.h)

        def finish_y(self):
            self.wait("y")
            self.join(0, self.level.nx)

        def finish(self):
            self.finish_y()
            self.finish_x()

    def clear_x(name, h):
        level, halo = FIELDS[name]
        f, zero = R[name], jnp.zeros((level.rows, 128), F32)

        @pl.when(gx == 0)
        def _():
            for x in range(-h, 0):
                f[x + halo] = zero

        @pl.when(gx == ngx - 1)
        def _():
            for x in range(level.nx, level.nx + h):
                f[x + halo] = zero

        if h > level.nx:

            @pl.when(gx == 1)
            def _():
                for x in range(-h, -level.nx):
                    f[x + halo] = zero

            @pl.when(gx == ngx - 2)
            def _():
                for x in range(2 * level.nx, level.nx + h):
                    f[x + halo] = zero

    def clear_y(name, lo, hi):
        level, halo = FIELDS[name]
        f, n = R[name], hi - lo
        rows = pl.ds(halo + lo, n)

        def side(row, first):
            cells = (rows, pl.ds(row, 8), slice(None))
            val = f[cells].reshape(n * 8, 128)
            keep = lanes(n * 8) >= 64 if first else lanes(n * 8) < 64
            f[cells] = jnp.where(keep, val, 0.0).reshape(n, 8, 128)

        @pl.when(gy == 0)
        def _():
            side(PAD - 8, True)

        @pl.when(gy == ngy - 1)
        def _():
            side(PAD + level.ny, False)

    class Rows:
        def __init__(self, field, far, near=0, source=None, cols=None):
            self.field, self.h = field, far
            level, a = FIELDS[field]
            nx, f, n = level.nx, R[field], far - near
            cols = pl.ds(8, level.ny + 16) if cols is None else pl.ds(*cols)
            last, first = (f.at[pl.ds(a + nx - far, n), cols], f.at[pl.ds(a + near, n), cols])
            if source is not None:
                last, first = source.at[pl.ds(n, n), cols], source.at[pl.ds(0, n), cols]
            self.x = [
                remote(last, f.at[pl.ds(a - far, n), cols], 1, 0),
                remote(first, f.at[pl.ds(a + nx + near, n), cols], -1, 0),
            ]

        def finish(self):
            for copy in self.x:
                copy.wait_recv()
            clear_x(self.field, self.h)

    def z_pair(c, lane):
        n = c.shape[0]
        z = lanes(n) & 63
        before = jnp.where(z >= lane, pltpu.roll(c, lane, 1), 0.0)
        after = jnp.where(z < 64 - lane, pltpu.roll(c, 128 - lane, 1), 0.0)
        return before, after

    def around(name, x, r, n):
        level, halo = FIELDS[name]
        f, i = R[name], x + halo
        c = f[i, pl.ds(r, n), :]
        before, after = z_pair(c, level.lane)
        side = f[i - 1, pl.ds(r, n), :] + f[i + 1, pl.ds(r, n), :]
        side = side + (f[i, pl.ds(r - 1, n), :] + f[i, pl.ds(r + 1, n), :])
        return c, side + (before + after)

    def get(name, x, r, n):
        return R[name][x + FIELDS[name][1], pl.ds(r, n), :]

    def put(name, x, r, n, val):
        R[name][x + FIELDS[name][1], pl.ds(r, n), :] = val

    def each(level, lo, hi, fn, own=False):
        def row(x):
            for r, n in level.own if own else level.parts:
                fn(x, r, n)

        loop(lo, hi, row, hi - lo if level is L2 else None)

    def first_sweep(w, b, to, lo, hi):
        def fn(x, r, n):
            put(to, x, r, n, get(w, x, r, n) * get(b, x, r, n))

        each(FIELDS[to][0], lo, hi, fn)

    def sweep(v, w, b, to, lo, hi, also=None):
        level = FIELDS[v][0]

        def fn(x, r, n, twice=also is not None):
            c, s = around(v, x, r, n)
            s = s if level.scale == 1.0 else s * level.scale
            new = 0.2 * c + get(w, x, r, n) * (get(b, x, r, n) + s)
            put(to, x, r, n, new)
            if twice:
                put(also, x, r, n, new)

        if also is None:
            each(level, lo, hi, fn)
        else:
            each(level, max(lo, 0), min(hi, level.nx), fn)
            each(level, lo, min(hi, 0), functools.partial(fn, twice=False))
            each(level, max(lo, level.nx), hi, functools.partial(fn, twice=False))

    def remainder(v, s, b, x, r, n):
        level = FIELDS[v][0]
        c, around_sum = around(v, x, r, n)
        return get(b, x, r, n) + level.scale * around_sum - (6.0 * level.scale + get(s, x, r, n)) * c

    def halve(pair, buf, k, lane):
        ny = pair[0].shape[0] * len(pair)
        for j, val in enumerate(pair):
            R[buf][k, pl.ds(j * val.shape[0], val.shape[0]), :] = val
        a = R[buf][k, pl.ds(0, ny // 2, stride=2), :] + R[buf][k, pl.ds(1, ny // 2, stride=2), :]
        even = (lanes(ny // 2) & lane) == 0
        return (a + jnp.where(even, pltpu.roll(a, 128 - lane, 1), pltpu.roll(a, lane, 1))) * 0.125

    def coarsen(level, fn, lo, hi, write, buf):
        def row(x):
            pair = [fn(2 * x, r, n) + fn(2 * x + 1, r, n) for r, n in level.own]
            write(x, halve(pair, buf, (x + 2) & 7 if lo < 0 else x, level.lane))

        loop(lo, hi, row)

    def spread(name, up, lo, hi):
        level = FIELDS[name][0]
        n = level.ny + 8

        def row(x):
            val = get(name, x, PAD - 4, n)
            R[up][x - lo, pl.ds(8, n, stride=2), :] = val
            R[up][x - lo, pl.ds(9, n, stride=2), :] = val

        loop(lo, hi, row)

    for k, name in enumerate(("U1", "U2", "U0", "S")):
        for copy in loads[2 * k : 2 * k + 2]:
            copy.wait()
        turn((1, 2, 0, 3)[k], name)
    pl.semaphore_wait(barrier, len(others))
    ex_u0, ex_u1, ex_u2, ex_s = Exchange("u0", "U0"), Exchange("u1", "U1"), Exchange("u2", "U2"), Exchange("s", "S")
    for ex in (ex_u1, ex_u2, ex_u0):
        ex.start_y()
    ex_u1.start_x()

    def target(x, r, n, low=True, high=True):
        before, after = z_pair(get("U0", x, r, n), 1)
        d = (after - before) + (get("U2", x, r + 1, n) - get("U2", x, r - 1, n))
        if high:
            d = d + get("U1", x + 1, r, n)
        if low:
            d = d - get("U1", x - 1, r, n)
        put("B", x, r, n, -0.5 * d)

    def edge_rows(r, n):
        for k, x in enumerate((0, 1, 14, 15)):
            target(x, r, n, low=x > 0, high=x < 15)
            R["BE"][k, pl.ds(r, n), :] = get("B", x, r, n)
        return Rows("B", 2, 0, R["BE"], (r, n))

    rows_b = [edge_rows(PAD + 8, 112)]
    ex_u1.start_diagonal()
    ex_s.start()

    coarsen(L0, lambda x, r, n: get("S", x, r, n), 0, 8, lambda x, v: put("S1", x, PAD, 64, v), "RS")
    coarsen(L1, lambda x, r, n: get("S1", x, r, n), 0, 4, lambda x, v: put("S2", x, PAD, 32, v), "RC")

    for ex in (ex_u1, ex_u2, ex_u0):
        ex.finish_y()
    rows_b += [edge_rows(PAD - 8, 16), edge_rows(PAD + 120, 16)]
    ex_s1, ex_s2 = Exchange("s1", "S1"), Exchange("s2", "S2")
    ex_s2.start()
    ex_s1.start()
    each(L0, 2, 14, target)

    def weights(s, w, lo, hi):
        level = FIELDS[s][0]

        def fn(x, r, n):
            put(w, x, r, n, 0.8 / (6.0 * level.scale + get(s, x, r, n)))

        each(level, lo, hi, fn)
        clear_y(w, lo, hi)

    def down_0(v1, keep, r_to, parts):
        for lo, hi in parts[0]:
            sweep(v1, "W", "B", "VB", lo, hi, also=keep)
        for lo, hi in parts[1]:
            coarsen(L0, functools.partial(remainder, "VB", "S", "B"), lo, hi, lambda x, v: put(r_to, x, PAD, 64, v), "RS")

    def coarse_weights_2():
        ex_s2.finish()
        weights("S2", "W2", -6, 10)
        clear_x("W2", 6)
        one = jnp.ones((L2.rows, 128), F32)
        for x in range(16):
            R["I2"][x] = one
        clear_x("I2", 6)
        clear_y("I2", -6, 10)

        def a_one(x, r, n):
            c, s = around("I2", x, r, n)
            put("X2", x, r, n, (6.0 * L2.scale + get("S2", x, r, n)) * c - L2.scale * s)
            put("Z2", x, r, n, c)

        each(L2, -4, 8, a_one)
        lo, hi = -4, 8
        for k in range(4):

            def weigh(x, r, n):
                e = get("W2", x, r, n) * get("X2", x, r, n)
                put("Y2", x, r, n, e)
                put("Z2", x, r, n, get("Z2", x, r, n) - e)

            each(L2, lo, hi, weigh)
            lo, hi = lo + 1, hi - 1
            if k < 3:

                def again(x, r, n):
                    put("X2", x, r, n, 0.2 * get("X2", x, r, n) + L2.scale * around("Y2", x, r, n)[1])

                each(L2, lo, hi, again)
        spread("Z2", "UP1", -1, 5)

    def coarse_weights_1():
        ex_s1.finish()
        weights("S1", "W1", -6, 14)
        clear_x("W1", 6)

        def scaled(x2):
            for k in range(2):
                for r, n in L1.parts:
                    put("X1", 2 * x2 + k, r, n, 0.125 * R["UP1"][x2 + 1, pl.ds(r, n), :])

        loop(-1, 5, scaled, 3)

        def a_of(x, r, n):
            c, s = around("X1", x, r, n)
            y = (6.0 * L1.scale + get("S1", x, r, n)) * c - L1.scale * s
            put("Y1", x, r, n, y)
            put("Z1", x, r, n, get("W1", x, r, n) * y)

        each(L1, -1, 9, a_of)

        def last(x, r, n):
            e, s = around("Z1", x, r, n)
            t = 0.2 * get("Y1", x, r, n) + L1.scale * s
            put("Q1", x, r, n, get("X1", x, r, n) - (e + get("W1", x, r, n) * t))

        each(L1, 0, 8, last)

    def coarse(b1, b2, source, ex1, ex2, sums, work, first):
        total = jnp.zeros((8, 128), F32)
        for x in range(8):
            val = get("Q1", x, PAD, 64) * get(b1, x, PAD, 64)
            total = total + jnp.sum(val.reshape(8, 8, 128), axis=0)
        R[sums + "_a"][...] = jnp.zeros((8, 128), F32)
        R[sums + "_a"][0:1] = jnp.sum(total, axis=0, keepdims=True) * 0.5
        if first:
            mass = jnp.zeros((8, 128), F32)
            for x in range(4):
                mass = mass + jnp.sum(get("S2", x, PAD, 32).reshape(4, 8, 128), axis=0)
            R[sums + "_a"][1:2] = jnp.sum(mass, axis=0, keepdims=True) * 0.25
        part_a = [remote(R[sums + "_a"], R[sums + "_ya"].at[k], 0, k) for k in range(1, ngy)]
        ex1.finish()
        first_sweep("W1", b1, "X1", -6, 14)
        sweep("X1", "W1", b1, "Y1", -5, 13)
        coarsen(L1, functools.partial(remainder, "Y1", "S1", b1), -2, 6, lambda x, v: put(source, x, PAD, 32, v), "RC")
        for x in range(4):
            put(b2, x, PAD, 32, get(source, x, PAD, 32))
        ex2 = Exchange(ex2, b2, source)
        ex2.start()
        both = R[sums + "_a"][...]
        for k, copy in zip(range(1, ngy), part_a, strict=True):
            copy.wait_recv()
            both = both + R[sums + "_ya"][k]
        R[sums + "_b"][...] = both
        part_b = [remote(R[sums + "_b"], R[sums + "_yb"].at[k], k, 0) for k in range(1, ngx)]
        work()
        ex2.finish()
        first_sweep("W2", b2, "X2", -6, 10)
        sweep("X2", "W2", b2, "Y2", -5, 9)
        sweep("Y2", "W2", b2, "X2", -4, 8)
        sweep("X2", "W2", b2, "Y2", -3, 7)
        for k, copy in zip(range(1, ngx), part_b, strict=True):
            copy.wait_recv()
            both = both + R[sums + "_yb"][k]
        return both

    def total_of(row):
        return jnp.sum(row, axis=1, keepdims=True)

    def up(shift, b1):
        def lift(x, r, n):
            put("X2", x, r, n, get("Y2", x, r, n) + shift * get("I2", x, r, n))

        each(L2, -3, 7, lift)
        spread("X2", "UP1", -3, 7)

        def add(x2):
            for k in range(2):
                for r, n in L1.parts:
                    x = 2 * x2 + k
                    put("Y1", x, r, n, get("Y1", x, r, n) + R["UP1"][x2 + 3, pl.ds(r, n), :])

        loop(-3, 7, add, 5)
        sweep("Y1", "W1", b1, "X1", -4, 12)
        sweep("X1", "W1", b1, "Z1", -3, 11)
        spread("Z1", "UP", -3, 11)

    def up_0(kept, p):
        def add(x, x1):
            for r, n in L0.parts:
                put(kept, x, r, n, get(kept, x, r, n) + R["UP"][x1 + 3, pl.ds(r, n), :])

        def pair(x1):
            add(2 * x1, x1)
            add(2 * x1 + 1, x1)

        add(-5, -3)
        loop(-2, 10, pair, 4)
        add(20, 10)
        sweep(kept, "W", "B", "VC", -4, 20)
        sweep("VC", "W", "B", p, -3, 19)

    ex_s.finish_y()
    weights("S", "W", 0, 16)
    first_sweep("W", "B", "VA", 1, 15)
    down_0("VA", "PA", "BA1", ([(2, 14)], [(2, 6)]))
    rows_v = [Rows("PA", 5, 2)]
    coarse_weights_2()
    ex_u1.finish_x()
    ex_s.finish_x()
    weights("S", "W", -2, 0)
    weights("S", "W", 16, 18)
    clear_x("W", 2)
    for rows in rows_b:
        for copy in rows.x:
            copy.wait_recv()
    for x, beside, sign in ((-1, 0, -0.5), (0, -1, 0.5), (15, 16, -0.5), (16, 15, 0.5)):
        for r, n in L0.parts:
            put("B", x, r, n, get("B", x, r, n) + sign * get("U1", beside, r, n))
    first_sweep("W", "B", "VA", -2, 1)
    first_sweep("W", "B", "VA", 15, 18)
    down_0("VA", "PA", "BA1", ([(-1, 2), (14, 17)], [(0, 2), (6, 8)]))
    ex1 = Exchange("ba1", "BA1")
    ex1.start()
    rows_v.append(Rows("PA", 2))
    coarse_weights_1()
    later = []

    def send_bs():
        later.append(Rows("B", 4, 2))
        later.append(Rows("S", 4, 2))

    sums_a = coarse("BA1", "BA2", "SA2", ex1, "ba2", "ra", send_bs, True)
    whole = (64 // 4, 16 * ngx // 4, 256 * ngy // 4)
    faces = 2.0 * (whole[0] * whole[1] + whole[1] * whole[2] + whole[0] * whole[2])
    mass = total_of(sums_a[1:2]) + L2.scale * faces
    up(total_of(sums_a[0:1]) / mass, "BA1")
    for rows in later:
        rows.finish()
    weights("S", "W", -4, -2)
    weights("S", "W", 18, 20)
    clear_x("W", 4)
    for copy in rows_v[0].x + rows_v[1].x:
        copy.wait()
    clear_x("PA", 5)
    later = [Rows("U1", 2, 1), Rows("U0", 1), Rows("U2", 1)]
    up_0("PA", "P1")

    sweep("P1", "W", "B", "VA", -2, 18)
    down_0("VA", "PB", "BB1", ([(-1, 17)], [(0, 8)]))
    ex1 = Exchange("bb1", "BB1")
    ex1.start()
    ex_v = Exchange("v", "PB")
    ex_v.start_x(0, 3)
    ex_v.start_diagonal()
    ex_v.start_y()
    sums_b = coarse("BB1", "BB2", "SB2", ex1, "bb2", "rb", lambda: ex_v.start_x(3, 5), False)
    up(total_of(sums_b[0:1]) / mass, "BB1")
    ex_v.finish()
    for copy in ex_v.x:
        copy.wait_send()
    up_0("PB", "P2")

    for rows in later:
        rows.finish()

    def move_1(x, r, n):
        put("VB", x, r, n, get("U1", x, r, n) - 0.5 * (get("P2", x + 1, r, n) - get("P2", x - 1, r, n)))

    each(L0, -2, 18, move_1)

    def move_02(x, r, n):
        before, after = z_pair(get("P2", x, r, n), 1)
        put("VA", x, r, n, get("U0", x, r, n) - 0.5 * (after - before))
        put("VC", x, r, n, get("U2", x, r, n) - 0.5 * (get("P2", x, r + 1, n) - get("P2", x, r - 1, n)))

    each(L0, -1, 17, move_02)
    clear_x("VB", 2)
    clear_y("VB", -2, 18)
    for name in ("VA", "VC"):
        clear_x(name, 1)
        clear_y(name, -1, 17)

    def product(a, b, x, r, n):
        return get(a, x, r, n) * get(b, x, r, n)

    def flux_1(x, r, n):
        d = product("VB", "VB", x + 1, r, n) - product("VB", "VB", x - 1, r, n)
        d = d + 2.0 * (product("VB", "VC", x, r + 1, n) - product("VB", "VC", x, r - 1, n))
        put("PB", x, r, n, d)

    each(L0, -1, 17, flux_1, own=True)
    clear_x("PB", 1)

    def flux_2(x, r, n):
        put("W", x, r, n, product("VC", "VC", x, r + 1, n) - product("VC", "VC", x, r - 1, n))

    each(L0, 0, 16, flux_2)
    clear_y("W", 0, 16)

    def source(x, r, n):
        before, after = z_pair(product("VA", "VA", x, r, n), 1)
        d = product("VA", "VB", x + 1, r, n) - product("VA", "VB", x - 1, r, n)
        d = d + (product("VA", "VC", x, r + 1, n) - product("VA", "VC", x, r - 1, n))
        before, after = z_pair((after - before) + 2.0 * d, 1)
        d = (after - before) + (get("PB", x + 1, r, n) - get("PB", x - 1, r, n))
        return 0.25 * (d + (get("W", x, r + 1, n) - get("W", x, r - 1, n)))

    coarsen(L0, source, 0, 8, lambda x, v: put("X1", x, PAD, 64, v), "RS")

    first = lanes(64) < 64
    for x in range(0, 8, 2):
        t = jnp.concatenate([get("X1", x, PAD, 64), get("X1", x + 1, PAD, 64)], axis=0).T
        low, high = t[:64], t[64:]
        R["G"][pl.ds(x, 64, stride=8), :] = jnp.where(first, low, pltpu.roll(high, 64, 1))
        R["G"][pl.ds(x + 1, 64, stride=8), :] = jnp.where(first, pltpu.roll(low, 64, 1), high)
    for z in range(32):
        R["GZ"][z] = R["G"][pl.ds(16 * z, 8), :]
    for p in range(32):
        R["out"][p] = R["GZ"][levels_ref[p]]
    own = 32 // ngx
    stores = []
    mine = a_hbm.at[:, pl.ds(gx * 8, 8), :]
    copy = pltpu.make_async_copy(R["out"].at[pl.ds(gx * own, own)], mine, R["local"].at[10])
    copy.start()
    stores.append(copy)
    last_ones = []
    for k in range(1, ngx):
        peer = lax.rem(gx + k, ngx)
        last_ones.append(remote(R["out"].at[pl.ds(peer * own, own)], mine, k, 0))
    def back(x):
        t = get("P2", x, PAD, 128).T
        for half in range(2):
            R["back"][half, pl.ds(x, 64, stride=16), :] = t[64 * half : 64 * half + 64]

    loop(0, 16, back, 8)
    for half in range(2):
        copy = pltpu.make_async_copy(R["back"].at[half], p_hbm.at[:, pl.ds(128 * half, 128)], R["local"].at[8 + half])
        copy.start()
        stores.append(copy)

    for copy in last_ones:
        copy.wait_recv()
    for copy in stores:
        copy.wait()
    done = [id(copy) for copy in rows_v[0].x + rows_v[1].x + ex_v.x]
    for copy in sent:
        if id(copy) not in done:
            copy.wait_send()


def hand_on(p_ref, a_ref, p_out, a_out, p_buf, a_buf, come, go):
    copies = []
    for k in range(9):
        rows = pl.ds(128 * k, 128)
        refs = [r.at[rows] for r in (p_ref, p_buf, p_out)] if k < 8 else [a_ref, a_buf, a_out]
        copies.append(
            (
                pltpu.make_async_copy(refs[0], refs[1], come.at[k]),
                pltpu.make_async_copy(refs[1], refs[2], go.at[k]),
            )
        )
    for first, _ in copies:
        first.start()
    for first, second in copies:
        first.wait()
        second.start()
    for _, second in copies:
        second.wait()


def solution(mesh):
    ngx, ngy = mesh.shape["gx"], mesh.shape["gy"]
    shapes = scratch(ngx, ngy)

    def body(velocity, screen, levels):
        pressure, acoustic = pl.pallas_call(
            functools.partial(kernel, tuple(shapes), ngx, ngy),
            out_shape=(
                jax.ShapeDtypeStruct((1024, 256), F32),
                jax.ShapeDtypeStruct((32 // ngx, 8 * ngx, 128), F32),
            ),
            in_specs=[
                pl.BlockSpec(memory_space=pltpu.SMEM),
                pl.BlockSpec(memory_space=pl.ANY),
                pl.BlockSpec(memory_space=pl.ANY),
            ],
            out_specs=(pl.BlockSpec(memory_space=pl.ANY), pl.BlockSpec(memory_space=pl.ANY)),
            scratch_shapes=list(shapes.values()),
            compiler_params=pltpu.CompilerParams(
                collective_id=0, has_side_effects=True, vmem_limit_bytes=60 * 2**20
            ),
        )(levels, velocity.reshape(3, 1024, 256), screen.reshape(1024, 256))
        pressure, acoustic = pl.pallas_call(
            hand_on,
            out_shape=(
                jax.ShapeDtypeStruct(pressure.shape, F32),
                jax.ShapeDtypeStruct(acoustic.shape, F32),
            ),
            in_specs=[pl.BlockSpec(memory_space=pl.ANY)] * 2,
            out_specs=[pl.BlockSpec(memory_space=pl.ANY)] * 2,
            scratch_shapes=[
                pltpu.VMEM(pressure.shape, F32),
                pltpu.VMEM(acoustic.shape, F32),
                pltpu.SemaphoreType.DMA((9,)),
                pltpu.SemaphoreType.DMA((9,)),
            ],
            compiler_params=pltpu.CompilerParams(vmem_limit_bytes=60 * 2**20),
        )(pressure, acoustic)
        return pressure.reshape(64, 16, 256), acoustic

    in_specs = (P(None, None, "gx", "gy"), P(None, "gx", "gy"), P())
    out_specs = (P(None, "gx", "gy"), P("gx", None, "gy"))
    return jax.shard_map(body, mesh=mesh, in_specs=in_specs, out_specs=out_specs, check_vma=False)
```

```python
import functools

import jax
import jax.numpy as jnp
from jax import lax
from jax.experimental import pallas as pl
from jax.experimental.pallas import tpu as pltpu
from jax.sharding import PartitionSpec as P


F32 = jnp.float32
MESH = pl.DeviceIdType.MESH
PAD = 16


class Level:
    def __init__(self, nx, ny, lane, scale, chunks):
        self.nx, self.ny, self.lane, self.scale = nx, ny, lane, scale
        self.rows = ny + 2 * PAD
        step = (ny + 16) // chunks
        self.parts = [(8 + k * step, step) for k in range(chunks)]
        own = ny // max(1, ny // 64)
        self.own = [(PAD + k * own, own) for k in range(ny // own)]


L0 = Level(16, 128, 1, 1.0, 3)
L1 = Level(8, 64, 2, 0.25, 2)
L2 = Level(4, 32, 4, 0.0625, 1)

FIELDS = {
    "U0": (L0, 1), "U1": (L0, 2), "U2": (L0, 1),
    "S": (L0, 4), "W": (L0, 4), "B": (L0, 4),
    "VA": (L0, 2), "VB": (L0, 2), "VC": (L0, 4),
    "PA": (L0, 5), "PB": (L0, 5),
    "P1": (L0, 3), "P2": (L0, 3),
    "S1": (L1, 6), "W1": (L1, 6), "BA1": (L1, 6), "BB1": (L1, 6),
    "X1": (L1, 6), "Y1": (L1, 6), "Z1": (L1, 6), "Q1": (L1, 0),
    "S2": (L2, 6), "W2": (L2, 6), "BA2": (L2, 6), "BB2": (L2, 6), "I2": (L2, 6),
    "X2": (L2, 6), "Y2": (L2, 6), "Z2": (L2, 6),
    "SA2": (L2, 2), "SB2": (L2, 2),
}
EXCHANGES = {
    "u0": (L0, 1, 0, False), "u1": (L0, 1, 0, False), "u2": (L0, 1, 0, False), "s": (L0, 2, 0, False), "v": (L0, 5, 0, False),
    "s1": (L1, 6, 0, False), "ba1": (L1, 6, 0, False), "bb1": (L1, 6, 0, False),
    "s2": (L2, 6, 0, True), "ba2": (L2, 6, 2, False), "bb2": (L2, 6, 2, False),
}
SUMS = ("ra", "rb")


def scratch(ngx, ngy):
    shapes = {}
    for name, (level, halo) in FIELDS.items():
        shapes[name] = pltpu.VMEM((level.nx + 2 * halo, level.rows, 128), F32)
    for name, (level, halo, more, _) in EXCHANGES.items():
        if level.lane > 1:
            packed = level.ny // level.lane
            shapes[name + "_px"] = pltpu.VMEM((level.nx + 2 * more, packed, 128), F32)
            shapes[name + "_qx"] = pltpu.VMEM((2, halo, packed, 128), F32)
        slots = max(-(-halo // level.lane), -(-level.nx // level.lane))
        for side in "lr":
            shapes[name + "_s" + side] = pltpu.VMEM((3, slots, 8, 128), F32)
            shapes[name + "_y" + side] = pltpu.VMEM((3, slots, 8, 128), F32)
    for name in SUMS:
        shapes[name + "_a"] = pltpu.VMEM((8, 128), F32)
        shapes[name + "_b"] = pltpu.VMEM((8, 128), F32)
        shapes[name + "_ya"] = pltpu.VMEM((ngy, 8, 128), F32)
        shapes[name + "_yb"] = pltpu.VMEM((ngx, 8, 128), F32)
    shapes["BE"] = pltpu.VMEM((4, L0.rows, 128), F32)
    shapes["raw"] = pltpu.VMEM((4, 2, 1024, 128), F32)
    shapes["back"] = pltpu.VMEM((2, 1024, 128), F32)
    shapes["UP"] = pltpu.VMEM((14, L0.rows, 128), F32)
    shapes["UP1"] = pltpu.VMEM((10, L1.rows, 128), F32)
    shapes["RS"] = pltpu.VMEM((8, 128, 128), F32)
    shapes["RC"] = pltpu.VMEM((8, 64, 128), F32)
    shapes["G"] = pltpu.VMEM((64 * 8, 128), F32)
    shapes["GZ"] = pltpu.VMEM((32, 8, 128), F32)
    shapes["out"] = pltpu.VMEM((32, 8, 128), F32)
    shapes["ship"] = pltpu.SemaphoreType.DMA((256,))
    shapes["land"] = pltpu.SemaphoreType.DMA((256,))
    shapes["local"] = pltpu.SemaphoreType.DMA((16,))
    return shapes


def kernel(names, ngx, ngy, levels_ref, u_hbm, s_hbm, p_hbm, a_hbm, *refs):
    R = dict(zip(names, refs, strict=True))
    gx, gy = lax.axis_index("gx"), lax.axis_index("gy")
    slots = [0]
    sent = []

    def at(dx, dy):
        return (lax.rem(gx + dx + ngx, ngx), lax.rem(gy + dy + ngy, ngy))

    def remote(src, dst, dx, dy):
        k = slots[0]
        slots[0] += 1
        copy = pltpu.make_async_remote_copy(
            src_ref=src,
            dst_ref=dst,
            send_sem=R["ship"].at[k],
            recv_sem=R["land"].at[k],
            device_id=at(dx, dy),
            device_id_type=MESH,
        )
        copy.start()
        sent.append(copy)
        return copy

    def lanes(n):
        return lax.broadcasted_iota(jnp.int32, (n, 128), 1)

    def loop(lo, hi, fn, step=None):
        n = hi - lo
        if step is None:
            step = next((k for k in (8, 9, 10, 7, 6, 5) if n % k == 0), n)
        whole = n // step

        def body(i, carry):
            for k in range(step):
                fn(lo + i * step + k)
            return carry

        if whole > 1:
            lax.fori_loop(0, whole, body, 0)
        else:
            whole = 0
        for x in range(lo + whole * step, hi):
            fn(x)

    loads = []
    for k, part in enumerate((1, 2, 0, 3)):
        for half in range(2):
            cols = pl.ds(128 * half, 128)
            src = s_hbm.at[:, cols] if part == 3 else u_hbm.at[part, :, cols]
            copy = pltpu.make_async_copy(src, R["raw"].at[part, half], R["local"].at[2 * k + half])
            copy.start()
            loads.append(copy)

    barrier = pltpu.get_barrier_semaphore()
    others = [(k, 0) for k in range(1, ngx)] + [(0, k) for k in range(1, ngy)]
    others += [(dx, dy) for dx in (-2, -1, 1, 2) for dy in (-1, 1)]
    for dx, dy in others:
        pl.semaphore_signal(barrier, inc=1, device_id=at(dx, dy), device_id_type=MESH)

    def turn(part, name):
        dst, halo = R[name], FIELDS[name][1]

        def one(x):
            both = [R["raw"][part, half, pl.ds(x, 64, stride=16), :] for half in range(2)]
            dst[x + halo, pl.ds(PAD, 128), :] = jnp.concatenate(both, axis=0).T

        loop(0, 16, one, 8)

    class Exchange:
        def __init__(self, name, field, source=None):
            self.name, self.field, self.source = name, field, source or field
            self.level, self.h, self.more, self.far = EXCHANGES[name]
            self.halo, self.shalo = FIELDS[field][1], FIELDS[self.source][1]
            self.sl, self.sr, self.yl, self.yr = (R[name + k] for k in ("_sl", "_sr", "_yl", "_yr"))

        def hops(self):
            nx, h = self.level.nx, self.h
            if not self.far:
                return [(1, 0, 0, range(nx - h, nx)), (-1, 2, 0, range(h))]
            more = h - nx
            return [(1, 0, 1, range(nx)), (-1, 2, 0, range(nx)), (2, 0, 0, range(nx - more, nx)), (-2, 2, 1, range(more))]

        def slot(self, x):
            nx, h, d = self.level.nx, self.h, self.level.lane
            if 0 <= x < nx:
                return 1, x // d, x % d
            if x < 0:
                k, cut, kind = x + h, h - nx, 0
            else:
                k, cut, kind = x - nx, nx, 2
            if not self.far:
                return kind, k // d, k % d
            return (kind, 0, k) if k < cut else (kind, 1, k - cut)

        def pack(self, kind, slot, rows):
            lv, src, d = self.level, R[self.source], self.level.lane
            count = -(-len(rows) // d)
            which = lanes(8) & (d - 1)
            for buf, row in ((self.sl, PAD), (self.sr, PAD + lv.ny - 8)):
                if d == 1:
                    n = len(rows)
                    val = src[pl.ds(rows[0] + self.shalo, n), pl.ds(row, 8), :].reshape(n * 8, 128)
                    buf[kind, pl.ds(slot, n)] = pltpu.roll(val, 64, 1).reshape(n, 8, 128)
                    continue
                for q in range(count):
                    val = None
                    for g, x in enumerate(rows[q * d : q * d + d]):
                        edge = src[x + self.shalo, pl.ds(row, 8), :]
                        val = edge if val is None else jnp.where(which == g, edge, val)
                    buf[kind, slot + q] = pltpu.roll(val, 64, 1)
            return pl.ds(slot, count)

        def start_y(self):
            at = self.pack(1, 0, range(self.level.nx)) or pl.ds(0, self.level.nx)
            self.y = [
                remote(self.sr.at[1, at], self.yl.at[1, at], 0, 1),
                remote(self.sl.at[1, at], self.yr.at[1, at], 0, -1),
            ]

        def start_diagonal(self):
            self.d = []
            for dx, kind, slot, rows in self.hops():
                at = self.pack(kind, slot, rows) or pl.ds(slot, len(rows))
                self.d.append(remote(self.sr.at[kind, at], self.yl.at[kind, at], dx, 1))
                self.d.append(remote(self.sl.at[kind, at], self.yr.at[kind, at], dx, -1))

        def start_x(self, near=0, far=None):
            lv, src, dst = self.level, R[self.source], R[self.field]
            if lv.lane == 1:
                far = far or self.h
                cols, n, a, e = pl.ds(PAD, lv.ny), far - near, self.halo, self.shalo
                self.x = getattr(self, "x", []) + [
                    remote(src.at[pl.ds(e + lv.nx - far, n), cols], dst.at[pl.ds(a - far, n), cols], 1, 0),
                    remote(src.at[pl.ds(e + near, n), cols], dst.at[pl.ds(a + lv.nx + near, n), cols], -1, 0),
                ]
                return
            px, qx, m = R[self.name + "_px"], R[self.name + "_qx"], lv.ny // lv.lane
            which = lanes(m) & (lv.lane - 1)
            for i in range(lv.nx + 2 * self.more):
                val = src[i + self.shalo - self.more, pl.ds(PAD, m), :]
                for g in range(1, lv.lane):
                    val = jnp.where(which == g, src[i + self.shalo - self.more, pl.ds(PAD + g * m, m), :], val)
                px[i] = val
            self.x = []
            for dx, kind, slot, rows in self.hops():
                to = (self.h - lv.nx if kind == 0 else lv.nx) if slot else 0
                rows = pl.ds(rows[0] + self.more, len(rows))
                self.x.append(remote(px.at[rows], qx.at[kind // 2, pl.ds(to, rows.size)], dx, 0))

        def spread_lanes(self, val, g):
            which = lanes(val.shape[0]) & (self.level.lane - 1)
            t = jnp.where(which == g, val, 0.0)
            for bit in (1, 2)[: self.level.lane // 2]:
                t = t + pltpu.roll(t, 128 - bit if g & bit else bit, 1)
            return t

        def unpack(self):
            lv, f, qx = self.level, R[self.field], R[self.name + "_qx"]
            m = lv.ny // lv.lane
            for side in range(2):
                for i in range(self.h):
                    val = qx[side, i]
                    row = self.halo - self.h + i if side == 0 else self.halo + lv.nx + i
                    for g in range(lv.lane):
                        f[row, pl.ds(PAD + g * m, m), :] = self.spread_lanes(val, g)

        def start(self):
            self.start_diagonal()
            self.start_x()
            self.start_y()

        def wait(self, which):
            for copy in getattr(self, which):
                copy.wait_recv()

        def join(self, lo, hi):
            lv, f = self.level, R[self.field]
            inside = jnp.where(gx > 0, 1.0, 0.0) if hi <= 0 else jnp.where(gx < ngx - 1, 1.0, 0.0) if lo >= lv.nx else 1.0
            left = jnp.where(gy > 0, 1.0, 0.0) * inside
            right = jnp.where(gy < ngy - 1, 1.0, 0.0) * inside
            first = lanes(8) < 64
            if lv.lane > 1:
                for x in range(lo, hi):
                    kind, slot, g = self.slot(x)
                    cells = f.at[x + self.halo]
                    top, low = cells[pl.ds(PAD + lv.ny - 8, 8), :], cells[pl.ds(PAD, 8), :]
                    got = self.spread_lanes(self.yl[kind, slot] * left, g)
                    cells[pl.ds(PAD - 8, 8), :] = jnp.where(first, got, pltpu.roll(top, 64, 1))
                    got = self.spread_lanes(self.yr[kind, slot] * right, g)
                    cells[pl.ds(PAD + lv.ny, 8), :] = jnp.where(first, pltpu.roll(low, 64, 1), got)
                return
            n = hi - lo
            rows = pl.ds(lo + self.halo, n)
            kind, slot, _ = self.slot(lo)
            first = lanes(n * 8) < 64
            top = f[rows, pl.ds(PAD + lv.ny - 8, 8), :].reshape(n * 8, 128)
            got = self.yl[kind, pl.ds(slot, n)].reshape(n * 8, 128) * left
            f[rows, pl.ds(PAD - 8, 8), :] = jnp.where(first, got, pltpu.roll(top, 64, 1)).reshape(n, 8, 128)
            low = f[rows, pl.ds(PAD, 8), :].reshape(n * 8, 128)
            got = self.yr[kind, pl.ds(slot, n)].reshape(n * 8, 128) * right
            f[rows, pl.ds(PAD + lv.ny, 8), :] = jnp.where(first, pltpu.roll(low, 64, 1), got).reshape(n, 8, 128)

        def finish_x(self):
            self.wait("x")
            if self.level.lane > 1:
                self.unpack()
            clear_x(self.field, self.h)
            self.wait("d")
            self.join(-self.h, 0)
            self.join(self.level.nx, self.level.nx + self.h)

        def finish_y(self):
            self.wait("y")
            self.join(0, self.level.nx)

        def finish(self):
            self.finish_y()
            self.finish_x()

    def clear_x(name, h):
        level, halo = FIELDS[name]
        f, zero = R[name], jnp.zeros((level.rows, 128), F32)

        @pl.when(gx == 0)
        def _():
            for x in range(-h, 0):
                f[x + halo] = zero

        @pl.when(gx == ngx - 1)
        def _():
            for x in range(level.nx, level.nx + h):
                f[x + halo] = zero

        if h > level.nx:

            @pl.when(gx == 1)
            def _():
                for x in range(-h, -level.nx):
                    f[x + halo] = zero

            @pl.when(gx == ngx - 2)
            def _():
                for x in range(2 * level.nx, level.nx + h):
                    f[x + halo] = zero

    def clear_y(name, lo, hi):
        level, halo = FIELDS[name]
        f, n = R[name], hi - lo
        rows = pl.ds(halo + lo, n)

        def side(row, first):
            cells = (rows, pl.ds(row, 8), slice(None))
            val = f[cells].reshape(n * 8, 128)
            keep = lanes(n * 8) >= 64 if first else lanes(n * 8) < 64
            f[cells] = jnp.where(keep, val, 0.0).reshape(n, 8, 128)

        @pl.when(gy == 0)
        def _():
            side(PAD - 8, True)

        @pl.when(gy == ngy - 1)
        def _():
            side(PAD + level.ny, False)

    class Rows:
        def __init__(self, field, far, near=0, source=None, cols=None):
            self.field, self.h = field, far
            level, a = FIELDS[field]
            nx, f, n = level.nx, R[field], far - near
            cols = pl.ds(8, level.ny + 16) if cols is None else pl.ds(*cols)
            last, first = (f.at[pl.ds(a + nx - far, n), cols], f.at[pl.ds(a + near, n), cols])
            if source is not None:
                last, first = source.at[pl.ds(n, n), cols], source.at[pl.ds(0, n), cols]
            self.x = [
                remote(last, f.at[pl.ds(a - far, n), cols], 1, 0),
                remote(first, f.at[pl.ds(a + nx + near, n), cols], -1, 0),
            ]

        def finish(self):
            for copy in self.x:
                copy.wait_recv()
            clear_x(self.field, self.h)

    def z_pair(c, lane):
        n = c.shape[0]
        z = lanes(n) & 63
        before = jnp.where(z >= lane, pltpu.roll(c, lane, 1), 0.0)
        after = jnp.where(z < 64 - lane, pltpu.roll(c, 128 - lane, 1), 0.0)
        return before, after

    def around(name, x, r, n):
        level, halo = FIELDS[name]
        f, i = R[name], x + halo
        c = f[i, pl.ds(r, n), :]
        before, after = z_pair(c, level.lane)
        side = f[i - 1, pl.ds(r, n), :] + f[i + 1, pl.ds(r, n), :]
        side = side + (f[i, pl.ds(r - 1, n), :] + f[i, pl.ds(r + 1, n), :])
        return c, side + (before + after)

    def get(name, x, r, n):
        return R[name][x + FIELDS[name][1], pl.ds(r, n), :]

    def put(name, x, r, n, val):
        R[name][x + FIELDS[name][1], pl.ds(r, n), :] = val

    def each(level, lo, hi, fn, own=False):
        def row(x):
            for r, n in level.own if own else level.parts:
                fn(x, r, n)

        loop(lo, hi, row, hi - lo if level is L2 else None)

    def first_sweep(w, b, to, lo, hi):
        def fn(x, r, n):
            put(to, x, r, n, get(w, x, r, n) * get(b, x, r, n))

        each(FIELDS[to][0], lo, hi, fn)

    def sweep(v, w, b, to, lo, hi, also=None):
        level = FIELDS[v][0]

        def fn(x, r, n, twice=also is not None):
            c, s = around(v, x, r, n)
            s = s if level.scale == 1.0 else s * level.scale
            new = 0.2 * c + get(w, x, r, n) * (get(b, x, r, n) + s)
            put(to, x, r, n, new)
            if twice:
                put(also, x, r, n, new)

        if also is None:
            each(level, lo, hi, fn)
        else:
            each(level, max(lo, 0), min(hi, level.nx), fn)
            each(level, lo, min(hi, 0), functools.partial(fn, twice=False))
            each(level, max(lo, level.nx), hi, functools.partial(fn, twice=False))

    def remainder(v, s, b, x, r, n):
        level = FIELDS[v][0]
        c, around_sum = around(v, x, r, n)
        return get(b, x, r, n) + level.scale * around_sum - (6.0 * level.scale + get(s, x, r, n)) * c

    def halve(pair, buf, k, lane):
        ny = pair[0].shape[0] * len(pair)
        for j, val in enumerate(pair):
            R[buf][k, pl.ds(j * val.shape[0], val.shape[0]), :] = val
        a = R[buf][k, pl.ds(0, ny // 2, stride=2), :] + R[buf][k, pl.ds(1, ny // 2, stride=2), :]
        even = (lanes(ny // 2) & lane) == 0
        return (a + jnp.where(even, pltpu.roll(a, 128 - lane, 1), pltpu.roll(a, lane, 1))) * 0.125

    def coarsen(level, fn, lo, hi, write, buf):
        def row(x):
            pair = [fn(2 * x, r, n) + fn(2 * x + 1, r, n) for r, n in level.own]
            write(x, halve(pair, buf, (x + 2) & 7 if lo < 0 else x, level.lane))

        loop(lo, hi, row)

    def spread(name, up, lo, hi):
        level = FIELDS[name][0]
        n = level.ny + 8

        def row(x):
            val = get(name, x, PAD - 4, n)
            R[up][x - lo, pl.ds(8, n, stride=2), :] = val
            R[up][x - lo, pl.ds(9, n, stride=2), :] = val

        loop(lo, hi, row)

    for k, name in enumerate(("U1", "U2", "U0", "S")):
        for copy in loads[2 * k : 2 * k + 2]:
            copy.wait()
        turn((1, 2, 0, 3)[k], name)
    pl.semaphore_wait(barrier, len(others))
    ex_u0, ex_u1, ex_u2, ex_s = Exchange("u0", "U0"), Exchange("u1", "U1"), Exchange("u2", "U2"), Exchange("s", "S")
    for ex in (ex_u1, ex_u2, ex_u0):
        ex.start_y()
    ex_u1.start_x()

    def target(x, r, n, low=True, high=True):
        before, after = z_pair(get("U0", x, r, n), 1)
        d = (after - before) + (get("U2", x, r + 1, n) - get("U2", x, r - 1, n))
        if high:
            d = d + get("U1", x + 1, r, n)
        if low:
            d = d - get("U1", x - 1, r, n)
        put("B", x, r, n, -0.5 * d)

    def edge_rows(r, n):
        for k, x in enumerate((0, 1, 14, 15)):
            target(x, r, n, low=x > 0, high=x < 15)
            R["BE"][k, pl.ds(r, n), :] = get("B", x, r, n)
        return Rows("B", 2, 0, R["BE"], (r, n))

    rows_b = [edge_rows(PAD + 8, 112)]
    ex_u1.start_diagonal()
    ex_s.start()

    coarsen(L0, lambda x, r, n: get("S", x, r, n), 0, 8, lambda x, v: put("S1", x, PAD, 64, v), "RS")
    coarsen(L1, lambda x, r, n: get("S1", x, r, n), 0, 4, lambda x, v: put("S2", x, PAD, 32, v), "RC")

    for ex in (ex_u1, ex_u2, ex_u0):
        ex.finish_y()
    rows_b += [edge_rows(PAD - 8, 16), edge_rows(PAD + 120, 16)]
    ex_s1, ex_s2 = Exchange("s1", "S1"), Exchange("s2", "S2")
    ex_s2.start()
    ex_s1.start()
    each(L0, 2, 14, target)

    def weights(s, w, lo, hi):
        level = FIELDS[s][0]

        def fn(x, r, n):
            put(w, x, r, n, 0.8 / (6.0 * level.scale + get(s, x, r, n)))

        each(level, lo, hi, fn)
        clear_y(w, lo, hi)

    def down_0(v1, keep, r_to, parts):
        for lo, hi in parts[0]:
            sweep(v1, "W", "B", "VB", lo, hi, also=keep)
        for lo, hi in parts[1]:
            coarsen(L0, functools.partial(remainder, "VB", "S", "B"), lo, hi, lambda x, v: put(r_to, x, PAD, 64, v), "RS")

    def coarse_weights_2():
        ex_s2.finish()
        weights("S2", "W2", -6, 10)
        clear_x("W2", 6)
        one = jnp.ones((L2.rows, 128), F32)
        for x in range(16):
            R["I2"][x] = one
        clear_x("I2", 6)
        clear_y("I2", -6, 10)

        def a_one(x, r, n):
            c, s = around("I2", x, r, n)
            put("X2", x, r, n, (6.0 * L2.scale + get("S2", x, r, n)) * c - L2.scale * s)
            put("Z2", x, r, n, c)

        each(L2, -4, 8, a_one)
        lo, hi = -4, 8
        for k in range(4):

            def weigh(x, r, n):
                e = get("W2", x, r, n) * get("X2", x, r, n)
                put("Y2", x, r, n, e)
                put("Z2", x, r, n, get("Z2", x, r, n) - e)

            each(L2, lo, hi, weigh)
            lo, hi = lo + 1, hi - 1
            if k < 3:

                def again(x, r, n):
                    put("X2", x, r, n, 0.2 * get("X2", x, r, n) + L2.scale * around("Y2", x, r, n)[1])

                each(L2, lo, hi, again)
        spread("Z2", "UP1", -1, 5)

    def coarse_weights_1():
        ex_s1.finish()
        weights("S1", "W1", -6, 14)
        clear_x("W1", 6)

        def scaled(x2):
            for k in range(2):
                for r, n in L1.parts:
                    put("X1", 2 * x2 + k, r, n, 0.125 * R["UP1"][x2 + 1, pl.ds(r, n), :])

        loop(-1, 5, scaled, 3)

        def a_of(x, r, n):
            c, s = around("X1", x, r, n)
            y = (6.0 * L1.scale + get("S1", x, r, n)) * c - L1.scale * s
            put("Y1", x, r, n, y)
            put("Z1", x, r, n, get("W1", x, r, n) * y)

        each(L1, -1, 9, a_of)

        def last(x, r, n):
            e, s = around("Z1", x, r, n)
            t = 0.2 * get("Y1", x, r, n) + L1.scale * s
            put("Q1", x, r, n, get("X1", x, r, n) - (e + get("W1", x, r, n) * t))

        each(L1, 0, 8, last)

    def coarse(b1, b2, source, ex1, ex2, sums, work, first):
        total = jnp.zeros((8, 128), F32)
        for x in range(8):
            val = get("Q1", x, PAD, 64) * get(b1, x, PAD, 64)
            total = total + jnp.sum(val.reshape(8, 8, 128), axis=0)
        R[sums + "_a"][...] = jnp.zeros((8, 128), F32)
        R[sums + "_a"][0:1] = jnp.sum(total, axis=0, keepdims=True) * 0.5
        if first:
            mass = jnp.zeros((8, 128), F32)
            for x in range(4):
                mass = mass + jnp.sum(get("S2", x, PAD, 32).reshape(4, 8, 128), axis=0)
            R[sums + "_a"][1:2] = jnp.sum(mass, axis=0, keepdims=True) * 0.25
        part_a = [remote(R[sums + "_a"], R[sums + "_ya"].at[k], 0, k) for k in range(1, ngy)]
        ex1.finish()
        first_sweep("W1", b1, "X1", -6, 14)
        sweep("X1", "W1", b1, "Y1", -5, 13)
        coarsen(L1, functools.partial(remainder, "Y1", "S1", b1), -2, 6, lambda x, v: put(source, x, PAD, 32, v), "RC")
        for x in range(4):
            put(b2, x, PAD, 32, get(source, x, PAD, 32))
        ex2 = Exchange(ex2, b2, source)
        ex2.start()
        both = R[sums + "_a"][...]
        for k, copy in zip(range(1, ngy), part_a, strict=True):
            copy.wait_recv()
            both = both + R[sums + "_ya"][k]
        R[sums + "_b"][...] = both
        part_b = [remote(R[sums + "_b"], R[sums + "_yb"].at[k], k, 0) for k in range(1, ngx)]
        work()
        ex2.finish()
        first_sweep("W2", b2, "X2", -6, 10)
        sweep("X2", "W2", b2, "Y2", -5, 9)
        sweep("Y2", "W2", b2, "X2", -4, 8)
        sweep("X2", "W2", b2, "Y2", -3, 7)
        for k, copy in zip(range(1, ngx), part_b, strict=True):
            copy.wait_recv()
            both = both + R[sums + "_yb"][k]
        return both

    def total_of(row):
        return jnp.sum(row, axis=1, keepdims=True)

    def up(shift, b1):
        def lift(x, r, n):
            put("X2", x, r, n, get("Y2", x, r, n) + shift * get("I2", x, r, n))

        each(L2, -3, 7, lift)
        spread("X2", "UP1", -3, 7)

        def add(x2):
            for k in range(2):
                for r, n in L1.parts:
                    x = 2 * x2 + k
                    put("Y1", x, r, n, get("Y1", x, r, n) + R["UP1"][x2 + 3, pl.ds(r, n), :])

        loop(-3, 7, add, 5)
        sweep("Y1", "W1", b1, "X1", -4, 12)
        sweep("X1", "W1", b1, "Z1", -3, 11)
        spread("Z1", "UP", -3, 11)

    def up_0(kept, p):
        def add(x, x1):
            for r, n in L0.parts:
                put(kept, x, r, n, get(kept, x, r, n) + R["UP"][x1 + 3, pl.ds(r, n), :])

        def pair(x1):
            add(2 * x1, x1)
            add(2 * x1 + 1, x1)

        add(-5, -3)
        loop(-2, 10, pair, 4)
        add(20, 10)
        sweep(kept, "W", "B", "VC", -4, 20)
        sweep("VC", "W", "B", p, -3, 19)

    ex_s.finish_y()
    weights("S", "W", 0, 16)
    first_sweep("W", "B", "VA", 1, 15)
    down_0("VA", "PA", "BA1", ([(2, 14)], [(2, 6)]))
    rows_v = [Rows("PA", 5, 2)]
    coarse_weights_2()
    ex_u1.finish_x()
    ex_s.finish_x()
    weights("S", "W", -2, 0)
    weights("S", "W", 16, 18)
    clear_x("W", 2)
    for rows in rows_b:
        for copy in rows.x:
            copy.wait_recv()
    for x, beside, sign in ((-1, 0, -0.5), (0, -1, 0.5), (15, 16, -0.5), (16, 15, 0.5)):
        for r, n in L0.parts:
            put("B", x, r, n, get("B", x, r, n) + sign * get("U1", beside, r, n))
    first_sweep("W", "B", "VA", -2, 1)
    first_sweep("W", "B", "VA", 15, 18)
    down_0("VA", "PA", "BA1", ([(-1, 2), (14, 17)], [(0, 2), (6, 8)]))
    ex1 = Exchange("ba1", "BA1")
    ex1.start()
    rows_v.append(Rows("PA", 2))
    rows_s = Rows("S", 4, 2)
    coarse_weights_1()
    later = [rows_s]
    sums_a = coarse("BA1", "BA2", "SA2", ex1, "ba2", "ra", lambda: later.append(Rows("B", 4, 2)), True)
    whole = (64 // 4, 16 * ngx // 4, 256 * ngy // 4)
    faces = 2.0 * (whole[0] * whole[1] + whole[1] * whole[2] + whole[0] * whole[2])
    mass = total_of(sums_a[1:2]) + L2.scale * faces
    up(total_of(sums_a[0:1]) / mass, "BA1")
    for rows in later:
        rows.finish()
    weights("S", "W", -4, -2)
    weights("S", "W", 18, 20)
    clear_x("W", 4)
    for copy in rows_v[0].x + rows_v[1].x:
        copy.wait()
    clear_x("PA", 5)
    later = [Rows("U1", 2, 1), Rows("U0", 1), Rows("U2", 1)]
    up_0("PA", "P1")

    sweep("P1", "W", "B", "VA", -2, 18)
    down_0("VA", "PB", "BB1", ([(-1, 17)], [(0, 8)]))
    ex1 = Exchange("bb1", "BB1")
    ex1.start()
    ex_v = Exchange("v", "PB")
    ex_v.start_x(0, 3)
    ex_v.start_diagonal()
    ex_v.start_y()
    sums_b = coarse("BB1", "BB2", "SB2", ex1, "bb2", "rb", lambda: ex_v.start_x(3, 5), False)
    up(total_of(sums_b[0:1]) / mass, "BB1")
    ex_v.finish()
    for copy in ex_v.x:
        copy.wait_send()
    up_0("PB", "P2")

    for rows in later:
        rows.finish()

    def move_1(x, r, n):
        put("VB", x, r, n, get("U1", x, r, n) - 0.5 * (get("P2", x + 1, r, n) - get("P2", x - 1, r, n)))

    each(L0, -2, 18, move_1)

    def move_02(x, r, n):
        before, after = z_pair(get("P2", x, r, n), 1)
        put("VA", x, r, n, get("U0", x, r, n) - 0.5 * (after - before))
        put("VC", x, r, n, get("U2", x, r, n) - 0.5 * (get("P2", x, r + 1, n) - get("P2", x, r - 1, n)))

    each(L0, -1, 17, move_02)
    clear_x("VB", 2)
    clear_y("VB", -2, 18)
    for name in ("VA", "VC"):
        clear_x(name, 1)
        clear_y(name, -1, 17)

    def product(a, b, x, r, n):
        return get(a, x, r, n) * get(b, x, r, n)

    def flux_1(x, r, n):
        d = product("VB", "VB", x + 1, r, n) - product("VB", "VB", x - 1, r, n)
        d = d + 2.0 * (product("VB", "VC", x, r + 1, n) - product("VB", "VC", x, r - 1, n))
        put("PB", x, r, n, d)

    each(L0, -1, 17, flux_1, own=True)
    clear_x("PB", 1)

    def flux_2(x, r, n):
        put("W", x, r, n, product("VC", "VC", x, r + 1, n) - product("VC", "VC", x, r - 1, n))

    each(L0, 0, 16, flux_2)
    clear_y("W", 0, 16)

    def source(x, r, n):
        before, after = z_pair(product("VA", "VA", x, r, n), 1)
        d = product("VA", "VB", x + 1, r, n) - product("VA", "VB", x - 1, r, n)
        d = d + (product("VA", "VC", x, r + 1, n) - product("VA", "VC", x, r - 1, n))
        before, after = z_pair((after - before) + 2.0 * d, 1)
        d = (after - before) + (get("PB", x + 1, r, n) - get("PB", x - 1, r, n))
        return 0.25 * (d + (get("W", x, r + 1, n) - get("W", x, r - 1, n)))

    coarsen(L0, source, 0, 8, lambda x, v: put("X1", x, PAD, 64, v), "RS")

    first = lanes(64) < 64
    for x in range(0, 8, 2):
        t = jnp.concatenate([get("X1", x, PAD, 64), get("X1", x + 1, PAD, 64)], axis=0).T
        low, high = t[:64], t[64:]
        R["G"][pl.ds(x, 64, stride=8), :] = jnp.where(first, low, pltpu.roll(high, 64, 1))
        R["G"][pl.ds(x + 1, 64, stride=8), :] = jnp.where(first, pltpu.roll(low, 64, 1), high)
    for z in range(32):
        R["GZ"][z] = R["G"][pl.ds(16 * z, 8), :]
    for p in range(32):
        R["out"][p] = R["GZ"][levels_ref[p]]
    own = 32 // ngx
    stores = []
    mine = a_hbm.at[:, pl.ds(gx * 8, 8), :]
    copy = pltpu.make_async_copy(R["out"].at[pl.ds(gx * own, own)], mine, R["local"].at[10])
    copy.start()
    stores.append(copy)
    last_ones = []
    for k in range(1, ngx):
        peer = lax.rem(gx + k, ngx)
        last_ones.append(remote(R["out"].at[pl.ds(peer * own, own)], mine, k, 0))
    def back(x):
        t = get("P2", x, PAD, 128).T
        for half in range(2):
            R["back"][half, pl.ds(x, 64, stride=16), :] = t[64 * half : 64 * half + 64]

    loop(0, 16, back, 8)
    for half in range(2):
        copy = pltpu.make_async_copy(R["back"].at[half], p_hbm.at[:, pl.ds(128 * half, 128)], R["local"].at[8 + half])
        copy.start()
        stores.append(copy)

    for copy in last_ones:
        copy.wait_recv()
    for copy in stores:
        copy.wait()
    done = [id(copy) for copy in rows_v[0].x + rows_v[1].x + ex_v.x]
    for copy in sent:
        if id(copy) not in done:
            copy.wait_send()


def hand_on(p_ref, a_ref, p_out, a_out, sems):
    copies = [pltpu.make_async_copy(a_ref, a_out, sems.at[4])]
    for k in range(4):
        rows = pl.ds(256 * k, 256)
        copies.append(pltpu.make_async_copy(p_ref.at[rows], p_out.at[rows], sems.at[k]))
    for copy in copies:
        copy.start()
    for copy in copies:
        copy.wait()


def solution(mesh):
    ngx, ngy = mesh.shape["gx"], mesh.shape["gy"]
    shapes = scratch(ngx, ngy)

    def body(velocity, screen, levels):
        pressure, acoustic = pl.pallas_call(
            functools.partial(kernel, tuple(shapes), ngx, ngy),
            out_shape=(
                pltpu.VMEM((1024, 256), F32),
                pltpu.VMEM((32 // ngx, 8 * ngx, 128), F32),
            ),
            in_specs=[
                pl.BlockSpec(memory_space=pltpu.SMEM),
                pl.BlockSpec(memory_space=pl.ANY),
                pl.BlockSpec(memory_space=pl.ANY),
            ],
            out_specs=(pl.BlockSpec(memory_space=pltpu.VMEM), pl.BlockSpec(memory_space=pltpu.VMEM)),
            scratch_shapes=list(shapes.values()),
            compiler_params=pltpu.CompilerParams(
                collective_id=0, has_side_effects=True, vmem_limit_bytes=56 * 2**20
            ),
        )(levels, velocity.reshape(3, 1024, 256), screen.reshape(1024, 256))
        pressure, acoustic = pl.pallas_call(
            hand_on,
            out_shape=(
                jax.ShapeDtypeStruct(pressure.shape, F32),
                jax.ShapeDtypeStruct(acoustic.shape, F32),
            ),
            in_specs=[pl.BlockSpec(memory_space=pltpu.VMEM)] * 2,
            out_specs=[pl.BlockSpec(memory_space=pl.ANY)] * 2,
            scratch_shapes=[pltpu.SemaphoreType.DMA((5,))],
            compiler_params=pltpu.CompilerParams(vmem_limit_bytes=4 * 2**20),
        )(pressure, acoustic)
        return pressure.reshape(64, 16, 256), acoustic

    in_specs = (P(None, None, "gx", "gy"), P(None, "gx", "gy"), P())
    out_specs = (P(None, "gx", "gy"), P("gx", None, "gy"))
    return jax.shard_map(body, mesh=mesh, in_specs=in_specs, out_specs=out_specs, check_vma=False)
```

```python
import functools

import jax
import jax.numpy as jnp
from jax import lax
from jax.experimental import pallas as pl
from jax.experimental.pallas import tpu as pltpu
from jax.sharding import PartitionSpec as P


F32 = jnp.float32
MESH = pl.DeviceIdType.MESH
PAD = 16


class Level:
    def __init__(self, nx, ny, lane, scale, chunks):
        self.nx, self.ny, self.lane, self.scale = nx, ny, lane, scale
        self.rows = ny + 2 * PAD
        step = (ny + 16) // chunks
        self.parts = [(8 + k * step, step) for k in range(chunks)]
        own = ny // max(1, ny // 64)
        self.own = [(PAD + k * own, own) for k in range(ny // own)]


L0 = Level(16, 128, 1, 1.0, 3)
L1 = Level(8, 64, 2, 0.25, 2)
L2 = Level(4, 32, 4, 0.0625, 1)

FIELDS = {
    "U0": (L0, 1), "U1": (L0, 2), "U2": (L0, 1),
    "S": (L0, 4), "W": (L0, 4), "B": (L0, 4),
    "VA": (L0, 2), "VB": (L0, 2), "VC": (L0, 4),
    "PA": (L0, 5), "PB": (L0, 5),
    "P1": (L0, 3), "P2": (L0, 3),
    "S1": (L1, 6), "W1": (L1, 6), "BA1": (L1, 6), "BB1": (L1, 6),
    "X1": (L1, 6), "Y1": (L1, 6), "Z1": (L1, 6), "Q1": (L1, 0),
    "S2": (L2, 6), "W2": (L2, 6), "BA2": (L2, 6), "BB2": (L2, 6), "I2": (L2, 6),
    "X2": (L2, 6), "Y2": (L2, 6), "Z2": (L2, 6),
    "SA2": (L2, 2), "SB2": (L2, 2),
}
EXCHANGES = {
    "u0": (L0, 1, 0, False), "u1": (L0, 1, 0, False), "u2": (L0, 1, 0, False), "s": (L0, 2, 0, False), "v": (L0, 5, 0, False),
    "s1": (L1, 6, 0, False), "ba1": (L1, 6, 0, False), "bb1": (L1, 6, 0, False),
    "s2": (L2, 6, 0, True), "ba2": (L2, 6, 2, False), "bb2": (L2, 6, 2, False),
}
SUMS = ("ra", "rb")


def scratch(ngx, ngy):
    shapes = {}
    for name, (level, halo) in FIELDS.items():
        shapes[name] = pltpu.VMEM((level.nx + 2 * halo, level.rows, 128), F32)
    for name, (level, halo, more, _) in EXCHANGES.items():
        if level.lane > 1:
            packed = level.ny // level.lane
            shapes[name + "_px"] = pltpu.VMEM((level.nx + 2 * more, packed, 128), F32)
            shapes[name + "_qx"] = pltpu.VMEM((2, halo, packed, 128), F32)
        slots = max(-(-halo // level.lane), -(-level.nx // level.lane))
        for side in "lr":
            shapes[name + "_s" + side] = pltpu.VMEM((3, slots, 8, 128), F32)
            shapes[name + "_y" + side] = pltpu.VMEM((3, slots, 8, 128), F32)
    for name in SUMS:
        shapes[name + "_a"] = pltpu.VMEM((8, 128), F32)
        shapes[name + "_b"] = pltpu.VMEM((8, 128), F32)
        shapes[name + "_ya"] = pltpu.VMEM((ngy, 8, 128), F32)
        shapes[name + "_yb"] = pltpu.VMEM((ngx, 8, 128), F32)
    shapes["BE"] = pltpu.VMEM((4, L0.rows, 128), F32)
    shapes["raw"] = pltpu.VMEM((4, 2, 1024, 128), F32)
    shapes["back"] = pltpu.VMEM((2, 1024, 128), F32)
    shapes["UP"] = pltpu.VMEM((14, L0.rows, 128), F32)
    shapes["UP1"] = pltpu.VMEM((10, L1.rows, 128), F32)
    shapes["RS"] = pltpu.VMEM((8, 128, 128), F32)
    shapes["RC"] = pltpu.VMEM((8, 64, 128), F32)
    shapes["G"] = pltpu.VMEM((64 * 8, 128), F32)
    shapes["GZ"] = pltpu.VMEM((32, 8, 128), F32)
    shapes["out"] = pltpu.VMEM((32, 8, 128), F32)
    shapes["ship"] = pltpu.SemaphoreType.DMA((256,))
    shapes["land"] = pltpu.SemaphoreType.DMA((256,))
    shapes["local"] = pltpu.SemaphoreType.DMA((16,))
    return shapes


def kernel(names, ngx, ngy, levels_ref, u_hbm, s_hbm, p_hbm, a_hbm, *refs):
    R = dict(zip(names, refs, strict=True))
    gx, gy = lax.axis_index("gx"), lax.axis_index("gy")
    slots = [0]
    sent = []

    def at(dx, dy):
        return (lax.rem(gx + dx + ngx, ngx), lax.rem(gy + dy + ngy, ngy))

    def remote(src, dst, dx, dy):
        k = slots[0]
        slots[0] += 1
        copy = pltpu.make_async_remote_copy(
            src_ref=src,
            dst_ref=dst,
            send_sem=R["ship"].at[k],
            recv_sem=R["land"].at[k],
            device_id=at(dx, dy),
            device_id_type=MESH,
        )
        copy.start()
        sent.append(copy)
        return copy

    def lanes(n):
        return lax.broadcasted_iota(jnp.int32, (n, 128), 1)

    def loop(lo, hi, fn, step=None):
        n = hi - lo
        if step is None:
            step = next((k for k in (8, 9, 10, 7, 6, 5) if n % k == 0), n)
        whole = n // step

        def body(i, carry):
            for k in range(step):
                fn(lo + i * step + k)
            return carry

        if whole > 1:
            lax.fori_loop(0, whole, body, 0)
        else:
            whole = 0
        for x in range(lo + whole * step, hi):
            fn(x)

    loads = []
    for k, part in enumerate((1, 2, 0, 3)):
        for half in range(2):
            cols = pl.ds(128 * half, 128)
            src = s_hbm.at[:, cols] if part == 3 else u_hbm.at[part, :, cols]
            copy = pltpu.make_async_copy(src, R["raw"].at[part, half], R["local"].at[2 * k + half])
            copy.start()
            loads.append(copy)

    barrier = pltpu.get_barrier_semaphore()
    others = [(k, 0) for k in range(1, ngx)] + [(0, k) for k in range(1, ngy)]
    others += [(dx, dy) for dx in (-2, -1, 1, 2) for dy in (-1, 1)]
    for dx, dy in others:
        pl.semaphore_signal(barrier, inc=1, device_id=at(dx, dy), device_id_type=MESH)

    def turn(part, name):
        dst, halo = R[name], FIELDS[name][1]

        def one(x):
            both = [R["raw"][part, half, pl.ds(x, 64, stride=16), :] for half in range(2)]
            dst[x + halo, pl.ds(PAD, 128), :] = jnp.concatenate(both, axis=0).T

        loop(0, 16, one, 8)

    class Exchange:
        def __init__(self, name, field, source=None):
            self.name, self.field, self.source = name, field, source or field
            self.level, self.h, self.more, self.far = EXCHANGES[name]
            self.halo, self.shalo = FIELDS[field][1], FIELDS[self.source][1]
            self.sl, self.sr, self.yl, self.yr = (R[name + k] for k in ("_sl", "_sr", "_yl", "_yr"))

        def hops(self):
            nx, h = self.level.nx, self.h
            if not self.far:
                return [(1, 0, 0, range(nx - h, nx)), (-1, 2, 0, range(h))]
            more = h - nx
            return [(1, 0, 1, range(nx)), (-1, 2, 0, range(nx)), (2, 0, 0, range(nx - more, nx)), (-2, 2, 1, range(more))]

        def slot(self, x):
            nx, h, d = self.level.nx, self.h, self.level.lane
            if 0 <= x < nx:
                return 1, x // d, x % d
            if x < 0:
                k, cut, kind = x + h, h - nx, 0
            else:
                k, cut, kind = x - nx, nx, 2
            if not self.far:
                return kind, k // d, k % d
            return (kind, 0, k) if k < cut else (kind, 1, k - cut)

        def pack(self, kind, slot, rows):
            lv, src, d = self.level, R[self.source], self.level.lane
            count = -(-len(rows) // d)
            which = lanes(8) & (d - 1)
            for buf, row in ((self.sl, PAD), (self.sr, PAD + lv.ny - 8)):
                if d == 1:
                    n = len(rows)
                    val = src[pl.ds(rows[0] + self.shalo, n), pl.ds(row, 8), :].reshape(n * 8, 128)
                    buf[kind, pl.ds(slot, n)] = pltpu.roll(val, 64, 1).reshape(n, 8, 128)
                    continue
                for q in range(count):
                    val = None
                    for g, x in enumerate(rows[q * d : q * d + d]):
                        edge = src[x + self.shalo, pl.ds(row, 8), :]
                        val = edge if val is None else jnp.where(which == g, edge, val)
                    buf[kind, slot + q] = pltpu.roll(val, 64, 1)
            return pl.ds(slot, count)

        def start_y(self):
            at = self.pack(1, 0, range(self.level.nx)) or pl.ds(0, self.level.nx)
            self.y = [
                remote(self.sr.at[1, at], self.yl.at[1, at], 0, 1),
                remote(self.sl.at[1, at], self.yr.at[1, at], 0, -1),
            ]

        def start_diagonal(self):
            self.d = []
            for dx, kind, slot, rows in self.hops():
                at = self.pack(kind, slot, rows) or pl.ds(slot, len(rows))
                self.d.append(remote(self.sr.at[kind, at], self.yl.at[kind, at], dx, 1))
                self.d.append(remote(self.sl.at[kind, at], self.yr.at[kind, at], dx, -1))

        def start_x(self, near=0, far=None):
            lv, src, dst = self.level, R[self.source], R[self.field]
            if lv.lane == 1:
                far = far or self.h
                cols, n, a, e = pl.ds(PAD, lv.ny), far - near, self.halo, self.shalo
                self.x = getattr(self, "x", []) + [
                    remote(src.at[pl.ds(e + lv.nx - far, n), cols], dst.at[pl.ds(a - far, n), cols], 1, 0),
                    remote(src.at[pl.ds(e + near, n), cols], dst.at[pl.ds(a + lv.nx + near, n), cols], -1, 0),
                ]
                return
            px, qx, m = R[self.name + "_px"], R[self.name + "_qx"], lv.ny // lv.lane
            which = lanes(m) & (lv.lane - 1)
            for i in range(lv.nx + 2 * self.more):
                val = src[i + self.shalo - self.more, pl.ds(PAD, m), :]
                for g in range(1, lv.lane):
                    val = jnp.where(which == g, src[i + self.shalo - self.more, pl.ds(PAD + g * m, m), :], val)
                px[i] = val
            self.x = []
            for dx, kind, slot, rows in self.hops():
                to = (self.h - lv.nx if kind == 0 else lv.nx) if slot else 0
                rows = pl.ds(rows[0] + self.more, len(rows))
                self.x.append(remote(px.at[rows], qx.at[kind // 2, pl.ds(to, rows.size)], dx, 0))

        def spread_lanes(self, val, g):
            which = lanes(val.shape[0]) & (self.level.lane - 1)
            t = jnp.where(which == g, val, 0.0)
            for bit in (1, 2)[: self.level.lane // 2]:
                t = t + pltpu.roll(t, 128 - bit if g & bit else bit, 1)
            return t

        def unpack(self):
            lv, f, qx = self.level, R[self.field], R[self.name + "_qx"]
            m = lv.ny // lv.lane
            for side in range(2):
                for i in range(self.h):
                    val = qx[side, i]
                    row = self.halo - self.h + i if side == 0 else self.halo + lv.nx + i
                    for g in range(lv.lane):
                        f[row, pl.ds(PAD + g * m, m), :] = self.spread_lanes(val, g)

        def start(self):
            self.start_diagonal()
            self.start_x()
            self.start_y()

        def wait(self, which):
            for copy in getattr(self, which):
                copy.wait_recv()

        def join(self, lo, hi):
            lv, f = self.level, R[self.field]
            inside = jnp.where(gx > 0, 1.0, 0.0) if hi <= 0 else jnp.where(gx < ngx - 1, 1.0, 0.0) if lo >= lv.nx else 1.0
            left = jnp.where(gy > 0, 1.0, 0.0) * inside
            right = jnp.where(gy < ngy - 1, 1.0, 0.0) * inside
            first = lanes(8) < 64
            if lv.lane > 1:
                for x in range(lo, hi):
                    kind, slot, g = self.slot(x)
                    cells = f.at[x + self.halo]
                    top, low = cells[pl.ds(PAD + lv.ny - 8, 8), :], cells[pl.ds(PAD, 8), :]
                    got = self.spread_lanes(self.yl[kind, slot] * left, g)
                    cells[pl.ds(PAD - 8, 8), :] = jnp.where(first, got, pltpu.roll(top, 64, 1))
                    got = self.spread_lanes(self.yr[kind, slot] * right, g)
                    cells[pl.ds(PAD + lv.ny, 8), :] = jnp.where(first, pltpu.roll(low, 64, 1), got)
                return
            n = hi - lo
            rows = pl.ds(lo + self.halo, n)
            kind, slot, _ = self.slot(lo)
            first = lanes(n * 8) < 64
            top = f[rows, pl.ds(PAD + lv.ny - 8, 8), :].reshape(n * 8, 128)
            got = self.yl[kind, pl.ds(slot, n)].reshape(n * 8, 128) * left
            f[rows, pl.ds(PAD - 8, 8), :] = jnp.where(first, got, pltpu.roll(top, 64, 1)).reshape(n, 8, 128)
            low = f[rows, pl.ds(PAD, 8), :].reshape(n * 8, 128)
            got = self.yr[kind, pl.ds(slot, n)].reshape(n * 8, 128) * right
            f[rows, pl.ds(PAD + lv.ny, 8), :] = jnp.where(first, pltpu.roll(low, 64, 1), got).reshape(n, 8, 128)

        def finish_x(self):
            self.wait("x")
            if self.level.lane > 1:
                self.unpack()
            clear_x(self.field, self.h)
            self.wait("d")
            self.join(-self.h, 0)
            self.join(self.level.nx, self.level.nx + self.h)

        def finish_y(self):
            self.wait("y")
            self.join(0, self.level.nx)

        def finish(self):
            self.finish_y()
            self.finish_x()

    def clear_x(name, h):
        level, halo = FIELDS[name]
        f, zero = R[name], jnp.zeros((level.rows, 128), F32)

        @pl.when(gx == 0)
        def _():
            for x in range(-h, 0):
                f[x + halo] = zero

        @pl.when(gx == ngx - 1)
        def _():
            for x in range(level.nx, level.nx + h):
                f[x + halo] = zero

        if h > level.nx:

            @pl.when(gx == 1)
            def _():
                for x in range(-h, -level.nx):
                    f[x + halo] = zero

            @pl.when(gx == ngx - 2)
            def _():
                for x in range(2 * level.nx, level.nx + h):
                    f[x + halo] = zero

    def clear_y(name, lo, hi):
        level, halo = FIELDS[name]
        f, n = R[name], hi - lo
        rows = pl.ds(halo + lo, n)

        def side(row, first):
            cells = (rows, pl.ds(row, 8), slice(None))
            val = f[cells].reshape(n * 8, 128)
            keep = lanes(n * 8) >= 64 if first else lanes(n * 8) < 64
            f[cells] = jnp.where(keep, val, 0.0).reshape(n, 8, 128)

        @pl.when(gy == 0)
        def _():
            side(PAD - 8, True)

        @pl.when(gy == ngy - 1)
        def _():
            side(PAD + level.ny, False)

    class Rows:
        def __init__(self, field, far, near=0, source=None, cols=None):
            self.field, self.h = field, far
            level, a = FIELDS[field]
            nx, f, n = level.nx, R[field], far - near
            cols = pl.ds(8, level.ny + 16) if cols is None else pl.ds(*cols)
            last, first = (f.at[pl.ds(a + nx - far, n), cols], f.at[pl.ds(a + near, n), cols])
            if source is not None:
                last, first = source.at[pl.ds(n, n), cols], source.at[pl.ds(0, n), cols]
            self.x = [
                remote(last, f.at[pl.ds(a - far, n), cols], 1, 0),
                remote(first, f.at[pl.ds(a + nx + near, n), cols], -1, 0),
            ]

        def finish(self):
            for copy in self.x:
                copy.wait_recv()
            clear_x(self.field, self.h)

    def z_pair(c, lane):
        n = c.shape[0]
        z = lanes(n) & 63
        before = jnp.where(z >= lane, pltpu.roll(c, lane, 1), 0.0)
        after = jnp.where(z < 64 - lane, pltpu.roll(c, 128 - lane, 1), 0.0)
        return before, after

    def around(name, x, r, n):
        level, halo = FIELDS[name]
        f, i = R[name], x + halo
        c = f[i, pl.ds(r, n), :]
        before, after = z_pair(c, level.lane)
        side = f[i - 1, pl.ds(r, n), :] + f[i + 1, pl.ds(r, n), :]
        side = side + (f[i, pl.ds(r - 1, n), :] + f[i, pl.ds(r + 1, n), :])
        return c, side + (before + after)

    def get(name, x, r, n):
        return R[name][x + FIELDS[name][1], pl.ds(r, n), :]

    def put(name, x, r, n, val):
        R[name][x + FIELDS[name][1], pl.ds(r, n), :] = val

    def each(level, lo, hi, fn, own=False):
        def row(x):
            for r, n in level.own if own else level.parts:
                fn(x, r, n)

        loop(lo, hi, row, hi - lo if level is L2 else None)

    def first_sweep(w, b, to, lo, hi):
        def fn(x, r, n):
            put(to, x, r, n, get(w, x, r, n) * get(b, x, r, n))

        each(FIELDS[to][0], lo, hi, fn)

    def sweep(v, w, b, to, lo, hi, also=None):
        level = FIELDS[v][0]

        def fn(x, r, n, twice=also is not None):
            c, s = around(v, x, r, n)
            s = s if level.scale == 1.0 else s * level.scale
            new = 0.2 * c + get(w, x, r, n) * (get(b, x, r, n) + s)
            put(to, x, r, n, new)
            if twice:
                put(also, x, r, n, new)

        if also is None:
            each(level, lo, hi, fn)
        else:
            each(level, max(lo, 0), min(hi, level.nx), fn)
            each(level, lo, min(hi, 0), functools.partial(fn, twice=False))
            each(level, max(lo, level.nx), hi, functools.partial(fn, twice=False))

    def remainder(v, s, b, x, r, n):
        level = FIELDS[v][0]
        c, around_sum = around(v, x, r, n)
        return get(b, x, r, n) + level.scale * around_sum - (6.0 * level.scale + get(s, x, r, n)) * c

    def halve(pair, buf, k, lane):
        ny = pair[0].shape[0] * len(pair)
        for j, val in enumerate(pair):
            R[buf][k, pl.ds(j * val.shape[0], val.shape[0]), :] = val
        a = R[buf][k, pl.ds(0, ny // 2, stride=2), :] + R[buf][k, pl.ds(1, ny // 2, stride=2), :]
        even = (lanes(ny // 2) & lane) == 0
        return (a + jnp.where(even, pltpu.roll(a, 128 - lane, 1), pltpu.roll(a, lane, 1))) * 0.125

    def coarsen(level, fn, lo, hi, write, buf):
        def row(x):
            pair = [fn(2 * x, r, n) + fn(2 * x + 1, r, n) for r, n in level.own]
            write(x, halve(pair, buf, (x + 2) & 7 if lo < 0 else x, level.lane))

        loop(lo, hi, row)

    def spread(name, up, lo, hi):
        level = FIELDS[name][0]
        n = level.ny + 8

        def row(x):
            val = get(name, x, PAD - 4, n)
            R[up][x - lo, pl.ds(8, n, stride=2), :] = val
            R[up][x - lo, pl.ds(9, n, stride=2), :] = val

        loop(lo, hi, row)

    for k, name in enumerate(("U1", "U2", "U0", "S")):
        for copy in loads[2 * k : 2 * k + 2]:
            copy.wait()
        turn((1, 2, 0, 3)[k], name)
    pl.semaphore_wait(barrier, len(others))
    ex_u0, ex_u1, ex_u2, ex_s = Exchange("u0", "U0"), Exchange("u1", "U1"), Exchange("u2", "U2"), Exchange("s", "S")
    for ex in (ex_u1, ex_u2, ex_u0):
        ex.start_y()
    ex_u1.start_x()

    def target(x, r, n, low=True, high=True):
        before, after = z_pair(get("U0", x, r, n), 1)
        d = (after - before) + (get("U2", x, r + 1, n) - get("U2", x, r - 1, n))
        if high:
            d = d + get("U1", x + 1, r, n)
        if low:
            d = d - get("U1", x - 1, r, n)
        put("B", x, r, n, -0.5 * d)

    def edge_rows(r, n):
        for k, x in enumerate((0, 1, 14, 15)):
            target(x, r, n, low=x > 0, high=x < 15)
            R["BE"][k, pl.ds(r, n), :] = get("B", x, r, n)
        return Rows("B", 2, 0, R["BE"], (r, n))

    rows_b = [edge_rows(PAD + 8, 112)]
    ex_u1.start_diagonal()
    ex_s.start()

    coarsen(L0, lambda x, r, n: get("S", x, r, n), 0, 8, lambda x, v: put("S1", x, PAD, 64, v), "RS")
    coarsen(L1, lambda x, r, n: get("S1", x, r, n), 0, 4, lambda x, v: put("S2", x, PAD, 32, v), "RC")

    for ex in (ex_u1, ex_u2, ex_u0):
        ex.finish_y()
    rows_b += [edge_rows(PAD - 8, 16), edge_rows(PAD + 120, 16)]
    ex_s1, ex_s2 = Exchange("s1", "S1"), Exchange("s2", "S2")
    ex_s2.start()
    ex_s1.start()
    each(L0, 2, 14, target)

    def weights(s, w, lo, hi):
        level = FIELDS[s][0]

        def fn(x, r, n):
            put(w, x, r, n, 0.8 / (6.0 * level.scale + get(s, x, r, n)))

        each(level, lo, hi, fn)
        clear_y(w, lo, hi)

    def down_0(v1, keep, r_to, parts):
        for lo, hi in parts[0]:
            sweep(v1, "W", "B", "VB", lo, hi, also=keep)
        for lo, hi in parts[1]:
            coarsen(L0, functools.partial(remainder, "VB", "S", "B"), lo, hi, lambda x, v: put(r_to, x, PAD, 64, v), "RS")

    def coarse_weights_2():
        ex_s2.finish()
        weights("S2", "W2", -6, 10)
        clear_x("W2", 6)
        one = jnp.ones((L2.rows, 128), F32)
        for x in range(16):
            R["I2"][x] = one
        clear_x("I2", 6)
        clear_y("I2", -6, 10)

        def a_one(x, r, n):
            c, s = around("I2", x, r, n)
            put("X2", x, r, n, (6.0 * L2.scale + get("S2", x, r, n)) * c - L2.scale * s)
            put("Z2", x, r, n, c)

        each(L2, -4, 8, a_one)
        lo, hi = -4, 8
        for k in range(4):

            def weigh(x, r, n):
                e = get("W2", x, r, n) * get("X2", x, r, n)
                put("Y2", x, r, n, e)
                put("Z2", x, r, n, get("Z2", x, r, n) - e)

            each(L2, lo, hi, weigh)
            lo, hi = lo + 1, hi - 1
            if k < 3:

                def again(x, r, n):
                    put("X2", x, r, n, 0.2 * get("X2", x, r, n) + L2.scale * around("Y2", x, r, n)[1])

                each(L2, lo, hi, again)
        spread("Z2", "UP1", -1, 5)

    def coarse_weights_1():
        ex_s1.finish()
        weights("S1", "W1", -6, 14)
        clear_x("W1", 6)

        def scaled(x2):
            for k in range(2):
                for r, n in L1.parts:
                    put("X1", 2 * x2 + k, r, n, 0.125 * R["UP1"][x2 + 1, pl.ds(r, n), :])

        loop(-1, 5, scaled, 3)

        def a_of(x, r, n):
            c, s = around("X1", x, r, n)
            y = (6.0 * L1.scale + get("S1", x, r, n)) * c - L1.scale * s
            put("Y1", x, r, n, y)
            put("Z1", x, r, n, get("W1", x, r, n) * y)

        each(L1, -1, 9, a_of)

        def last(x, r, n):
            e, s = around("Z1", x, r, n)
            t = 0.2 * get("Y1", x, r, n) + L1.scale * s
            put("Q1", x, r, n, get("X1", x, r, n) - (e + get("W1", x, r, n) * t))

        each(L1, 0, 8, last)

    def coarse(b1, b2, source, ex1, ex2, sums, work, first):
        total = jnp.zeros((8, 128), F32)
        for x in range(8):
            val = get("Q1", x, PAD, 64) * get(b1, x, PAD, 64)
            total = total + jnp.sum(val.reshape(8, 8, 128), axis=0)
        R[sums + "_a"][...] = jnp.zeros((8, 128), F32)
        R[sums + "_a"][0:1] = jnp.sum(total, axis=0, keepdims=True) * 0.5
        if first:
            mass = jnp.zeros((8, 128), F32)
            for x in range(4):
                mass = mass + jnp.sum(get("S2", x, PAD, 32).reshape(4, 8, 128), axis=0)
            R[sums + "_a"][1:2] = jnp.sum(mass, axis=0, keepdims=True) * 0.25
        part_a = [remote(R[sums + "_a"], R[sums + "_ya"].at[k], 0, k) for k in range(1, ngy)]
        ex1.finish()
        first_sweep("W1", b1, "X1", -6, 14)
        sweep("X1", "W1", b1, "Y1", -5, 13)
        coarsen(L1, functools.partial(remainder, "Y1", "S1", b1), -2, 6, lambda x, v: put(source, x, PAD, 32, v), "RC")
        ex2 = Exchange(ex2, b2, source)
        ex2.start()
        for x in range(4):
            put(b2, x, PAD, 32, get(source, x, PAD, 32))
        both = R[sums + "_a"][...]
        for k, copy in zip(range(1, ngy), part_a, strict=True):
            copy.wait_recv()
            both = both + R[sums + "_ya"][k]
        R[sums + "_b"][...] = both
        part_b = [remote(R[sums + "_b"], R[sums + "_yb"].at[k], k, 0) for k in range(1, ngx)]
        work()
        ex2.finish()
        first_sweep("W2", b2, "X2", -6, 10)
        sweep("X2", "W2", b2, "Y2", -5, 9)
        sweep("Y2", "W2", b2, "X2", -4, 8)
        sweep("X2", "W2", b2, "Y2", -3, 7)
        for k, copy in zip(range(1, ngx), part_b, strict=True):
            copy.wait_recv()
            both = both + R[sums + "_yb"][k]
        return both

    def total_of(row):
        return jnp.sum(row, axis=1, keepdims=True)

    def up(shift, b1):
        def lift(x, r, n):
            put("X2", x, r, n, get("Y2", x, r, n) + shift * get("I2", x, r, n))

        each(L2, -3, 7, lift)
        spread("X2", "UP1", -3, 7)

        def add(x2):
            for k in range(2):
                for r, n in L1.parts:
                    x = 2 * x2 + k
                    put("Y1", x, r, n, get("Y1", x, r, n) + R["UP1"][x2 + 3, pl.ds(r, n), :])

        loop(-3, 7, add, 5)
        sweep("Y1", "W1", b1, "X1", -4, 12)
        sweep("X1", "W1", b1, "Z1", -3, 11)
        spread("Z1", "UP", -3, 11)

    def up_0(kept, p):
        def add(x, x1):
            for r, n in L0.parts:
                put(kept, x, r, n, get(kept, x, r, n) + R["UP"][x1 + 3, pl.ds(r, n), :])

        def pair(x1):
            add(2 * x1, x1)
            add(2 * x1 + 1, x1)

        add(-5, -3)
        loop(-2, 10, pair, 4)
        add(20, 10)
        sweep(kept, "W", "B", "VC", -4, 20)
        sweep("VC", "W", "B", p, -3, 19)

    ex_s.finish_y()
    weights("S", "W", 0, 16)
    first_sweep("W", "B", "VA", 1, 15)
    down_0("VA", "PA", "BA1", ([(2, 14)], [(2, 6)]))
    rows_v = [Rows("PA", 5, 2)]
    coarse_weights_2()
    ex_u1.finish_x()
    ex_s.finish_x()
    weights("S", "W", -2, 0)
    weights("S", "W", 16, 18)
    clear_x("W", 2)
    for rows in rows_b:
        for copy in rows.x:
            copy.wait_recv()
    for x, beside, sign in ((-1, 0, -0.5), (0, -1, 0.5), (15, 16, -0.5), (16, 15, 0.5)):
        for r, n in L0.parts:
            put("B", x, r, n, get("B", x, r, n) + sign * get("U1", beside, r, n))
    first_sweep("W", "B", "VA", -2, 1)
    first_sweep("W", "B", "VA", 15, 18)
    down_0("VA", "PA", "BA1", ([(-1, 2), (14, 17)], [(0, 2), (6, 8)]))
    ex1 = Exchange("ba1", "BA1")
    ex1.start()
    rows_v.append(Rows("PA", 2))
    rows_s = Rows("S", 4, 2)
    coarse_weights_1()
    later = [rows_s]
    sums_a = coarse("BA1", "BA2", "SA2", ex1, "ba2", "ra", lambda: later.append(Rows("B", 4, 2)), True)
    whole = (64 // 4, 16 * ngx // 4, 256 * ngy // 4)
    faces = 2.0 * (whole[0] * whole[1] + whole[1] * whole[2] + whole[0] * whole[2])
    mass = total_of(sums_a[1:2]) + L2.scale * faces
    up(total_of(sums_a[0:1]) / mass, "BA1")
    for rows in later:
        rows.finish()
    weights("S", "W", -4, -2)
    weights("S", "W", 18, 20)
    clear_x("W", 4)
    for copy in rows_v[0].x + rows_v[1].x:
        copy.wait()
    clear_x("PA", 5)
    later = [Rows("U1", 2, 1), Rows("U0", 1), Rows("U2", 1)]
    up_0("PA", "P1")

    sweep("P1", "W", "B", "VA", -2, 18)
    down_0("VA", "PB", "BB1", ([(-1, 17)], [(0, 8)]))
    ex1 = Exchange("bb1", "BB1")
    ex1.start()
    ex_v = Exchange("v", "PB")
    ex_v.start_x(0, 3)
    ex_v.start_diagonal()
    ex_v.start_y()
    sums_b = coarse("BB1", "BB2", "SB2", ex1, "bb2", "rb", lambda: ex_v.start_x(3, 5), False)
    up(total_of(sums_b[0:1]) / mass, "BB1")
    ex_v.finish()
    for copy in ex_v.x:
        copy.wait_send()
    up_0("PB", "P2")

    for rows in later:
        rows.finish()

    def move_1(x, r, n):
        put("VB", x, r, n, get("U1", x, r, n) - 0.5 * (get("P2", x + 1, r, n) - get("P2", x - 1, r, n)))

    each(L0, -2, 18, move_1)

    def move_02(x, r, n):
        before, after = z_pair(get("P2", x, r, n), 1)
        put("VA", x, r, n, get("U0", x, r, n) - 0.5 * (after - before))
        put("VC", x, r, n, get("U2", x, r, n) - 0.5 * (get("P2", x, r + 1, n) - get("P2", x, r - 1, n)))

    each(L0, -1, 17, move_02)
    clear_x("VB", 2)
    clear_y("VB", -2, 18)
    for name in ("VA", "VC"):
        clear_x(name, 1)
        clear_y(name, -1, 17)

    def product(a, b, x, r, n):
        return get(a, x, r, n) * get(b, x, r, n)

    def flux_1(x, r, n):
        d = product("VB", "VB", x + 1, r, n) - product("VB", "VB", x - 1, r, n)
        d = d + 2.0 * (product("VB", "VC", x, r + 1, n) - product("VB", "VC", x, r - 1, n))
        put("PB", x, r, n, d)

    each(L0, -1, 17, flux_1, own=True)
    clear_x("PB", 1)

    def flux_2(x, r, n):
        put("W", x, r, n, product("VC", "VC", x, r + 1, n) - product("VC", "VC", x, r - 1, n))

    each(L0, 0, 16, flux_2)
    clear_y("W", 0, 16)

    def source(x, r, n):
        before, after = z_pair(product("VA", "VA", x, r, n), 1)
        d = product("VA", "VB", x + 1, r, n) - product("VA", "VB", x - 1, r, n)
        d = d + (product("VA", "VC", x, r + 1, n) - product("VA", "VC", x, r - 1, n))
        before, after = z_pair((after - before) + 2.0 * d, 1)
        d = (after - before) + (get("PB", x + 1, r, n) - get("PB", x - 1, r, n))
        return 0.25 * (d + (get("W", x, r + 1, n) - get("W", x, r - 1, n)))

    coarsen(L0, source, 0, 8, lambda x, v: put("X1", x, PAD, 64, v), "RS")

    first = lanes(64) < 64
    for x in range(0, 8, 2):
        t = jnp.concatenate([get("X1", x, PAD, 64), get("X1", x + 1, PAD, 64)], axis=0).T
        low, high = t[:64], t[64:]
        R["G"][pl.ds(x, 64, stride=8), :] = jnp.where(first, low, pltpu.roll(high, 64, 1))
        R["G"][pl.ds(x + 1, 64, stride=8), :] = jnp.where(first, pltpu.roll(low, 64, 1), high)
    for z in range(32):
        R["GZ"][z] = R["G"][pl.ds(16 * z, 8), :]
    for p in range(32):
        R["out"][p] = R["GZ"][levels_ref[p]]
    own = 32 // ngx
    stores = []
    mine = a_hbm.at[:, pl.ds(gx * 8, 8), :]
    copy = pltpu.make_async_copy(R["out"].at[pl.ds(gx * own, own)], mine, R["local"].at[10])
    copy.start()
    stores.append(copy)
    last_ones = []
    for k in range(1, ngx):
        peer = lax.rem(gx + k, ngx)
        last_ones.append(remote(R["out"].at[pl.ds(peer * own, own)], mine, k, 0))
    def back(x):
        t = get("P2", x, PAD, 128).T
        for half in range(2):
            R["back"][half, pl.ds(x, 64, stride=16), :] = t[64 * half : 64 * half + 64]

    loop(0, 16, back, 8)
    for half in range(2):
        copy = pltpu.make_async_copy(R["back"].at[half], p_hbm.at[:, pl.ds(128 * half, 128)], R["local"].at[8 + half])
        copy.start()
        stores.append(copy)

    done = [id(copy) for copy in rows_v[0].x + rows_v[1].x + ex_v.x + last_ones]
    for copy in sent:
        if id(copy) not in done:
            copy.wait_send()
    for copy in stores:
        copy.wait()
    for copy in last_ones:
        copy.wait()


def hand_on(p_ref, a_ref, p_out, a_out, sems):
    copies = [pltpu.make_async_copy(a_ref, a_out, sems.at[4])]
    for k in range(4):
        rows = pl.ds(256 * k, 256)
        copies.append(pltpu.make_async_copy(p_ref.at[rows], p_out.at[rows], sems.at[k]))
    for copy in copies:
        copy.start()
    for copy in copies:
        copy.wait()


def solution(mesh):
    ngx, ngy = mesh.shape["gx"], mesh.shape["gy"]
    shapes = scratch(ngx, ngy)

    def body(velocity, screen, levels):
        pressure, acoustic = pl.pallas_call(
            functools.partial(kernel, tuple(shapes), ngx, ngy),
            out_shape=(
                pltpu.VMEM((1024, 256), F32),
                pltpu.VMEM((32 // ngx, 8 * ngx, 128), F32),
            ),
            in_specs=[
                pl.BlockSpec(memory_space=pltpu.SMEM),
                pl.BlockSpec(memory_space=pl.ANY),
                pl.BlockSpec(memory_space=pl.ANY),
            ],
            out_specs=(pl.BlockSpec(memory_space=pltpu.VMEM), pl.BlockSpec(memory_space=pltpu.VMEM)),
            scratch_shapes=list(shapes.values()),
            compiler_params=pltpu.CompilerParams(
                collective_id=0, has_side_effects=True, vmem_limit_bytes=56 * 2**20
            ),
        )(levels, velocity.reshape(3, 1024, 256), screen.reshape(1024, 256))
        pressure, acoustic = pl.pallas_call(
            hand_on,
            out_shape=(
                jax.ShapeDtypeStruct(pressure.shape, F32),
                jax.ShapeDtypeStruct(acoustic.shape, F32),
            ),
            in_specs=[pl.BlockSpec(memory_space=pltpu.VMEM)] * 2,
            out_specs=[pl.BlockSpec(memory_space=pl.ANY)] * 2,
            scratch_shapes=[pltpu.SemaphoreType.DMA((5,))],
            compiler_params=pltpu.CompilerParams(vmem_limit_bytes=4 * 2**20),
        )(pressure, acoustic)
        return pressure.reshape(64, 16, 256), acoustic

    in_specs = (P(None, None, "gx", "gy"), P(None, "gx", "gy"), P())
    out_specs = (P(None, "gx", "gy"), P("gx", None, "gy"))
    return jax.shard_map(body, mesh=mesh, in_specs=in_specs, out_specs=out_specs, check_vma=False)
```

```python
import functools

import jax
import jax.numpy as jnp
from jax import lax
from jax.experimental import pallas as pl
from jax.experimental.pallas import tpu as pltpu
from jax.sharding import PartitionSpec as P


F32 = jnp.float32
MESH = pl.DeviceIdType.MESH
PAD = 16


class Level:
    def __init__(self, nx, ny, lane, scale, chunks):
        self.nx, self.ny, self.lane, self.scale = nx, ny, lane, scale
        self.rows = ny + 2 * PAD
        step = (ny + 16) // chunks
        self.parts = [(8 + k * step, step) for k in range(chunks)]
        own = ny // max(1, ny // 64)
        self.own = [(PAD + k * own, own) for k in range(ny // own)]


L0 = Level(16, 128, 1, 1.0, 3)
L1 = Level(8, 64, 2, 0.25, 2)
L2 = Level(4, 32, 4, 0.0625, 1)

FIELDS = {
    "U0": (L0, 1), "U1": (L0, 2), "U2": (L0, 1),
    "S": (L0, 4), "W": (L0, 4), "B": (L0, 4),
    "VA": (L0, 2), "VB": (L0, 2), "VC": (L0, 4),
    "PA": (L0, 5), "PB": (L0, 5),
    "P1": (L0, 3), "P2": (L0, 3),
    "S1": (L1, 6), "W1": (L1, 6), "BA1": (L1, 6), "BB1": (L1, 6),
    "X1": (L1, 6), "Y1": (L1, 6), "Z1": (L1, 6), "Q1": (L1, 0),
    "S2": (L2, 6), "W2": (L2, 6), "BA2": (L2, 6), "BB2": (L2, 6), "I2": (L2, 6),
    "X2": (L2, 6), "Y2": (L2, 6), "Z2": (L2, 6),
    "SA2": (L2, 2), "SB2": (L2, 2),
}
EXCHANGES = {
    "u0": (L0, 1, 0, False), "u1": (L0, 1, 0, False), "u2": (L0, 1, 0, False), "s": (L0, 2, 0, False), "v": (L0, 5, 0, False),
    "s1": (L1, 6, 0, False), "ba1": (L1, 6, 0, False), "bb1": (L1, 6, 0, False),
    "s2": (L2, 6, 0, True), "ba2": (L2, 6, 2, False), "bb2": (L2, 6, 2, False),
}
SUMS = ("ra", "rb")


def scratch(ngx, ngy):
    shapes = {}
    for name, (level, halo) in FIELDS.items():
        shapes[name] = pltpu.VMEM((level.nx + 2 * halo, level.rows, 128), F32)
    for name, (level, halo, more, _) in EXCHANGES.items():
        if level.lane > 1:
            packed = level.ny // level.lane
            shapes[name + "_px"] = pltpu.VMEM((level.nx + 2 * more, packed, 128), F32)
            shapes[name + "_qx"] = pltpu.VMEM((2, halo, packed, 128), F32)
        slots = max(-(-halo // level.lane), -(-level.nx // level.lane))
        for side in "lr":
            shapes[name + "_s" + side] = pltpu.VMEM((3, slots, 8, 128), F32)
            shapes[name + "_y" + side] = pltpu.VMEM((3, slots, 8, 128), F32)
    for name in SUMS:
        shapes[name + "_a"] = pltpu.VMEM((8, 128), F32)
        shapes[name + "_b"] = pltpu.VMEM((8, 128), F32)
        shapes[name + "_ya"] = pltpu.VMEM((ngy, 8, 128), F32)
        shapes[name + "_yb"] = pltpu.VMEM((ngx, 8, 128), F32)
    shapes["BE"] = pltpu.VMEM((4, L0.rows, 128), F32)
    shapes["raw"] = pltpu.VMEM((4, 2, 1024, 128), F32)
    shapes["back"] = pltpu.VMEM((2, 1024, 128), F32)
    shapes["UP"] = pltpu.VMEM((14, L0.rows, 128), F32)
    shapes["UP1"] = pltpu.VMEM((10, L1.rows, 128), F32)
    shapes["RS"] = pltpu.VMEM((8, 128, 128), F32)
    shapes["RC"] = pltpu.VMEM((8, 64, 128), F32)
    shapes["G"] = pltpu.VMEM((64 * 8, 128), F32)
    shapes["GZ"] = pltpu.VMEM((32, 8, 128), F32)
    shapes["out"] = pltpu.VMEM((32, 8, 128), F32)
    shapes["ship"] = pltpu.SemaphoreType.DMA((256,))
    shapes["land"] = pltpu.SemaphoreType.DMA((256,))
    shapes["local"] = pltpu.SemaphoreType.DMA((16,))
    return shapes


def kernel(names, ngx, ngy, levels_ref, u_hbm, s_hbm, p_hbm, a_hbm, *refs):
    R = dict(zip(names, refs, strict=True))
    gx, gy = lax.axis_index("gx"), lax.axis_index("gy")
    slots = [0]
    sent = []

    def at(dx, dy):
        return (lax.rem(gx + dx + ngx, ngx), lax.rem(gy + dy + ngy, ngy))

    def remote(src, dst, dx, dy):
        k = slots[0]
        slots[0] += 1
        copy = pltpu.make_async_remote_copy(
            src_ref=src,
            dst_ref=dst,
            send_sem=R["ship"].at[k],
            recv_sem=R["land"].at[k],
            device_id=at(dx, dy),
            device_id_type=MESH,
        )
        copy.start()
        sent.append(copy)
        return copy

    def lanes(n):
        return lax.broadcasted_iota(jnp.int32, (n, 128), 1)

    def loop(lo, hi, fn, step=None):
        n = hi - lo
        if step is None:
            step = next((k for k in (8, 9, 10, 7, 6, 5) if n % k == 0), n)
        whole = n // step

        def body(i, carry):
            for k in range(step):
                fn(lo + i * step + k)
            return carry

        if whole > 1:
            lax.fori_loop(0, whole, body, 0)
        else:
            whole = 0
        for x in range(lo + whole * step, hi):
            fn(x)

    loads = []
    for k, part in enumerate((1, 2, 0, 3)):
        for half in range(2):
            cols = pl.ds(128 * half, 128)
            src = s_hbm.at[:, cols] if part == 3 else u_hbm.at[part, :, cols]
            copy = pltpu.make_async_copy(src, R["raw"].at[part, half], R["local"].at[2 * k + half])
            copy.start()
            loads.append(copy)

    barrier = pltpu.get_barrier_semaphore()
    others = [(k, 0) for k in range(1, ngx)] + [(0, k) for k in range(1, ngy)]
    others += [(dx, dy) for dx in (-2, -1, 1, 2) for dy in (-1, 1)]
    for dx, dy in others:
        pl.semaphore_signal(barrier, inc=1, device_id=at(dx, dy), device_id_type=MESH)

    def turn(part, name):
        dst, halo = R[name], FIELDS[name][1]

        def one(x):
            both = [R["raw"][part, half, pl.ds(x, 64, stride=16), :] for half in range(2)]
            dst[x + halo, pl.ds(PAD, 128), :] = jnp.concatenate(both, axis=0).T

        loop(0, 16, one, 8)

    class Exchange:
        def __init__(self, name, field, source=None):
            self.name, self.field, self.source = name, field, source or field
            self.level, self.h, self.more, self.far = EXCHANGES[name]
            self.halo, self.shalo = FIELDS[field][1], FIELDS[self.source][1]
            self.sl, self.sr, self.yl, self.yr = (R[name + k] for k in ("_sl", "_sr", "_yl", "_yr"))

        def hops(self):
            nx, h = self.level.nx, self.h
            if not self.far:
                return [(1, 0, 0, range(nx - h, nx)), (-1, 2, 0, range(h))]
            more = h - nx
            return [(1, 0, 1, range(nx)), (-1, 2, 0, range(nx)), (2, 0, 0, range(nx - more, nx)), (-2, 2, 1, range(more))]

        def slot(self, x):
            nx, h, d = self.level.nx, self.h, self.level.lane
            if 0 <= x < nx:
                return 1, x // d, x % d
            if x < 0:
                k, cut, kind = x + h, h - nx, 0
            else:
                k, cut, kind = x - nx, nx, 2
            if not self.far:
                return kind, k // d, k % d
            return (kind, 0, k) if k < cut else (kind, 1, k - cut)

        def pack(self, kind, slot, rows):
            lv, src, d = self.level, R[self.source], self.level.lane
            count = -(-len(rows) // d)
            which = lanes(8) & (d - 1)
            for buf, row in ((self.sl, PAD), (self.sr, PAD + lv.ny - 8)):
                if d == 1:
                    n = len(rows)
                    val = src[pl.ds(rows[0] + self.shalo, n), pl.ds(row, 8), :].reshape(n * 8, 128)
                    buf[kind, pl.ds(slot, n)] = pltpu.roll(val, 64, 1).reshape(n, 8, 128)
                    continue
                for q in range(count):
                    val = None
                    for g, x in enumerate(rows[q * d : q * d + d]):
                        edge = src[x + self.shalo, pl.ds(row, 8), :]
                        val = edge if val is None else jnp.where(which == g, edge, val)
                    buf[kind, slot + q] = pltpu.roll(val, 64, 1)
            return pl.ds(slot, count)

        def start_y(self):
            at = self.pack(1, 0, range(self.level.nx)) or pl.ds(0, self.level.nx)
            self.y = [
                remote(self.sr.at[1, at], self.yl.at[1, at], 0, 1),
                remote(self.sl.at[1, at], self.yr.at[1, at], 0, -1),
            ]

        def start_diagonal(self):
            self.d = []
            for dx, kind, slot, rows in self.hops():
                at = self.pack(kind, slot, rows) or pl.ds(slot, len(rows))
                self.d.append(remote(self.sr.at[kind, at], self.yl.at[kind, at], dx, 1))
                self.d.append(remote(self.sl.at[kind, at], self.yr.at[kind, at], dx, -1))

        def start_x(self, near=0, far=None):
            lv, src, dst = self.level, R[self.source], R[self.field]
            if lv.lane == 1:
                far = far or self.h
                cols, n, a, e = pl.ds(PAD, lv.ny), far - near, self.halo, self.shalo
                self.x = getattr(self, "x", []) + [
                    remote(src.at[pl.ds(e + lv.nx - far, n), cols], dst.at[pl.ds(a - far, n), cols], 1, 0),
                    remote(src.at[pl.ds(e + near, n), cols], dst.at[pl.ds(a + lv.nx + near, n), cols], -1, 0),
                ]
                return
            px, qx, m = R[self.name + "_px"], R[self.name + "_qx"], lv.ny // lv.lane
            which = lanes(m) & (lv.lane - 1)
            for i in range(lv.nx + 2 * self.more):
                val = src[i + self.shalo - self.more, pl.ds(PAD, m), :]
                for g in range(1, lv.lane):
                    val = jnp.where(which == g, src[i + self.shalo - self.more, pl.ds(PAD + g * m, m), :], val)
                px[i] = val
            self.x = []
            for dx, kind, slot, rows in self.hops():
                to = (self.h - lv.nx if kind == 0 else lv.nx) if slot else 0
                rows = pl.ds(rows[0] + self.more, len(rows))
                self.x.append(remote(px.at[rows], qx.at[kind // 2, pl.ds(to, rows.size)], dx, 0))

        def spread_lanes(self, val, g):
            which = lanes(val.shape[0]) & (self.level.lane - 1)
            t = jnp.where(which == g, val, 0.0)
            for bit in (1, 2)[: self.level.lane // 2]:
                t = t + pltpu.roll(t, 128 - bit if g & bit else bit, 1)
            return t

        def unpack(self):
            lv, f, qx = self.level, R[self.field], R[self.name + "_qx"]
            m = lv.ny // lv.lane
            for side in range(2):
                for i in range(self.h):
                    val = qx[side, i]
                    row = self.halo - self.h + i if side == 0 else self.halo + lv.nx + i
                    for g in range(lv.lane):
                        f[row, pl.ds(PAD + g * m, m), :] = self.spread_lanes(val, g)

        def start(self):
            self.start_diagonal()
            self.start_x()
            self.start_y()

        def wait(self, which):
            for copy in getattr(self, which):
                copy.wait_recv()

        def join(self, lo, hi):
            lv, f = self.level, R[self.field]
            inside = jnp.where(gx > 0, 1.0, 0.0) if hi <= 0 else jnp.where(gx < ngx - 1, 1.0, 0.0) if lo >= lv.nx else 1.0
            left = jnp.where(gy > 0, 1.0, 0.0) * inside
            right = jnp.where(gy < ngy - 1, 1.0, 0.0) * inside
            first = lanes(8) < 64
            if lv.lane > 1:
                for x in range(lo, hi):
                    kind, slot, g = self.slot(x)
                    cells = f.at[x + self.halo]
                    top, low = cells[pl.ds(PAD + lv.ny - 8, 8), :], cells[pl.ds(PAD, 8), :]
                    got = self.spread_lanes(self.yl[kind, slot] * left, g)
                    cells[pl.ds(PAD - 8, 8), :] = jnp.where(first, got, pltpu.roll(top, 64, 1))
                    got = self.spread_lanes(self.yr[kind, slot] * right, g)
                    cells[pl.ds(PAD + lv.ny, 8), :] = jnp.where(first, pltpu.roll(low, 64, 1), got)
                return
            n = hi - lo
            rows = pl.ds(lo + self.halo, n)
            kind, slot, _ = self.slot(lo)
            first = lanes(n * 8) < 64
            top = f[rows, pl.ds(PAD + lv.ny - 8, 8), :].reshape(n * 8, 128)
            got = self.yl[kind, pl.ds(slot, n)].reshape(n * 8, 128) * left
            f[rows, pl.ds(PAD - 8, 8), :] = jnp.where(first, got, pltpu.roll(top, 64, 1)).reshape(n, 8, 128)
            low = f[rows, pl.ds(PAD, 8), :].reshape(n * 8, 128)
            got = self.yr[kind, pl.ds(slot, n)].reshape(n * 8, 128) * right
            f[rows, pl.ds(PAD + lv.ny, 8), :] = jnp.where(first, pltpu.roll(low, 64, 1), got).reshape(n, 8, 128)

        def finish_x(self):
            self.wait("x")
            if self.level.lane > 1:
                self.unpack()
            clear_x(self.field, self.h)
            self.wait("d")
            self.join(-self.h, 0)
            self.join(self.level.nx, self.level.nx + self.h)

        def finish_y(self):
            self.wait("y")
            self.join(0, self.level.nx)

        def finish(self):
            self.finish_y()
            self.finish_x()

    def clear_x(name, h):
        level, halo = FIELDS[name]
        f, zero = R[name], jnp.zeros((level.rows, 128), F32)

        @pl.when(gx == 0)
        def _():
            for x in range(-h, 0):
                f[x + halo] = zero

        @pl.when(gx == ngx - 1)
        def _():
            for x in range(level.nx, level.nx + h):
                f[x + halo] = zero

        if h > level.nx:

            @pl.when(gx == 1)
            def _():
                for x in range(-h, -level.nx):
                    f[x + halo] = zero

            @pl.when(gx == ngx - 2)
            def _():
                for x in range(2 * level.nx, level.nx + h):
                    f[x + halo] = zero

    def clear_y(name, lo, hi):
        level, halo = FIELDS[name]
        f, n = R[name], hi - lo
        rows = pl.ds(halo + lo, n)

        def side(row, first):
            cells = (rows, pl.ds(row, 8), slice(None))
            val = f[cells].reshape(n * 8, 128)
            keep = lanes(n * 8) >= 64 if first else lanes(n * 8) < 64
            f[cells] = jnp.where(keep, val, 0.0).reshape(n, 8, 128)

        @pl.when(gy == 0)
        def _():
            side(PAD - 8, True)

        @pl.when(gy == ngy - 1)
        def _():
            side(PAD + level.ny, False)

    class Rows:
        def __init__(self, field, far, near=0, source=None, cols=None):
            self.field, self.h = field, far
            level, a = FIELDS[field]
            nx, f, n = level.nx, R[field], far - near
            cols = pl.ds(8, level.ny + 16) if cols is None else pl.ds(*cols)
            last, first = (f.at[pl.ds(a + nx - far, n), cols], f.at[pl.ds(a + near, n), cols])
            if source is not None:
                last, first = source.at[pl.ds(n, n), cols], source.at[pl.ds(0, n), cols]
            self.x = [
                remote(last, f.at[pl.ds(a - far, n), cols], 1, 0),
                remote(first, f.at[pl.ds(a + nx + near, n), cols], -1, 0),
            ]

        def finish(self):
            for copy in self.x:
                copy.wait_recv()
            clear_x(self.field, self.h)

    def z_pair(c, lane):
        n = c.shape[0]
        z = lanes(n) & 63
        before = jnp.where(z >= lane, pltpu.roll(c, lane, 1), 0.0)
        after = jnp.where(z < 64 - lane, pltpu.roll(c, 128 - lane, 1), 0.0)
        return before, after

    def around(name, x, r, n):
        level, halo = FIELDS[name]
        f, i = R[name], x + halo
        c = f[i, pl.ds(r, n), :]
        before, after = z_pair(c, level.lane)
        side = f[i - 1, pl.ds(r, n), :] + f[i + 1, pl.ds(r, n), :]
        side = side + (f[i, pl.ds(r - 1, n), :] + f[i, pl.ds(r + 1, n), :])
        return c, side + (before + after)

    def get(name, x, r, n):
        return R[name][x + FIELDS[name][1], pl.ds(r, n), :]

    def put(name, x, r, n, val):
        R[name][x + FIELDS[name][1], pl.ds(r, n), :] = val

    def each(level, lo, hi, fn, own=False):
        def row(x):
            for r, n in level.own if own else level.parts:
                fn(x, r, n)

        loop(lo, hi, row, hi - lo if level is L2 else None)

    def first_sweep(w, b, to, lo, hi):
        def fn(x, r, n):
            put(to, x, r, n, get(w, x, r, n) * get(b, x, r, n))

        each(FIELDS[to][0], lo, hi, fn)

    def sweep(v, w, b, to, lo, hi, also=None):
        level = FIELDS[v][0]

        def fn(x, r, n, twice=also is not None):
            c, s = around(v, x, r, n)
            s = s if level.scale == 1.0 else s * level.scale
            new = 0.2 * c + get(w, x, r, n) * (get(b, x, r, n) + s)
            put(to, x, r, n, new)
            if twice:
                put(also, x, r, n, new)

        if also is None:
            each(level, lo, hi, fn)
        else:
            each(level, max(lo, 0), min(hi, level.nx), fn)
            each(level, lo, min(hi, 0), functools.partial(fn, twice=False))
            each(level, max(lo, level.nx), hi, functools.partial(fn, twice=False))

    def remainder(v, s, b, x, r, n):
        level = FIELDS[v][0]
        c, around_sum = around(v, x, r, n)
        return get(b, x, r, n) + level.scale * around_sum - (6.0 * level.scale + get(s, x, r, n)) * c

    def halve(pair, buf, k, lane):
        ny = pair[0].shape[0] * len(pair)
        for j, val in enumerate(pair):
            R[buf][k, pl.ds(j * val.shape[0], val.shape[0]), :] = val
        a = R[buf][k, pl.ds(0, ny // 2, stride=2), :] + R[buf][k, pl.ds(1, ny // 2, stride=2), :]
        even = (lanes(ny // 2) & lane) == 0
        return (a + jnp.where(even, pltpu.roll(a, 128 - lane, 1), pltpu.roll(a, lane, 1))) * 0.125

    def coarsen(level, fn, lo, hi, write, buf):
        def row(x):
            pair = [fn(2 * x, r, n) + fn(2 * x + 1, r, n) for r, n in level.own]
            write(x, halve(pair, buf, (x + 2) & 7 if lo < 0 else x, level.lane))

        loop(lo, hi, row)

    def spread(name, up, lo, hi):
        level = FIELDS[name][0]
        n = level.ny + 8

        def row(x):
            val = get(name, x, PAD - 4, n)
            R[up][x - lo, pl.ds(8, n, stride=2), :] = val
            R[up][x - lo, pl.ds(9, n, stride=2), :] = val

        loop(lo, hi, row)

    for k, name in enumerate(("U1", "U2", "U0", "S")):
        for copy in loads[2 * k : 2 * k + 2]:
            copy.wait()
        turn((1, 2, 0, 3)[k], name)
    pl.semaphore_wait(barrier, len(others))
    ex_u0, ex_u1, ex_u2, ex_s = Exchange("u0", "U0"), Exchange("u1", "U1"), Exchange("u2", "U2"), Exchange("s", "S")
    for ex in (ex_u1, ex_u2, ex_u0):
        ex.start_y()
    ex_u1.start_x()

    def target(x, r, n, low=True, high=True):
        before, after = z_pair(get("U0", x, r, n), 1)
        d = (after - before) + (get("U2", x, r + 1, n) - get("U2", x, r - 1, n))
        if high:
            d = d + get("U1", x + 1, r, n)
        if low:
            d = d - get("U1", x - 1, r, n)
        put("B", x, r, n, -0.5 * d)

    def edge_rows(r, n):
        for k, x in enumerate((0, 1, 14, 15)):
            target(x, r, n, low=x > 0, high=x < 15)
            R["BE"][k, pl.ds(r, n), :] = get("B", x, r, n)
        return Rows("B", 2, 0, R["BE"], (r, n))

    rows_b = [edge_rows(PAD + 8, 112)]
    ex_u1.start_diagonal()
    ex_s.start()

    coarsen(L0, lambda x, r, n: get("S", x, r, n), 0, 8, lambda x, v: put("S1", x, PAD, 64, v), "RS")
    coarsen(L1, lambda x, r, n: get("S1", x, r, n), 0, 4, lambda x, v: put("S2", x, PAD, 32, v), "RC")

    for ex in (ex_u1, ex_u2, ex_u0):
        ex.finish_y()
    rows_b += [edge_rows(PAD - 8, 16), edge_rows(PAD + 120, 16)]
    ex_s1, ex_s2 = Exchange("s1", "S1"), Exchange("s2", "S2")
    ex_s2.start()
    ex_s1.start()
    each(L0, 2, 14, target)

    def weights(s, w, lo, hi):
        level = FIELDS[s][0]

        def fn(x, r, n):
            put(w, x, r, n, 0.8 / (6.0 * level.scale + get(s, x, r, n)))

        each(level, lo, hi, fn)
        clear_y(w, lo, hi)

    def down_0(v1, keep, r_to, parts):
        for lo, hi in parts[0]:
            sweep(v1, "W", "B", "VB", lo, hi, also=keep)
        for lo, hi in parts[1]:
            coarsen(L0, functools.partial(remainder, "VB", "S", "B"), lo, hi, lambda x, v: put(r_to, x, PAD, 64, v), "RS")

    def coarse_weights_2():
        ex_s2.finish()
        weights("S2", "W2", -6, 10)
        clear_x("W2", 6)
        one = jnp.ones((L2.rows, 128), F32)
        for x in range(16):
            R["I2"][x] = one
        clear_x("I2", 6)
        clear_y("I2", -6, 10)

        def a_one(x, r, n):
            c, s = around("I2", x, r, n)
            put("X2", x, r, n, (6.0 * L2.scale + get("S2", x, r, n)) * c - L2.scale * s)
            put("Z2", x, r, n, c)

        each(L2, -4, 8, a_one)
        lo, hi = -4, 8
        for k in range(4):

            def weigh(x, r, n):
                e = get("W2", x, r, n) * get("X2", x, r, n)
                put("Y2", x, r, n, e)
                put("Z2", x, r, n, get("Z2", x, r, n) - e)

            each(L2, lo, hi, weigh)
            lo, hi = lo + 1, hi - 1
            if k < 3:

                def again(x, r, n):
                    put("X2", x, r, n, 0.2 * get("X2", x, r, n) + L2.scale * around("Y2", x, r, n)[1])

                each(L2, lo, hi, again)
        spread("Z2", "UP1", -1, 5)

    def coarse_weights_1():
        ex_s1.finish()
        weights("S1", "W1", -6, 14)
        clear_x("W1", 6)

        def scaled(x2):
            for k in range(2):
                for r, n in L1.parts:
                    put("X1", 2 * x2 + k, r, n, 0.125 * R["UP1"][x2 + 1, pl.ds(r, n), :])

        loop(-1, 5, scaled, 3)

        def a_of(x, r, n):
            c, s = around("X1", x, r, n)
            y = (6.0 * L1.scale + get("S1", x, r, n)) * c - L1.scale * s
            put("Y1", x, r, n, y)
            put("Z1", x, r, n, get("W1", x, r, n) * y)

        each(L1, -1, 9, a_of)

        def last(x, r, n):
            e, s = around("Z1", x, r, n)
            t = 0.2 * get("Y1", x, r, n) + L1.scale * s
            put("Q1", x, r, n, get("X1", x, r, n) - (e + get("W1", x, r, n) * t))

        each(L1, 0, 8, last)

    def coarse(b1, b2, source, ex1, ex2, sums, work, first):
        total = jnp.zeros((8, 128), F32)
        for x in range(8):
            val = get("Q1", x, PAD, 64) * get(b1, x, PAD, 64)
            total = total + jnp.sum(val.reshape(8, 8, 128), axis=0)
        R[sums + "_a"][...] = jnp.zeros((8, 128), F32)
        R[sums + "_a"][0:1] = jnp.sum(total, axis=0, keepdims=True) * 0.5
        if first:
            mass = jnp.zeros((8, 128), F32)
            for x in range(4):
                mass = mass + jnp.sum(get("S2", x, PAD, 32).reshape(4, 8, 128), axis=0)
            R[sums + "_a"][1:2] = jnp.sum(mass, axis=0, keepdims=True) * 0.25
        part_a = [remote(R[sums + "_a"], R[sums + "_ya"].at[k], 0, k) for k in range(1, ngy)]
        ex1.finish()
        first_sweep("W1", b1, "X1", -6, 14)
        sweep("X1", "W1", b1, "Y1", -5, 13)
        coarsen(L1, functools.partial(remainder, "Y1", "S1", b1), -2, 6, lambda x, v: put(source, x, PAD, 32, v), "RC")
        ex2 = Exchange(ex2, b2, source)
        ex2.start()
        for x in range(4):
            put(b2, x, PAD, 32, get(source, x, PAD, 32))
        both = R[sums + "_a"][...]
        for k, copy in zip(range(1, ngy), part_a, strict=True):
            copy.wait_recv()
            both = both + R[sums + "_ya"][k]
        R[sums + "_b"][...] = both
        part_b = [remote(R[sums + "_b"], R[sums + "_yb"].at[k], k, 0) for k in range(1, ngx)]
        work()
        ex2.finish()
        first_sweep("W2", b2, "X2", -6, 10)
        sweep("X2", "W2", b2, "Y2", -5, 9)
        sweep("Y2", "W2", b2, "X2", -4, 8)
        sweep("X2", "W2", b2, "Y2", -3, 7)
        for k, copy in zip(range(1, ngx), part_b, strict=True):
            copy.wait_recv()
            both = both + R[sums + "_yb"][k]
        return both

    def total_of(row):
        return jnp.sum(row, axis=1, keepdims=True)

    def up(shift, b1):
        def lift(x, r, n):
            put("X2", x, r, n, get("Y2", x, r, n) + shift * get("I2", x, r, n))

        each(L2, -3, 7, lift)
        spread("X2", "UP1", -3, 7)

        def add(x2):
            for k in range(2):
                for r, n in L1.parts:
                    x = 2 * x2 + k
                    put("Y1", x, r, n, get("Y1", x, r, n) + R["UP1"][x2 + 3, pl.ds(r, n), :])

        loop(-3, 7, add, 5)
        sweep("Y1", "W1", b1, "X1", -4, 12)
        sweep("X1", "W1", b1, "Z1", -3, 11)
        spread("Z1", "UP", -3, 11)

    def up_0(kept, p):
        def add(x, x1):
            for r, n in L0.parts:
                put(kept, x, r, n, get(kept, x, r, n) + R["UP"][x1 + 3, pl.ds(r, n), :])

        def pair(x1):
            add(2 * x1, x1)
            add(2 * x1 + 1, x1)

        add(-5, -3)
        loop(-2, 10, pair, 4)
        add(20, 10)
        sweep(kept, "W", "B", "VC", -4, 20)
        sweep("VC", "W", "B", p, -3, 19)

    ex_s.finish_y()
    weights("S", "W", 0, 16)
    first_sweep("W", "B", "VA", 1, 15)
    down_0("VA", "PA", "BA1", ([(2, 14)], [(2, 6)]))
    rows_v = [Rows("PA", 5, 2)]
    coarse_weights_2()
    ex_u1.finish_x()
    ex_s.finish_x()
    weights("S", "W", -2, 0)
    weights("S", "W", 16, 18)
    clear_x("W", 2)
    for rows in rows_b:
        for copy in rows.x:
            copy.wait_recv()
    for x, beside, sign in ((-1, 0, -0.5), (0, -1, 0.5), (15, 16, -0.5), (16, 15, 0.5)):
        for r, n in L0.parts:
            put("B", x, r, n, get("B", x, r, n) + sign * get("U1", beside, r, n))
    first_sweep("W", "B", "VA", -2, 1)
    first_sweep("W", "B", "VA", 15, 18)
    down_0("VA", "PA", "BA1", ([(-1, 2), (14, 17)], [(0, 2), (6, 8)]))
    ex1 = Exchange("ba1", "BA1")
    ex1.start()
    rows_v.append(Rows("PA", 2))
    rows_s = Rows("S", 4, 2)
    coarse_weights_1()
    later = []

    def far_rows():
        later.append(Rows("B", 4, 2))
        for copy in rows_v[0].x + rows_v[1].x:
            copy.wait()
        clear_x("PA", 5)
        rows_s.finish()
        weights("S", "W", -4, -2)
        weights("S", "W", 18, 20)
        clear_x("W", 4)

    sums_a = coarse("BA1", "BA2", "SA2", ex1, "ba2", "ra", far_rows, True)
    whole = (64 // 4, 16 * ngx // 4, 256 * ngy // 4)
    faces = 2.0 * (whole[0] * whole[1] + whole[1] * whole[2] + whole[0] * whole[2])
    mass = total_of(sums_a[1:2]) + L2.scale * faces
    up(total_of(sums_a[0:1]) / mass, "BA1")
    for rows in later:
        rows.finish()
    later = [Rows("U1", 2, 1), Rows("U0", 1), Rows("U2", 1)]
    up_0("PA", "P1")

    sweep("P1", "W", "B", "VA", -2, 18)
    down_0("VA", "PB", "BB1", ([(-1, 17)], [(0, 8)]))
    ex1 = Exchange("bb1", "BB1")
    ex1.start()
    ex_v = Exchange("v", "PB")
    ex_v.start_x(0, 3)
    ex_v.start_diagonal()
    ex_v.start_y()
    sums_b = coarse("BB1", "BB2", "SB2", ex1, "bb2", "rb", lambda: ex_v.start_x(3, 5), False)
    up(total_of(sums_b[0:1]) / mass, "BB1")
    ex_v.finish()
    for copy in ex_v.x:
        copy.wait_send()
    up_0("PB", "P2")

    for rows in later:
        rows.finish()

    def move_1(x, r, n):
        put("VB", x, r, n, get("U1", x, r, n) - 0.5 * (get("P2", x + 1, r, n) - get("P2", x - 1, r, n)))

    each(L0, -2, 18, move_1)

    def move_02(x, r, n):
        before, after = z_pair(get("P2", x, r, n), 1)
        put("VA", x, r, n, get("U0", x, r, n) - 0.5 * (after - before))
        put("VC", x, r, n, get("U2", x, r, n) - 0.5 * (get("P2", x, r + 1, n) - get("P2", x, r - 1, n)))

    each(L0, -1, 17, move_02)
    clear_x("VB", 2)
    clear_y("VB", -2, 18)
    for name in ("VA", "VC"):
        clear_x(name, 1)
        clear_y(name, -1, 17)

    def product(a, b, x, r, n):
        return get(a, x, r, n) * get(b, x, r, n)

    def flux_1(x, r, n):
        d = product("VB", "VB", x + 1, r, n) - product("VB", "VB", x - 1, r, n)
        d = d + 2.0 * (product("VB", "VC", x, r + 1, n) - product("VB", "VC", x, r - 1, n))
        put("PB", x, r, n, d)

    each(L0, -1, 17, flux_1, own=True)
    clear_x("PB", 1)

    def flux_2(x, r, n):
        put("W", x, r, n, product("VC", "VC", x, r + 1, n) - product("VC", "VC", x, r - 1, n))

    each(L0, 0, 16, flux_2)
    clear_y("W", 0, 16)

    def source(x, r, n):
        before, after = z_pair(product("VA", "VA", x, r, n), 1)
        d = product("VA", "VB", x + 1, r, n) - product("VA", "VB", x - 1, r, n)
        d = d + (product("VA", "VC", x, r + 1, n) - product("VA", "VC", x, r - 1, n))
        before, after = z_pair((after - before) + 2.0 * d, 1)
        d = (after - before) + (get("PB", x + 1, r, n) - get("PB", x - 1, r, n))
        return 0.25 * (d + (get("W", x, r + 1, n) - get("W", x, r - 1, n)))

    coarsen(L0, source, 0, 8, lambda x, v: put("X1", x, PAD, 64, v), "RS")

    first = lanes(64) < 64
    for x in range(0, 8, 2):
        t = jnp.concatenate([get("X1", x, PAD, 64), get("X1", x + 1, PAD, 64)], axis=0).T
        low, high = t[:64], t[64:]
        R["G"][pl.ds(x, 64, stride=8), :] = jnp.where(first, low, pltpu.roll(high, 64, 1))
        R["G"][pl.ds(x + 1, 64, stride=8), :] = jnp.where(first, pltpu.roll(low, 64, 1), high)
    for z in range(32):
        R["GZ"][z] = R["G"][pl.ds(16 * z, 8), :]
    for p in range(32):
        R["out"][p] = R["GZ"][levels_ref[p]]
    own = 32 // ngx
    stores = []
    mine = a_hbm.at[:, pl.ds(gx * 8, 8), :]
    copy = pltpu.make_async_copy(R["out"].at[pl.ds(gx * own, own)], mine, R["local"].at[10])
    copy.start()
    stores.append(copy)
    last_ones = []
    for k in range(1, ngx):
        peer = lax.rem(gx + k, ngx)
        last_ones.append(remote(R["out"].at[pl.ds(peer * own, own)], mine, k, 0))
    def back(x):
        t = get("P2", x, PAD, 128).T
        for half in range(2):
            R["back"][half, pl.ds(x, 64, stride=16), :] = t[64 * half : 64 * half + 64]

    loop(0, 16, back, 8)
    for half in range(2):
        copy = pltpu.make_async_copy(R["back"].at[half], p_hbm.at[:, pl.ds(128 * half, 128)], R["local"].at[8 + half])
        copy.start()
        stores.append(copy)

    done = [id(copy) for copy in rows_v[0].x + rows_v[1].x + ex_v.x + last_ones]
    for copy in sent:
        if id(copy) not in done:
            copy.wait_send()
    for copy in stores:
        copy.wait()
    for copy in last_ones:
        copy.wait()


def hand_on(p_ref, a_ref, p_out, a_out, sems):
    copies = [pltpu.make_async_copy(a_ref, a_out, sems.at[4])]
    for k in range(4):
        rows = pl.ds(256 * k, 256)
        copies.append(pltpu.make_async_copy(p_ref.at[rows], p_out.at[rows], sems.at[k]))
    for copy in copies:
        copy.start()
    for copy in copies:
        copy.wait()


def solution(mesh):
    ngx, ngy = mesh.shape["gx"], mesh.shape["gy"]
    shapes = scratch(ngx, ngy)

    def body(velocity, screen, levels):
        pressure, acoustic = pl.pallas_call(
            functools.partial(kernel, tuple(shapes), ngx, ngy),
            out_shape=(
                pltpu.VMEM((1024, 256), F32),
                pltpu.VMEM((32 // ngx, 8 * ngx, 128), F32),
            ),
            in_specs=[
                pl.BlockSpec(memory_space=pltpu.SMEM),
                pl.BlockSpec(memory_space=pl.ANY),
                pl.BlockSpec(memory_space=pl.ANY),
            ],
            out_specs=(pl.BlockSpec(memory_space=pltpu.VMEM), pl.BlockSpec(memory_space=pltpu.VMEM)),
            scratch_shapes=list(shapes.values()),
            compiler_params=pltpu.CompilerParams(
                collective_id=0, has_side_effects=True, vmem_limit_bytes=56 * 2**20
            ),
        )(levels, velocity.reshape(3, 1024, 256), screen.reshape(1024, 256))
        pressure, acoustic = pl.pallas_call(
            hand_on,
            out_shape=(
                jax.ShapeDtypeStruct(pressure.shape, F32),
                jax.ShapeDtypeStruct(acoustic.shape, F32),
            ),
            in_specs=[pl.BlockSpec(memory_space=pltpu.VMEM)] * 2,
            out_specs=[pl.BlockSpec(memory_space=pl.ANY)] * 2,
            scratch_shapes=[pltpu.SemaphoreType.DMA((5,))],
            compiler_params=pltpu.CompilerParams(vmem_limit_bytes=4 * 2**20),
        )(pressure, acoustic)
        return pressure.reshape(64, 16, 256), acoustic

    in_specs = (P(None, None, "gx", "gy"), P(None, "gx", "gy"), P())
    out_specs = (P(None, "gx", "gy"), P("gx", None, "gy"))
    return jax.shard_map(body, mesh=mesh, in_specs=in_specs, out_specs=out_specs, check_vma=False)
```
